128 devices in a mesh: seq: 16 (over y, x), patch: 8 (over z, core).
Axes of the slice: x: 4, y: 4, z: 4, core: 2. Of those that a mesh axis runs over, the one named last changes fastest.
Arguments:
- byte_states: bfloat16 [65536, 1024], P('seq'), may hold values from -16 to 16
- patch_len: int32 [16, 512], P('seq'), may hold values from 1 to 16, 4096 in all within a row
- shard_offset: int32 [16], P('seq'), may hold values from 0 to 15
- owner: int32 [16, 512], P('seq'), may hold values from 0 to 511, each once within a row
- cotangent: bfloat16 [8192, 4096], P('seq', 'patch'), may hold values from -6 to 6
- w_query: bfloat16 [1024, 1024], replicated, may hold values from -0.1875 to 0.1875
- w_key: bfloat16 [1024, 1024], replicated, may hold values from -0.1875 to 0.1875
- w_value: bfloat16 [1024, 1024], replicated, may hold values from -0.1875 to 0.1875
- w_out: bfloat16 [1024, 4096], P(None, 'patch'), may hold values from -0.1875 to 0.1875
Outputs:
- d_bytes: bfloat16 [65536, 1024], P('seq', 'patch')
- d_qkv: float32 [3, 1024, 1024], P(None, 'patch')
- d_wout: float32 [1024, 4096], P(None, 'patch')
- patch_rows: bfloat16 [8192, 1024], P(('seq', 'patch'))
The draws below stay inside these ranges and needn't reach their ends.
Inputs may be any that keep to these rules, and one draw needn't show every extreme that they name: `patch_len`: each row sums to 4096. `owner`: each row holds every number of 0 to 511 once.
All inputs are finite; a program needn't handle non-finite values.
Results may differ from the reference program's by a relative error of at most 0.013.
The reference program's roundings to bfloat16 on the way (of `window`, `pooled`, `query`, `probs_b`, `d_att`, `d_scores` and `d_keys`) count: a program that leaves them out, or rounds other values in their place, can miss the bound.
Values may be sent and summed in bfloat16 or wider, within the bound.
No kernel may reach another device: no remote copies, remote signals or barrier semaphores. Data moves between devices by JAX's collectives and lax.ppermute only.
A program may use at most 192 MiB of HBM per device.

```python
import math
import jax
import jax.numpy as jnp
import numpy as np
from jax import lax

DL = 1024
DG = 4096
HEADS = 16
MAXP = 16
S_DEV = 4096
P_SEQ = 512
RIM = 32
S = 65536
P_SIZE = 8192
N_SEQ = 16


def draw_byte_states(key, part):
    key = jax.random.fold_in(key, 1)
    first = jax.random.fold_in(key, 0)
    values = jnp.clip(jax.random.normal(first, (S, DL), jnp.float32), -6.0, 6.0)
    return values.astype(jnp.bfloat16)


def plant(values, key, low, largest):
    index_at = [jax.random.randint(jax.random.fold_in(key, axis), (), 0, length) for axis, length in enumerate(values.shape)]
    main_axis = values.shape.index(max(values.shape))
    beside = index_at[:main_axis] + [(index_at[main_axis] + 1) % values.shape[main_axis]] + index_at[main_axis + 1:]
    return values.at[tuple(index_at)].set(low).at[tuple(beside)].set(largest)


def shard_levels(stream_key, shape, pieces, low, largest):
    def one(axis_at, parts):
        heights = jax.random.uniform(jax.random.fold_in(jax.random.fold_in(stream_key, 6), axis_at), (parts,), jnp.float32, low / len(pieces), largest / len(pieces))
        return jnp.repeat(jnp.exp(heights), shape[axis_at] // parts).reshape((-1,) + (1,) * (len(shape) - axis_at - 1))

    gain = one(*pieces[0])
    for cut in pieces[1:]:
        gain = gain * one(*cut)
    return gain


def split_up(number_of, total, most, slope):
    loads = [(1 << 20) // math.isqrt(rank ** slope) + 1 for rank in range(2, number_of + 1)]
    rest, given = total - most - (number_of - 1), [1] * (number_of - 1)
    while rest > 0:
        free = [i for i in range(number_of - 1) if given[i] < most]
        pool, left = sum([loads[i] for i in free]), rest
        for i in free:
            addition = min(most - given[i], max(1, left * loads[i] // pool), rest)
            given[i] = given[i] + addition
            rest = rest - addition
    return np.array([most] + given)


def uneven_parts(own_key, count, total, most, lean):
    if count == 2:
        one = jax.random.randint(own_key, (), max(1, total - most), min(most, total - 1) + 1)
        return jnp.stack([one, total - one])
    sizes = jnp.asarray(split_up(count, total, most, lean), jnp.int32)
    pairs = (count - 1) // 2
    source_of, receiver = sizes[1:1 + 2 * pairs:2], sizes[2:2 + 2 * pairs:2]
    room = jnp.minimum(source_of - 1, most - receiver)
    shifted = jax.random.randint(jax.random.fold_in(own_key, 1), (pairs,), 0, 1 << 20) % (room + 1)
    sizes = sizes.at[1:1 + 2 * pairs:2].set(source_of - shifted).at[2:2 + 2 * pairs:2].set(receiver + shifted)
    return sizes[jax.random.permutation(jax.random.fold_in(own_key, 2), count)]


def bell_draw(stream_key, dims, spread, limit, pieces=(), kind=jnp.bfloat16):
    values = jax.random.normal(stream_key, dims, jnp.float32) * spread
    if len(pieces) > 0:
        values = shard_levels(stream_key, dims, pieces, -0.22, 0.18) * values
    return jnp.clip(values, min=-limit, max=limit).astype(kind)


def setup_inputs(seed: int = 0) -> dict:
    key_list = jax.random.split(jax.random.key(seed), 10)
    return {
        "byte_states": draw_byte_states(jax.random.fold_in(key_list[9], 71), 0),
        "patch_len": jax.vmap(lambda own: uneven_parts(own, P_SEQ, S_DEV, MAXP, 2))(jax.random.split(key_list[1], N_SEQ)).reshape((N_SEQ, P_SEQ)).astype(jnp.int32),
        "shard_offset": plant(jax.random.randint(key_list[2], (N_SEQ,), 0, MAXP), jax.random.fold_in(key_list[2], 1), 0, MAXP - 1).astype(jnp.int32),
        "owner": jax.vmap(lambda own: jax.random.permutation(own, P_SEQ))(jax.random.split(key_list[3], N_SEQ)).reshape((N_SEQ, P_SEQ)).astype(jnp.int32),
        "cotangent": bell_draw(key_list[4], (P_SIZE, DG), 1.0, 6.0, ((0, 16), (1, 8))),
        "w_query": bell_draw(key_list[5], (DL, DL), DL ** -0.5, 0.1875),
        "w_key": bell_draw(key_list[6], (DL, DL), DL ** -0.5, 0.1875),
        "w_value": bell_draw(key_list[7], (DL, DL), DL ** -0.5, 0.1875),
        "w_out": bell_draw(key_list[8], (DL, DG), DL ** -0.5, 0.1875, ((1, 8),)),
    }


def shard_terms(carry, inputs, byte_pad, w_query, w_key, w_value, w_out):
    acc, grad_q, grad_k, grad_v, grad_o = carry
    lengths, offset, order, cot, shard = inputs
    width = byte_pad.shape[1]
    head_dim = width // HEADS
    scale = head_dim ** -0.5
    starts = shard * S_DEV + offset + jnp.cumsum(lengths) - lengths
    offsets = jnp.arange(MAXP, dtype=jnp.int32)
    index = (starts[:, None] + offsets[None, :]).astype(jnp.int32)
    valid = offsets[None, :] < lengths[:, None]
    window = jnp.where(valid[:, :, None], byte_pad[index], jnp.zeros((), jnp.bfloat16))
    inv_len = 1.0 / lengths.astype(jnp.float32)
    pooled = (jnp.sum(window.astype(jnp.float32), 1) * inv_len[:, None]).astype(jnp.bfloat16)
    flat = window.reshape(-1, width)
    query = jnp.dot(pooled, w_query, preferred_element_type=jnp.float32).astype(jnp.bfloat16)
    keys = jnp.dot(flat, w_key, preferred_element_type=jnp.float32).astype(jnp.bfloat16)
    values = jnp.dot(flat, w_value, preferred_element_type=jnp.float32).astype(jnp.bfloat16)
    rows = lengths.shape[0]
    q3 = query.reshape(rows, HEADS, head_dim).astype(jnp.float32)
    k4 = keys.reshape(rows, MAXP, HEADS, head_dim).astype(jnp.float32)
    v4 = values.reshape(rows, MAXP, HEADS, head_dim).astype(jnp.float32)
    scores = jnp.einsum('phd,pjhd->phj', q3, k4) * scale
    scores = jnp.where(valid[:, None, :], scores, -1e30)
    peak = jnp.max(scores, -1, keepdims=True)
    expo = jnp.exp(scores - peak)
    probs = expo / jnp.sum(expo, -1, keepdims=True)
    probs_b = probs.astype(jnp.bfloat16).astype(jnp.float32)
    attended = jnp.einsum('phj,pjhd->phd', probs_b, v4).astype(jnp.bfloat16).reshape(rows, width)
    d_att = jnp.dot(cot, w_out.T, preferred_element_type=jnp.float32).astype(jnp.bfloat16)
    d_out = d_att.reshape(rows, HEADS, head_dim).astype(jnp.float32)
    d_probs = jnp.einsum('phd,pjhd->phj', d_out, v4)
    d_scores = (probs * (d_probs - jnp.sum(probs * d_probs, -1, keepdims=True)) * scale).astype(jnp.bfloat16).astype(jnp.float32)
    d_values = jnp.einsum('phj,phd->pjhd', probs_b, d_out).astype(jnp.bfloat16).reshape(-1, width)
    d_keys = jnp.einsum('phj,phd->pjhd', d_scores, q3).astype(jnp.bfloat16).reshape(-1, width)
    d_query = jnp.einsum('phj,pjhd->phd', d_scores, k4).astype(jnp.bfloat16).reshape(rows, width)
    d_window = jnp.dot(d_keys, w_key.T, preferred_element_type=jnp.float32) + jnp.dot(d_values, w_value.T, preferred_element_type=jnp.float32)
    d_pooled = jnp.dot(d_query, w_query.T, preferred_element_type=jnp.float32) * inv_len[:, None]
    d_window = d_window.reshape(rows, MAXP, width) + jnp.where(valid[:, :, None], d_pooled[:, None, :], jnp.zeros((), jnp.float32))
    acc = acc.at[index.reshape(-1)].add(d_window.reshape(-1, width))
    grad_q = grad_q + jnp.dot(pooled.T, d_query, preferred_element_type=jnp.float32)
    grad_k = grad_k + jnp.dot(flat.T, d_keys, preferred_element_type=jnp.float32)
    grad_v = grad_v + jnp.dot(flat.T, d_values, preferred_element_type=jnp.float32)
    grad_o = grad_o + jnp.dot(attended.T, cot, preferred_element_type=jnp.float32)
    return (acc, grad_q, grad_k, grad_v, grad_o), attended[order]


def reference(byte_states, patch_len, shard_offset, owner, cotangent, w_query, w_key, w_value, w_out):
    width = byte_states.shape[1]
    byte_pad = jnp.concatenate([byte_states, jnp.zeros((RIM, width), jnp.bfloat16)], 0)
    init = (jnp.zeros((S + RIM, width), jnp.float32), jnp.zeros((width, width), jnp.float32),
            jnp.zeros((width, width), jnp.float32), jnp.zeros((width, width), jnp.float32),
            jnp.zeros((width, DG), jnp.float32))
    inputs = (patch_len, shard_offset, owner, cotangent.reshape(N_SEQ, P_SEQ, DG), jnp.arange(N_SEQ, dtype=jnp.int32))

    def step(carry, item):
        return shard_terms(carry, item, byte_pad, w_query, w_key, w_value, w_out)

    final, ordered = lax.scan(step, init, inputs)
    acc, grad_q, grad_k, grad_v, grad_o = final
    d_bytes = acc[:S].astype(jnp.bfloat16)
    d_qkv = jnp.stack([grad_q, grad_k, grad_v])
    return d_bytes, d_qkv, grad_o, ordered.reshape(P_SIZE, width)
```

```python
import jax
import jax.numpy as jnp
from jax import lax
from jax.experimental import pallas as pl
from jax.experimental.pallas import tpu as pltpu
from jax.sharding import PartitionSpec as P

HEADS = 16
MAXP = 16
LANES = 128
TILE = 256
F32, BF16, I16, I32 = jnp.float32, jnp.bfloat16, jnp.int16, jnp.int32
NT = (((1,), (1,)), ((), ()))
VMEM_BYTES = 56 * 1024 * 1024


def params():
    return pltpu.CompilerParams(vmem_limit_bytes=VMEM_BYTES)


def cost(flops, moved):
    return pl.CostEstimate(flops=flops, bytes_accessed=moved, transcendentals=0)


def whole(shape):
    return pl.BlockSpec(shape, lambda *_: (0,) * len(shape))


def smem():
    return pl.BlockSpec(memory_space=pltpu.SMEM)


def dot(a, b):
    return jnp.dot(a, b, preferred_element_type=F32)


def dot_nt(a, b):
    return lax.dot_general(a, b, NT, preferred_element_type=F32)


def coded(value):
    peak = jnp.max(jnp.abs(value), axis=0, keepdims=True)
    power = jnp.ceil(jnp.log2(jnp.maximum(peak, 1e-30)))
    scaled = jnp.round(value * jnp.exp2(15.0 - power))
    return jnp.clip(scaled, -32767.0, 32767.0), power


def to_i16(value):
    return value.astype(I32).astype(I16)


def from_i16(value):
    return value.astype(I32).astype(F32)


def unit(power):
    return jnp.exp2(from_i16(power) - 15.0)


def padded_rows(row_list, count):
    width = row_list[0].shape[1]
    at = lax.broadcasted_iota(I32, (count, width), 0)
    out = jnp.zeros((count, width), F32)
    for i, row in enumerate(row_list):
        out = jnp.where(at == i, jnp.broadcast_to(row, (count, width)), out)
    return out


def member_block(start_ref, end_ref, block, base, width):
    rows = pl.ds(block * LANES, LANES)
    parts = []
    for at in range(width // LANES):
        byte = base + at * LANES + lax.broadcasted_iota(I32, (LANES, LANES), 1)
        inside = (byte >= start_ref[rows, :]) & (byte < end_ref[rows, :])
        parts.append(jnp.where(inside, 1.0, 0.0).astype(BF16))
    return parts[0] if len(parts) == 1 else jnp.concatenate(parts, axis=1)


def on_blocks(bounds, blocks, base, width, body):
    for block in range(blocks):
        @pl.when((bounds[block] < base + width) & (bounds[block + 1] > base))
        def _():
            body(block)


def over_segment(value, place, left, op):
    size = value.shape[1]
    before, after = value, value
    for step in (1, 2, 4, 8):
        before = jnp.where(place >= step, op(before, pltpu.roll(before, step, 1)), before)
        after = jnp.where(left >= step, op(after, pltpu.roll(after, size - step, 1)), after)
    return before, after


def head_rows(rows, dim):
    count, width = rows.shape
    return jnp.concatenate(
        [jnp.broadcast_to(rows[i:i + 1], (dim, width)) for i in range(count)], axis=0
    )


def split2(value):
    high = value.astype(BF16)
    return jnp.concatenate([high, (value - high.astype(F32)).astype(BF16)], axis=0)


def att_grad_kernel(w_ref, cot_ref, out_ref):
    own = w_ref.shape[0]
    part = dot_nt(w_ref[...], cot_ref[...])
    codes, power = coded(part)
    out_ref[0, :own, :] = to_i16(codes)
    out_ref[0, own:, :] = to_i16(jnp.broadcast_to(power, (16, power.shape[1])))


def att_grad(w_out, cot, groups):
    width, cols = w_out.shape
    rows = cot.shape[0]
    own = width // groups
    return pl.pallas_call(
        att_grad_kernel,
        grid=(groups,),
        in_specs=[pl.BlockSpec((own, cols), lambda i: (i, 0)), whole((rows, cols))],
        out_specs=pl.BlockSpec((1, own + 16, rows), lambda i: (i, 0, 0)),
        out_shape=jax.ShapeDtypeStruct((groups, own + 16, rows), I16),
        compiler_params=params(),
        cost_estimate=cost(2 * width * cols * rows, 4 << 20),
        name="att_grad",
    )(w_out, cot)


def forward_kernel(
    member, offset, len_ref, x_ref, rim_ref, wk_ref, wv_ref, wq_ref,
    kv_ref, qexp_ref, probs_ref, geo_ref, att_ref, pooled_ref, start_ref, end_ref, inv_ref, bounds,
    w_t, wq_t, acc, lhs, inv_col, exp, att_acc,
):
    step, steps = pl.program_id(0), pl.num_programs(0)
    tile = x_ref.shape[0]
    rim = rim_ref.shape[0]
    patches = len_ref.shape[1]
    blocks = patches // LANES
    own = wk_ref.shape[1]
    dim = 64
    s_dev = kv_ref.shape[1] - rim

    @pl.when(step == 0)
    def _():
        length = len_ref[...].astype(F32)
        before = lax.broadcasted_iota(I32, (patches, patches), 0)
        after = lax.broadcasted_iota(I32, (patches, patches), 1)
        off = offset[0].astype(F32)
        wide = jnp.broadcast_to(length, (LANES, patches)).astype(BF16)
        lower = jnp.where(after < before, 1.0, 0.0).astype(BF16)
        same = jnp.where(after == before, 1.0, 0.0).astype(BF16)
        start_col = (dot_nt(lower, wide) + off).astype(I32)
        len_col = dot_nt(same, wide)
        start_ref[...] = start_col
        end_ref[...] = start_col + len_col.astype(I32)
        inv_col[...] = 1.0 / len_col
        eight = jnp.broadcast_to(length, (8, patches))
        inv_ref[...] = 1.0 / eight
        upper = jnp.where(before < after, 1.0, 0.0).astype(BF16)
        start_row = (dot(eight.astype(BF16), upper) + off).astype(I32)
        at = lax.broadcasted_iota(I32, (16, patches), 0)
        start_row = jnp.concatenate([start_row, start_row], axis=0)
        geo = jnp.where(at == 0, start_row >> 6, jnp.where(at == 1, start_row & 63, 0)).astype(F32)
        geo = jnp.where(at == 2, jnp.broadcast_to(length, (16, patches)), geo)
        lhs[own:own + 16, :] = geo.astype(BF16)
        lane = lax.broadcasted_iota(I32, (1, patches), 1)
        for block in range(blocks + 1):
            total = jnp.sum(jnp.where(lane < block * LANES, length, 0.0))
            bounds[block] = (total + off).astype(I32)
        w_t[:own, :] = wk_ref[...].astype(F32).T.astype(BF16)
        w_t[own:, :] = wv_ref[...].astype(F32).T.astype(BF16)
        wq_t[...] = wq_ref[...].astype(F32).T.astype(BF16)
        acc[...] = jnp.zeros_like(acc)

    def project(rows, base, width):
        kv_ref[:, pl.ds(base, width)] = dot_nt(w_t[...], rows).astype(BF16)

        def pool(block):
            at = pl.ds(block * LANES, LANES)
            acc[at, :] += dot(member_block(start_ref, end_ref, block, base, width), rows)

        on_blocks(bounds, blocks, base, width, pool)

    project(x_ref[...], pl.multiple_of(step * tile, tile), tile)

    @pl.when(step == steps - 1)
    def _():
        project(rim_ref[...], s_dev, rim)
        pooled = (acc[...] * inv_col[:, :1]).astype(BF16)
        pooled_ref[...] = pooled
        lhs[:own, :] = dot_nt(wq_t[...], pooled).astype(BF16)

        def score(base, width):
            exp[:, :width] = jnp.zeros((own + 16, width), F32)

            def expand(block):
                exp[:, :width] += dot(
                    lhs[:, block * LANES:(block + 1) * LANES],
                    member_block(start_ref, end_ref, block, base, width),
                )

            on_blocks(bounds, blocks, base, width, expand)
            at = pl.ds(base, width)
            query = exp[:own, :width]
            qexp_ref[:, at] = query.astype(BF16)
            product = query * kv_ref[:own, at].astype(F32)
            rows = [jnp.sum(product[h * dim:(h + 1) * dim], axis=0, keepdims=True) for h in range(own // dim)]
            probs_ref[:, at] = padded_rows(rows, 8) * (dim ** -0.5)
            geo = exp[own:own + 8, :width]
            byte = (base + lax.broadcasted_iota(I32, (1, width), 1)).astype(F32)
            place = byte - (64.0 * geo[0:1] + geo[1:2])
            geo_ref[:, at] = padded_rows([place, geo[2:3] - 1.0 - place], 8)

        def tiles(body):
            def go(i, carry):
                body(pl.multiple_of(i * tile, tile), tile)
                return carry

            lax.fori_loop(0, steps, go, 0)
            body(s_dev, rim)

        tiles(score)
        place, left = geo_ref[0:1, :], geo_ref[1:2, :]
        scores = probs_ref[...]
        before, after = over_segment(scores, place, left, jnp.maximum)
        expo = jnp.exp(scores - jnp.maximum(before, after))
        before, after = over_segment(expo, place, left, jnp.add)
        probs_ref[...] = jnp.where(left >= 0.0, expo / (before + (after - expo)), 0.0)
        att_acc[...] = jnp.zeros_like(att_acc)

        def attend(base, width):
            at = pl.ds(base, width)
            probs_b = probs_ref[:, at].astype(BF16).astype(F32)[:own // dim]
            both = split2(head_rows(probs_b, dim) * kv_ref[own:, at].astype(F32))

            def add(block):
                att_acc[:, block * LANES:(block + 1) * LANES] += dot_nt(
                    both, member_block(start_ref, end_ref, block, base, width)
                )

            on_blocks(bounds, blocks, base, width, add)

        tiles(attend)
        att_ref[...] = (att_acc[:own, :] + att_acc[own:, :]).astype(BF16)


def forward(member, offset, lengths, x, rim, w_key, w_value, w_query, groups):
    s_dev, width = x.shape
    patches = lengths.shape[1]
    own = width // groups
    total = s_dev + rim.shape[0]
    col = pl.BlockSpec((width, own), lambda i, member, offset: (0, member[0]))
    outs = [
        ((2 * own, total), BF16), ((own, total), BF16), ((8, total), F32), ((8, total), F32),
        ((own, patches), BF16), ((patches, width), BF16), ((patches, LANES), I32),
        ((patches, LANES), I32), ((8, patches), F32),
    ]
    return pl.pallas_call(
        forward_kernel,
        grid_spec=pltpu.PrefetchScalarGridSpec(
            num_scalar_prefetch=2,
            grid=(s_dev // TILE,),
            in_specs=[
                whole(lengths.shape),
                pl.BlockSpec((TILE, width), lambda i, *_: (i, 0)),
                whole(rim.shape), col, col, col,
            ],
            out_specs=[whole(shape) for shape, _ in outs] + [smem()],
            scratch_shapes=[
                pltpu.VMEM((2 * own, width), BF16),
                pltpu.VMEM((own, width), BF16),
                pltpu.VMEM((patches, width), F32),
                pltpu.VMEM((own + 16, patches), BF16),
                pltpu.VMEM((patches, LANES), F32),
                pltpu.VMEM((own + 16, TILE), F32),
                pltpu.VMEM((2 * own, patches), F32),
            ],
        ),
        out_shape=[jax.ShapeDtypeStruct(shape, kind) for shape, kind in outs]
        + [jax.ShapeDtypeStruct((8,), I32)],
        compiler_params=params(),
        cost_estimate=cost(8 << 30, 12 << 20),
        name="forward",
    )(member, offset, lengths, x, rim, w_key, w_value, w_query)


def backward_kernel(
    bounds, x_ref, rim_ref, got_ref, kv_ref, qexp_ref, probs_ref, geo_ref, pooled_ref, start_ref, end_ref,
    grad_ref, factor_ref,
    d_kv, d_att, d_probs, d_scores, exp, dq_acc, acc,
):
    step, steps = pl.program_id(0), pl.num_programs(0)
    tile = x_ref.shape[0]
    rim = rim_ref.shape[0]
    own, total = qexp_ref.shape
    patches = pooled_ref.shape[0]
    blocks = patches // LANES
    s_dev = total - rim
    dim = 64
    heads = own // dim
    sources = got_ref.shape[0]

    def tiles(body):
        def go(i, carry):
            body(pl.multiple_of(i * tile, tile), tile)
            return carry

        lax.fori_loop(0, steps, go, 0)
        body(s_dev, rim)

    @pl.when(step == 0)
    def _():
        summed = jnp.zeros((own, patches), F32)
        for source in range(sources):
            summed = summed + from_i16(got_ref[source, :own, :]) * unit(got_ref[source, own:, :])[0:1]
        d_att[...] = summed.astype(BF16)
        factor_ref[:own, :] = summed.astype(BF16)

        def first(base, width):
            exp[:, :width] = jnp.zeros((own, width), F32)

            def expand(block):
                exp[:, :width] += dot(
                    d_att[:, block * LANES:(block + 1) * LANES],
                    member_block(start_ref, end_ref, block, base, width),
                )

            on_blocks(bounds, blocks, base, width, expand)
            at = pl.ds(base, width)
            d_out = exp[:, :width]
            product = d_out * kv_ref[own:, at].astype(F32)
            rows = [jnp.sum(product[h * dim:(h + 1) * dim], axis=0, keepdims=True) for h in range(heads)]
            d_probs[:, at] = padded_rows(rows, 8)
            probs_b = probs_ref[:, at].astype(BF16).astype(F32)[:heads]
            d_kv[own:, at] = (head_rows(probs_b, dim) * d_out).astype(BF16)

        tiles(first)
        place, left = geo_ref[0:1, :], geo_ref[1:2, :]
        probs = probs_ref[...]
        weighted = probs * d_probs[...]
        before, after = over_segment(weighted, place, left, jnp.add)
        inner = before + (after - weighted)
        slope = jnp.where(left >= 0.0, probs * (d_probs[...] - inner) * (dim ** -0.5), 0.0)
        d_scores[...] = slope.astype(BF16).astype(F32)
        dq_acc[...] = jnp.zeros_like(dq_acc)
        acc[...] = jnp.zeros_like(acc)

        def second(base, width):
            at = pl.ds(base, width)
            wide = head_rows(d_scores[:, at][:heads], dim)
            d_kv[:own, at] = (wide * qexp_ref[:, at].astype(F32)).astype(BF16)
            both = split2(wide * kv_ref[:own, at].astype(F32))

            def add(block):
                dq_acc[:, block * LANES:(block + 1) * LANES] += dot_nt(
                    both, member_block(start_ref, end_ref, block, base, width)
                )

            on_blocks(bounds, blocks, base, width, add)

        tiles(second)
        factor_ref[own:2 * own, :] = (dq_acc[:own, :] + dq_acc[own:, :]).astype(BF16)
        probs_b = probs.astype(BF16).astype(F32)
        rows = padded_rows(
            [d_scores[h:h + 1, :] for h in range(heads)] + [probs_b[h:h + 1, :] for h in range(heads)], 8
        )
        groups = [rows[:, at:at + patches] for at in range(0, s_dev, patches)]
        last = jnp.concatenate([rows[:, s_dev:], jnp.zeros((8, patches - rim), F32)], axis=1)
        spare = factor_ref.shape[0] - 2 * own - 8 * (len(groups) + 1)
        stack = groups + [last] + ([jnp.zeros((spare, patches), F32)] if spare else [])
        factor_ref[2 * own:, :] = jnp.concatenate(stack, axis=0).astype(BF16)

    acc[...] += dot(d_kv[:, pl.ds(pl.multiple_of(step * tile, tile), tile)], x_ref[...])

    @pl.when(step == steps - 1)
    def _():
        acc[...] += dot(d_kv[:, s_dev:], rim_ref[...])
        grad_q = dot(factor_ref[own:2 * own, :], pooled_ref[...])
        powers = []
        parts = grad_ref.shape[0]
        for k, grad in enumerate((grad_q, acc[:own, :], acc[own:, :])):
            codes, power = coded(grad.T)
            powers.append(power)
            rows = codes.shape[0] // parts
            spread = codes.reshape(rows // 8, parts, 8, own)
            for part in range(parts):
                grad_ref[part, k * rows:(k + 1) * rows, :] = to_i16(spread[:, part].reshape(rows, own))
        tail = to_i16(padded_rows(powers, 16))
        for part in range(parts):
            grad_ref[part, 3 * rows:, :] = tail


def backward(bounds, x, rim, got, kv, qexp, probs, geo, pooled, start, end, parts):
    s_dev, width = x.shape
    own, total = qexp.shape
    patches = pooled.shape[0]
    extra = -(-8 * (s_dev // patches + 1) // 16) * 16
    operands = (bounds, x, rim, got, kv, qexp, probs, geo, pooled, start, end)
    rows = width // parts
    return pl.pallas_call(
        backward_kernel,
        grid=(s_dev // TILE,),
        in_specs=[smem(), pl.BlockSpec((TILE, width), lambda i: (i, 0))] + [whole(v.shape) for v in operands[2:]],
        out_specs=[whole((parts, 3 * rows + 16, own)), whole((2 * own + extra, patches))],
        out_shape=[
            jax.ShapeDtypeStruct((parts, 3 * rows + 16, own), I16),
            jax.ShapeDtypeStruct((2 * own + extra, patches), BF16),
        ],
        scratch_shapes=[
            pltpu.VMEM((2 * own, total), BF16),
            pltpu.VMEM((own, patches), BF16),
            pltpu.VMEM((8, total), F32),
            pltpu.VMEM((8, total), F32),
            pltpu.VMEM((own, TILE), F32),
            pltpu.VMEM((2 * own, patches), F32),
            pltpu.VMEM((2 * own, width), F32),
        ],
        compiler_params=params(),
        cost_estimate=cost(6 << 30, 16 << 20),
        name="backward",
    )(*operands)


def out_grad_kernel(member, att_ref, cot_ref, owner_ref, out_ref, rows_ref):
    groups, own, patches = att_ref.shape
    att = att_ref[...].reshape(groups * own, patches)
    codes, power = coded(dot(att, cot_ref[...]))
    parts = out_ref.shape[0]
    rows = codes.shape[0] // parts
    slabs = codes.shape[1] // LANES
    tail = to_i16(padded_rows([power[:, at * LANES:(at + 1) * LANES] for at in range(slabs)], 16))
    for part in range(parts):
        for at in range(slabs):
            block = codes[part * rows:(part + 1) * rows, at * LANES:(at + 1) * LANES]
            out_ref[part, at * rows:(at + 1) * rows, :] = to_i16(block)
        out_ref[part, slabs * rows:, :] = tail
    count = rows_ref.shape[0]
    order = jnp.broadcast_to(owner_ref[...], (8, patches))
    order = pltpu.roll(order, lax.rem(patches - member[0] * count, patches), 1)[0:1, :LANES]
    pick = jnp.where(lax.broadcasted_iota(I32, (patches, LANES), 0) == order, 1.0, 0.0).astype(BF16)
    rows_ref[...] = dot(att, pick).T[:count].astype(BF16)


def out_grad(member, att, cot, owner, parts):
    groups, own, patches = att.shape
    width, cols = groups * own, cot.shape[1]
    rows = cols // LANES * (width // parts) + 16
    count = patches // groups
    return pl.pallas_call(
        out_grad_kernel,
        in_specs=[smem()] + [pl.BlockSpec(memory_space=pltpu.VMEM)] * 3,
        out_specs=[pl.BlockSpec(memory_space=pltpu.VMEM)] * 2,
        out_shape=[
            jax.ShapeDtypeStruct((parts, rows, LANES), I16),
            jax.ShapeDtypeStruct((count, width), BF16),
        ],
        compiler_params=params(),
        cost_estimate=cost(2 * width * cols * patches, 4 << 20),
        name="out_grad",
    )(member, att, cot, owner)


def out_sum_kernel(got_ref, out_ref):
    sources, rows, lanes = got_ref.shape
    slabs = out_ref.shape[1] // lanes
    count = out_ref.shape[0]
    for at in range(slabs):
        total = jnp.zeros((count, lanes), F32)
        for source in range(sources):
            scale = unit(got_ref[source, slabs * count:, :])[at:at + 1]
            total = total + from_i16(got_ref[source, at * count:(at + 1) * count, :]) * scale
        out_ref[:, at * lanes:(at + 1) * lanes] = total.astype(BF16)


def out_sum(got, cols):
    slabs = cols // LANES
    count = (got.shape[1] - 16) // slabs
    return pl.pallas_call(
        out_sum_kernel,
        in_specs=[pl.BlockSpec(memory_space=pltpu.VMEM)],
        out_specs=pl.BlockSpec(memory_space=pltpu.VMEM),
        out_shape=jax.ShapeDtypeStruct((count, cols), BF16),
        compiler_params=params(),
        cost_estimate=cost(1 << 20, 2 << 20),
        name="out_sum",
    )(got)


def qkv_sum_kernel(got_ref, out_ref):
    sources, rows, lanes = got_ref.shape
    groups = out_ref.shape[0]
    count = (rows - 16) // 3
    totals = []
    for k in range(3):
        total = jnp.zeros((count, lanes), F32)
        for source in range(sources):
            scale = unit(got_ref[source, 3 * count:, :])[k:k + 1]
            total = total + from_i16(got_ref[source, k * count:(k + 1) * count, :]) * scale
        totals.append(total)
    spare = jnp.zeros((8, lanes), F32)
    for group in range(groups):
        rows = [total[group * 8:(group + 1) * 8] for total in totals] + [spare]
        out_ref[group] = jnp.concatenate(rows, axis=0).astype(BF16)


def qkv_sum(got, groups):
    return pl.pallas_call(
        qkv_sum_kernel,
        in_specs=[pl.BlockSpec(memory_space=pltpu.VMEM)],
        out_specs=pl.BlockSpec(memory_space=pltpu.VMEM),
        out_shape=jax.ShapeDtypeStruct((groups, 32, LANES), BF16),
        compiler_params=params(),
        cost_estimate=cost(1 << 20, 2 << 20),
        name="qkv_sum",
    )(got)


def bytes_kernel(
    member, bounds, factor_ref, pooled_ref, wq_ref, wk_own, wv_own, wq_own, inv_ref, start_ref, end_ref,
    out_ref, head_ref, tail_ref,
    lhs, shares, exp, d_kv, w_own,
):
    step, steps = pl.program_id(0), pl.num_programs(0)
    groups, rows, patches = factor_ref.shape
    width = wq_ref.shape[0]
    own = wq_own.shape[0]
    dim = 64
    heads = own // dim
    blocks = patches // LANES
    tile = out_ref.shape[0]
    total = shares.shape[2]
    s_dev = steps * tile
    rim = total - s_dev

    @pl.when(step == 0)
    def _():
        lhs[:width, :] = dot(pooled_ref[...], wq_ref[...]).T.astype(BF16)
        lhs[width:2 * width, :] = factor_ref[:, :own, :].reshape(width, patches)
        d_query = factor_ref[:, own:2 * own, :].reshape(width, patches)
        lhs[2 * width:, :] = split2(dot(wq_own[...], d_query) * inv_ref[0:1, :])
        w_own[:, :width] = wk_own[...]
        w_own[:, width:] = wv_own[...]
        for group in range(groups):
            table = factor_ref[group, 2 * own:, :].astype(F32)
            for at in range(s_dev // patches):
                shares[group, :, at * patches:(at + 1) * patches] = table[8 * at:8 * at + 8]
            at = s_dev // patches
            shares[group, :, s_dev:] = table[8 * at:8 * at + 8, :rim]

    def tile_grad(base, span):
        exp[:, :span] = jnp.zeros((exp.shape[0], span), F32)

        def expand(block):
            exp[:, :span] += dot(
                lhs[:, block * LANES:(block + 1) * LANES],
                member_block(start_ref, end_ref, block, base, span),
            )

        on_blocks(bounds, blocks, base, span, expand)
        at = pl.ds(base, span)
        for group in range(groups):
            share = shares[group, :, at]
            for h in range(heads):
                row = group * own + h * dim
                slab = slice(row, row + dim)
                d_kv[slab, :span] = (share[h:h + 1] * exp[slab, :span]).astype(BF16)
                slab_v = slice(width + row, width + row + dim)
                d_kv[slab_v, :span] = (share[heads + h:heads + h + 1] * exp[slab_v, :span]).astype(BF16)
        grad = dot(w_own[...], d_kv[:, :span])
        grad = grad + (exp[2 * width:2 * width + own, :span] + exp[2 * width + own:, :span])
        return grad.T

    grad = tile_grad(pl.multiple_of(step * tile, tile), tile)
    out_ref[...] = grad.astype(BF16)

    @pl.when(step == 0)
    def _():
        head_ref[...] = grad[:16]

    @pl.when(step == steps - 1)
    def _():
        tail_ref[...] = tile_grad(s_dev, rim)[:16]


def byte_grads(member, bounds, factors, pooled, w_query, w_key, w_value, inv, start, end, s_dev):
    groups, rows, patches = factors.shape
    width = w_query.shape[0]
    own = width // groups
    rim = LANES
    mine = pl.BlockSpec((own, width), lambda i, member, bounds: (member[0], 0))
    return pl.pallas_call(
        bytes_kernel,
        grid_spec=pltpu.PrefetchScalarGridSpec(
            num_scalar_prefetch=2,
            grid=(s_dev // TILE,),
            in_specs=[
                whole(factors.shape), whole(pooled.shape), whole(w_query.shape), mine, mine, mine,
                whole(inv.shape), whole(start.shape), whole(end.shape),
            ],
            out_specs=[pl.BlockSpec((TILE, own), lambda i, *_: (i, 0)), whole((16, own)), whole((16, own))],
            scratch_shapes=[
                pltpu.VMEM((2 * width + 2 * own, patches), BF16),
                pltpu.VMEM((groups, 8, s_dev + rim), F32),
                pltpu.VMEM((2 * width + 2 * own, TILE), F32),
                pltpu.VMEM((2 * width, TILE), BF16),
                pltpu.VMEM((own, 2 * width), BF16),
            ],
        ),
        out_shape=[
            jax.ShapeDtypeStruct((s_dev, own), BF16),
            jax.ShapeDtypeStruct((16, own), F32),
            jax.ShapeDtypeStruct((16, own), F32),
        ],
        compiler_params=params(),
        cost_estimate=cost(8 << 30, 8 << 20),
        name="byte_grads",
    )(member, bounds, factors, pooled, w_query, w_key, w_value, w_query, inv, start, end)


def shifted(value, axis, steps):
    count = lax.axis_size(axis)
    first, last = (max(0, -steps), min(count, count - steps))
    return lax.ppermute(value, axis, [(source, source + steps) for source in range(first, last)])


def swap(value, axis):
    return lax.all_to_all(value, axis, split_axis=0, concat_axis=0, tiled=True)


def collect(value, axis):
    count = lax.axis_size(axis)
    return swap(jnp.broadcast_to(value[None], (count,) + value.shape), axis)


def local(byte_states, patch_len, shard_offset, owner, cotangent, w_query, w_key, w_value, w_out):
    s_dev, width = byte_states.shape
    groups = lax.axis_size("patch")
    parts = lax.axis_size("seq")
    member = lax.axis_index("patch").astype(I32).reshape(1)
    following = shifted(byte_states[:MAXP], "seq", -1)
    rim = jnp.pad(following, ((0, LANES - MAXP), (0, 0)))

    got_att = swap(att_grad(w_out, cotangent, groups), "patch")
    kv, qexp, probs, geo, att, pooled, start, end, inv, bounds = forward(
        member, shard_offset, patch_len, byte_states, rim, w_key, w_value, w_query, groups
    )
    grads, factor = backward(bounds, byte_states, rim, got_att, kv, qexp, probs, geo, pooled, start, end, parts)
    coded_out, patch_rows = out_grad(member, collect(att, "patch"), cotangent, owner, parts)
    got_qkv = swap(grads, "seq")
    got_out = swap(coded_out, "seq")
    d_wout = collect(out_sum(got_out, cotangent.shape[1]), "seq").reshape(width, -1).astype(F32)
    own_qkv = swap(qkv_sum(got_qkv, groups), "patch")
    all_qkv = collect(own_qkv, "seq")[:, :, :24].reshape(parts, groups, 3, 8, -1)
    d_qkv = all_qkv.transpose(2, 0, 3, 1, 4).reshape(3, width // groups, width).astype(F32)
    d_bytes, head, tail = byte_grads(
        member, bounds, collect(factor, "patch"), pooled, w_query, w_key, w_value, inv, start, end, s_dev
    )
    first = (head + shifted(tail, "seq", 1)).astype(BF16)
    d_bytes = lax.dynamic_update_slice(d_bytes, first, (0, 0))
    return (d_bytes, d_qkv, d_wout, patch_rows)


def solution(mesh):
    return jax.shard_map(
        local,
        mesh=mesh,
        in_specs=(
            P("seq", None), P("seq", None), P("seq"), P("seq", None), P("seq", "patch"),
            P(), P(), P(), P(None, "patch"),
        ),
        out_specs=(P("seq", "patch"), P(None, "patch", None), P(None, "patch"), P(("seq", "patch"), None)),
        check_vma=False,
    )
```

```python
import jax
import jax.numpy as jnp
from jax import lax
from jax.experimental import pallas as pl
from jax.experimental.pallas import tpu as pltpu
from jax.sharding import PartitionSpec as P

HEADS = 16
MAXP = 16
LANES = 128
TILE = 256
UNROLL = 4
F32, BF16, I16, I32 = jnp.float32, jnp.bfloat16, jnp.int16, jnp.int32
NT = (((1,), (1,)), ((), ()))
VMEM_BYTES = 56 * 1024 * 1024


def params():
    return pltpu.CompilerParams(vmem_limit_bytes=VMEM_BYTES)


def cost(flops, moved):
    return pl.CostEstimate(flops=flops, bytes_accessed=moved, transcendentals=0)


def whole(shape):
    return pl.BlockSpec(shape, lambda *_: (0,) * len(shape))


def smem():
    return pl.BlockSpec(memory_space=pltpu.SMEM)


def dot(a, b):
    return jnp.dot(a, b, preferred_element_type=F32)


def dot_nt(a, b):
    return lax.dot_general(a, b, NT, preferred_element_type=F32)


def coded(value):
    peak = jnp.max(jnp.abs(value), axis=0, keepdims=True)
    power = jnp.ceil(jnp.log2(jnp.maximum(peak, 1e-30)))
    return jnp.round(value * (32767.0 * jnp.exp2(-power))), power


def to_i16(value):
    return value.astype(I32).astype(I16)


def from_i16(value):
    return value.astype(I32).astype(F32)


def unit(power):
    return jnp.exp2(from_i16(power)) * (1.0 / 32767.0)


def padded_rows(row_list, count):
    width = row_list[0].shape[1]
    at = lax.broadcasted_iota(I32, (count, width), 0)
    out = jnp.zeros((count, width), F32)
    for i, row in enumerate(row_list):
        out = jnp.where(at == i, jnp.broadcast_to(row, (count, width)), out)
    return out


def window(bounds, blocks, base):
    block = jnp.int32(0)
    for at in range(1, blocks - 1):
        block = block + (bounds[at] <= base).astype(I32)
    return block


def patch_major(start_ref, end_ref, first, count, base, width):
    rows = pl.ds(pl.multiple_of(first, LANES), count)
    start, end = start_ref[rows, :], end_ref[rows, :]
    parts = []
    for at in range(0, width, LANES):
        byte = base + at + lax.broadcasted_iota(I32, (count, LANES), 1)
        parts.append(jnp.where((byte >= start) & (byte < end), 1.0, 0.0).astype(BF16))
    return parts[0] if len(parts) == 1 else jnp.concatenate(parts, axis=1)


def byte_major(row_ref, first, count, base, width):
    lanes = pl.ds(pl.multiple_of(first, LANES), count)
    byte = base + lax.broadcasted_iota(I32, (width, count), 0)
    inside = (byte >= row_ref[0:1, lanes]) & (byte < row_ref[8:9, lanes])
    return jnp.where(inside, 1.0, 0.0).astype(BF16)


def over_tiles(s_dev, rim, body):
    def go(i, carry):
        for at in range(UNROLL):
            body(pl.multiple_of(i * (UNROLL * LANES) + at * LANES, LANES))
        return carry

    lax.fori_loop(0, s_dev // (UNROLL * LANES), go, 0)
    for base in range(s_dev, s_dev + rim, LANES):
        body(base)


def columns_of(row_ref, start_ref, end_ref):
    patches = row_ref.shape[1]
    start_ref[...] = jnp.broadcast_to(row_ref[0:1, :], (LANES, patches)).T
    end_ref[...] = jnp.broadcast_to(row_ref[8:9, :], (LANES, patches)).T


def send_copies(source, target, sems):
    copies = [pltpu.make_async_copy(source, target.at[i], sems.at[i]) for i in range(target.shape[0])]
    for copy in copies:
        copy.start()
    return copies


def over_segment(value, place, left, op):
    size = value.shape[1]
    before, after = value, value
    for step in (1, 2, 4, 8):
        before = jnp.where(place >= step, op(before, pltpu.roll(before, step, 1)), before)
        after = jnp.where(left >= step, op(after, pltpu.roll(after, size - step, 1)), after)
    return before, after


def head_rows(rows, dim):
    count, width = rows.shape
    return jnp.concatenate(
        [jnp.broadcast_to(rows[i:i + 1], (dim, width)) for i in range(count)], axis=0
    )


def split2(value):
    high = value.astype(BF16)
    return jnp.concatenate([high, (value - high.astype(F32)).astype(BF16)], axis=0)


def att_grad_kernel(w_ref, cot_ref, out_ref, cot_t):
    groups = out_ref.shape[0]
    own = w_ref.shape[0] // groups
    cot_t[...] = cot_ref[...].astype(F32).T.astype(BF16)
    for group in range(groups):
        codes, power = coded(dot(w_ref[group * own:(group + 1) * own, :], cot_t[...]))
        out_ref[group, :own, :] = to_i16(codes)
        out_ref[group, own:, :] = to_i16(jnp.broadcast_to(power, (16, power.shape[1])))


def att_grad(w_out, cot, groups):
    width, cols = w_out.shape
    rows = cot.shape[0]
    own = width // groups
    return pl.pallas_call(
        att_grad_kernel,
        in_specs=[pl.BlockSpec(memory_space=pltpu.VMEM)] * 2,
        out_specs=pl.BlockSpec(memory_space=pltpu.VMEM),
        out_shape=jax.ShapeDtypeStruct((groups, own + 16, rows), I16),
        scratch_shapes=[pltpu.VMEM((cols, rows), BF16)],
        compiler_params=params(),
        cost_estimate=cost(2 * width * cols * rows, 4 << 20),
        name="att_grad",
    )(w_out, cot)


def forward_kernel(
    member, offset, len_ref, x_hbm, rim_ref, wk_ref, wv_ref, wq_ref,
    kv_hbm, pooled_hbm, att_hbm, query_ref, probs_ref, geo_ref, row_ref, bounds,
    x_ref, kv_ref, pooled_ref, att_ref, w_kv, wq_t, acc, lhs, start_ref, end_ref, inv_col, att_acc,
    x_sems, out_sems, att_sems,
):
    rim = rim_ref.shape[0]
    patches = len_ref.shape[1]
    blocks = patches // LANES
    own = wk_ref.shape[1]
    dim = 64
    heads = own // dim
    s_dev = x_hbm.shape[0]
    chunks = x_sems.shape[0]
    chunk = s_dev // chunks
    loads = []
    for i in range(chunks):
        at = slice(i * chunk, (i + 1) * chunk)
        loads.append(pltpu.make_async_copy(x_hbm.at[at, :], x_ref.at[at, :], x_sems.at[i]))
        loads[-1].start()

    length = len_ref[...].astype(F32)
    before = lax.broadcasted_iota(I32, (patches, patches), 0)
    after = lax.broadcasted_iota(I32, (patches, patches), 1)
    off = offset[0].astype(F32)
    eight = jnp.broadcast_to(length, (8, patches))
    upper = jnp.where(before < after, 1.0, 0.0).astype(BF16)
    start_row = (dot(eight.astype(BF16), upper) + off).astype(I32)
    row_ref[:8, :] = start_row
    row_ref[8:, :] = start_row + eight.astype(I32)
    columns_of(row_ref, start_ref, end_ref)
    inv_col[...] = 1.0 / jnp.broadcast_to(length, (LANES, patches)).T
    at = lax.broadcasted_iota(I32, (16, patches), 0)
    both = jnp.concatenate([start_row, start_row], axis=0)
    geo = jnp.where(at == 0, both >> 6, jnp.where(at == 1, both & 63, 0)).astype(F32)
    geo = jnp.where(at == 2, jnp.broadcast_to(length, (16, patches)), geo)
    lhs[own:own + 16, :] = geo.astype(BF16)
    lane = lax.broadcasted_iota(I32, (1, patches), 1)
    for block in range(blocks + 1):
        total = jnp.sum(jnp.where(lane < block * LANES, length, 0.0))
        bounds[block] = (total + off).astype(I32)

    def crowded(i, found):
        base = i * TILE
        third = window(bounds, blocks, base) + 2
        return found | ((third < blocks) & (bounds[third] < base + TILE)).astype(I32)

    bounds[blocks + 1] = lax.fori_loop(0, s_dev // TILE, crowded, jnp.int32(0))
    w_kv[:, :own] = wk_ref[...]
    w_kv[:, own:] = wv_ref[...]
    wq_t[...] = wq_ref[...].astype(F32).T.astype(BF16)
    acc[...] = jnp.zeros_like(acc)

    def project(rows, base, width):
        kv_ref[:, pl.ds(base, width)] = dot(rows, w_kv[...]).T.astype(BF16)
        first = pl.multiple_of(window(bounds, blocks, base) * LANES, LANES)
        at = pl.ds(first, 2 * LANES)
        acc[at, :] += dot(patch_major(start_ref, end_ref, first, 2 * LANES, base, width), rows)

    for i in range(chunks):
        loads[i].wait()
        for at in range(i * chunk, (i + 1) * chunk, TILE):
            project(x_ref[at:at + TILE, :], at, TILE)
    project(rim_ref[...], s_dev, rim)

    @pl.when(bounds[blocks + 1] > 0)
    def _():
        def rest(i, carry):
            base = pl.multiple_of(i * TILE, TILE)
            third = window(bounds, blocks, base) + 2

            @pl.when((third < blocks) & (bounds[third] < base + TILE))
            def _():
                first = pl.multiple_of(third * LANES, LANES)
                acc[pl.ds(first, LANES), :] += dot(
                    patch_major(start_ref, end_ref, first, LANES, base, TILE), x_ref[pl.ds(base, TILE), :]
                )

            return carry

        lax.fori_loop(0, s_dev // TILE, rest, 0)

    kv_copy = pltpu.make_async_copy(kv_ref, kv_hbm, out_sems.at[0])
    kv_copy.start()
    pooled = (acc[...] * inv_col[:, :1]).astype(BF16)
    pooled_ref[...] = pooled
    pooled_copy = pltpu.make_async_copy(pooled_ref, pooled_hbm, out_sems.at[1])
    pooled_copy.start()
    query = dot_nt(wq_t[...], pooled).astype(BF16)
    lhs[:own, :] = query
    query_ref[...] = query

    def score(base):
        first = pl.multiple_of(window(bounds, blocks, base) * LANES, LANES)
        exp = dot(
            lhs[:, pl.ds(first, 2 * LANES)],
            patch_major(start_ref, end_ref, first, 2 * LANES, base, LANES),
        )
        at = pl.ds(base, LANES)
        product = exp[:own] * kv_ref[:own, at].astype(F32)
        rows = [jnp.sum(product[h * dim:(h + 1) * dim], axis=0, keepdims=True) for h in range(heads)]
        probs_ref[:, at] = padded_rows(rows, 8) * (dim ** -0.5)
        geo = exp[own:own + 8]
        byte = (base + lax.broadcasted_iota(I32, (1, LANES), 1)).astype(F32)
        place = byte - (64.0 * geo[0:1] + geo[1:2])
        geo_ref[:, at] = padded_rows([place, geo[2:3] - 1.0 - place], 8)

    over_tiles(s_dev, rim, score)
    place, left = geo_ref[0:1, :], geo_ref[1:2, :]
    scores = probs_ref[...]
    before, after = over_segment(scores, place, left, jnp.maximum)
    expo = jnp.exp(scores - jnp.maximum(before, after))
    before, after = over_segment(expo, place, left, jnp.add)
    probs_ref[...] = jnp.where(left >= 0.0, expo / (before + (after - expo)), 0.0)
    att_acc[...] = jnp.zeros_like(att_acc)

    def attend(base):
        at = pl.ds(base, LANES)
        probs_b = probs_ref[:, at].astype(BF16).astype(F32)[:heads]
        both = split2(head_rows(probs_b, dim) * kv_ref[own:, at].astype(F32))
        first = pl.multiple_of(window(bounds, blocks, base) * LANES, LANES)
        att_acc[:, pl.ds(first, 2 * LANES)] += dot(
            both, byte_major(row_ref, first, 2 * LANES, base, LANES)
        )

    over_tiles(s_dev, rim, attend)
    att_ref[...] = (att_acc[:own, :] + att_acc[own:, :]).astype(BF16)
    for copy in send_copies(att_ref, att_hbm, att_sems) + [kv_copy, pooled_copy]:
        copy.wait()


def hbm():
    return pl.BlockSpec(memory_space=pl.ANY)


def forward(member, offset, lengths, x, rim, w_key, w_value, w_query, groups):
    s_dev, width = x.shape
    patches = lengths.shape[1]
    own = width // groups
    total = s_dev + rim.shape[0]
    col = pl.BlockSpec((width, own), lambda i, member, offset: (0, member[0]))
    shape = jax.ShapeDtypeStruct
    small = [
        shape((own, patches), BF16), shape((8, total), F32), shape((8, total), F32), shape((16, patches), I32),
    ]
    return pl.pallas_call(
        forward_kernel,
        grid_spec=pltpu.PrefetchScalarGridSpec(
            num_scalar_prefetch=2,
            grid=(1,),
            in_specs=[whole(lengths.shape), hbm(), whole(rim.shape), col, col, col],
            out_specs=[hbm()] * 3 + [whole(s.shape) for s in small] + [smem()],
            scratch_shapes=[
                pltpu.VMEM((s_dev, width), BF16),
                pltpu.VMEM((2 * own, total), BF16),
                pltpu.VMEM((patches, width), BF16),
                pltpu.VMEM((own, patches), BF16),
                pltpu.VMEM((width, 2 * own), BF16),
                pltpu.VMEM((own, width), BF16),
                pltpu.VMEM((patches, width), F32),
                pltpu.VMEM((own + 16, patches), BF16),
                pltpu.VMEM((patches, LANES), I32),
                pltpu.VMEM((patches, LANES), I32),
                pltpu.VMEM((patches, LANES), F32),
                pltpu.VMEM((2 * own, patches), F32),
                pltpu.SemaphoreType.DMA((8,)),
                pltpu.SemaphoreType.DMA((2,)),
                pltpu.SemaphoreType.DMA((groups,)),
            ],
        ),
        out_shape=[shape((2 * own, total), BF16), shape((patches, width), BF16), shape((groups, own, patches), BF16)]
        + small + [shape((8,), I32)],
        compiler_params=params(),
        cost_estimate=cost(8 << 30, 12 << 20),
        name="forward",
    )(member, offset, lengths, x, rim, w_key, w_value, w_query)


def backward_kernel(
    bounds, x_hbm, kv_hbm, pooled_hbm, rim_ref, got_ref, query_ref, probs_ref, geo_ref, row_ref,
    grad_ref, factor_hbm,
    x_ref, kv_ref, pooled_ref, factor_ref, start_ref, end_ref, d_kv, lhs, d_probs, d_scores, dq_acc, acc,
    x_sems, in_sems, factor_sems,
):
    rim = rim_ref.shape[0]
    s_dev = x_hbm.shape[0]
    own, patches = query_ref.shape
    blocks = patches // LANES
    dim = 64
    heads = own // dim
    sources = got_ref.shape[0]
    kv_copy = pltpu.make_async_copy(kv_hbm, kv_ref, in_sems.at[0])
    kv_copy.start()
    chunks = x_sems.shape[0]
    chunk = s_dev // chunks
    loads = []
    for i in range(chunks):
        at = slice(i * chunk, (i + 1) * chunk)
        loads.append(pltpu.make_async_copy(x_hbm.at[at, :], x_ref.at[at, :], x_sems.at[i]))
        loads[-1].start()
    pooled_copy = pltpu.make_async_copy(pooled_hbm, pooled_ref, in_sems.at[1])
    pooled_copy.start()

    columns_of(row_ref, start_ref, end_ref)
    summed = jnp.zeros((own, patches), F32)
    for source in range(sources):
        summed = summed + from_i16(got_ref[source, :own, :]) * unit(got_ref[source, own:, :])[0:1]
    lhs[:own, :] = summed.astype(BF16)
    lhs[own:, :] = query_ref[...]
    factor_ref[:own, :] = summed.astype(BF16)
    kv_copy.wait()

    def first_pass(base):
        first = pl.multiple_of(window(bounds, blocks, base) * LANES, LANES)
        exp = dot(
            lhs[:, pl.ds(first, 2 * LANES)],
            patch_major(start_ref, end_ref, first, 2 * LANES, base, LANES),
        )
        d_out = exp[:own]
        at = pl.ds(base, LANES)
        product = d_out * kv_ref[own:, at].astype(F32)
        rows = [jnp.sum(product[h * dim:(h + 1) * dim], axis=0, keepdims=True) for h in range(heads)]
        d_probs[:, at] = padded_rows(rows, 8)
        probs_b = probs_ref[:, at].astype(BF16).astype(F32)[:heads]
        d_kv[own:, at] = (head_rows(probs_b, dim) * d_out).astype(BF16)
        d_kv[:own, at] = exp[own:].astype(BF16)

    over_tiles(s_dev, rim, first_pass)
    place, left = geo_ref[0:1, :], geo_ref[1:2, :]
    probs = probs_ref[...]
    weighted = probs * d_probs[...]
    before, after = over_segment(weighted, place, left, jnp.add)
    inner = before + (after - weighted)
    slope = jnp.where(left >= 0.0, probs * (d_probs[...] - inner) * (dim ** -0.5), 0.0)
    d_scores[...] = slope.astype(BF16).astype(F32)
    dq_acc[...] = jnp.zeros_like(dq_acc)

    def second_pass(base):
        at = pl.ds(base, LANES)
        wide = head_rows(d_scores[:, at][:heads], dim)
        d_kv[:own, at] = (wide * d_kv[:own, at].astype(F32)).astype(BF16)
        both = split2(wide * kv_ref[:own, at].astype(F32))
        first = pl.multiple_of(window(bounds, blocks, base) * LANES, LANES)
        dq_acc[:, pl.ds(first, 2 * LANES)] += dot(
            both, byte_major(row_ref, first, 2 * LANES, base, LANES)
        )

    over_tiles(s_dev, rim, second_pass)
    factor_ref[own:2 * own, :] = (dq_acc[:own, :] + dq_acc[own:, :]).astype(BF16)
    probs_b = probs.astype(BF16).astype(F32)
    rows = padded_rows(
        [d_scores[h:h + 1, :] for h in range(heads)] + [probs_b[h:h + 1, :] for h in range(heads)], 8
    )
    groups = [rows[:, at:at + patches] for at in range(0, s_dev, patches)]
    last = jnp.concatenate([rows[:, s_dev:], jnp.zeros((8, patches - rim), F32)], axis=1)
    spare = factor_ref.shape[0] - 2 * own - 8 * (len(groups) + 1)
    stack = groups + [last] + ([jnp.zeros((spare, patches), F32)] if spare else [])
    factor_ref[2 * own:, :] = jnp.concatenate(stack, axis=0).astype(BF16)
    sends = send_copies(factor_ref, factor_hbm, factor_sems)

    acc[...] = dot(d_kv[:, s_dev:], rim_ref[...])
    for i in range(chunks):
        loads[i].wait()
    acc[...] += dot(d_kv[:, :s_dev], x_ref[...])
    pooled_copy.wait()
    grad_q = dot(factor_ref[own:2 * own, :], pooled_ref[...])
    powers = []
    parts = grad_ref.shape[0]
    for k, grad in enumerate((grad_q, acc[:own, :], acc[own:, :])):
        codes, power = coded(grad.T)
        powers.append(power)
        rows = codes.shape[0] // parts
        spread = codes.reshape(rows // 8, parts, 8, own)
        for part in range(parts):
            grad_ref[part, k * rows:(k + 1) * rows, :] = to_i16(spread[:, part].reshape(rows, own))
    tail = to_i16(padded_rows(powers, 16))
    for part in range(parts):
        grad_ref[part, 3 * rows:, :] = tail
    for copy in sends:
        copy.wait()


def backward(bounds, x, kv, pooled, rim, got, query, probs, geo, row, parts):
    s_dev, width = x.shape
    own, patches = query.shape
    groups = got.shape[0]
    total = kv.shape[1]
    extra = -(-8 * (s_dev // patches + 1) // 16) * 16
    rows = width // parts
    vmem = pl.BlockSpec(memory_space=pltpu.VMEM)
    return pl.pallas_call(
        backward_kernel,
        in_specs=[smem()] + [hbm()] * 3 + [vmem] * 6,
        out_specs=[vmem, hbm()],
        out_shape=[
            jax.ShapeDtypeStruct((parts, 3 * rows + 16, own), I16),
            jax.ShapeDtypeStruct((groups, 2 * own + extra, patches), BF16),
        ],
        scratch_shapes=[
            pltpu.VMEM((s_dev, width), BF16),
            pltpu.VMEM((2 * own, total), BF16),
            pltpu.VMEM((patches, width), BF16),
            pltpu.VMEM((2 * own + extra, patches), BF16),
            pltpu.VMEM((patches, LANES), I32),
            pltpu.VMEM((patches, LANES), I32),
            pltpu.VMEM((2 * own, total), BF16),
            pltpu.VMEM((2 * own, patches), BF16),
            pltpu.VMEM((8, total), F32),
            pltpu.VMEM((8, total), F32),
            pltpu.VMEM((2 * own, patches), F32),
            pltpu.VMEM((2 * own, width), F32),
            pltpu.SemaphoreType.DMA((4,)),
            pltpu.SemaphoreType.DMA((2,)),
            pltpu.SemaphoreType.DMA((groups,)),
        ],
        compiler_params=params(),
        cost_estimate=cost(6 << 30, 16 << 20),
        name="backward",
    )(bounds, x, kv, pooled, rim, got, query, probs, geo, row)


def queries_kernel(pooled_ref, wq_ref, out_ref):
    out_ref[...] = dot(pooled_ref[...], wq_ref[...]).T.astype(BF16)


def queries(pooled, w_query):
    patches, width = pooled.shape
    return pl.pallas_call(
        queries_kernel,
        in_specs=[pl.BlockSpec(memory_space=pltpu.VMEM)] * 2,
        out_specs=pl.BlockSpec(memory_space=pltpu.VMEM),
        out_shape=jax.ShapeDtypeStruct((width, patches), BF16),
        compiler_params=params(),
        cost_estimate=cost(1 << 30, 4 << 20),
        name="queries",
    )(pooled, w_query)


def out_grad_kernel(member, att_ref, cot_ref, owner_ref, out_ref, rows_ref):
    groups, own, patches = att_ref.shape
    att = att_ref[...].reshape(groups * own, patches)
    codes, power = coded(dot(att, cot_ref[...]))
    parts = out_ref.shape[0]
    rows = codes.shape[0] // parts
    slabs = codes.shape[1] // LANES
    tail = to_i16(padded_rows([power[:, at * LANES:(at + 1) * LANES] for at in range(slabs)], 16))
    for part in range(parts):
        for at in range(slabs):
            block = codes[part * rows:(part + 1) * rows, at * LANES:(at + 1) * LANES]
            out_ref[part, at * rows:(at + 1) * rows, :] = to_i16(block)
        out_ref[part, slabs * rows:, :] = tail
    count = rows_ref.shape[0]
    order = jnp.broadcast_to(owner_ref[...], (8, patches))
    order = pltpu.roll(order, lax.rem(patches - member[0] * count, patches), 1)[0:1, :LANES]
    pick = jnp.where(lax.broadcasted_iota(I32, (patches, LANES), 0) == order, 1.0, 0.0).astype(BF16)
    rows_ref[...] = dot(att, pick).T[:count].astype(BF16)


def out_grad(member, att, cot, owner, parts):
    groups, own, patches = att.shape
    width, cols = groups * own, cot.shape[1]
    rows = cols // LANES * (width // parts) + 16
    count = patches // groups
    return pl.pallas_call(
        out_grad_kernel,
        in_specs=[smem()] + [pl.BlockSpec(memory_space=pltpu.VMEM)] * 3,
        out_specs=[pl.BlockSpec(memory_space=pltpu.VMEM)] * 2,
        out_shape=[
            jax.ShapeDtypeStruct((parts, rows, LANES), I16),
            jax.ShapeDtypeStruct((count, width), BF16),
        ],
        compiler_params=params(),
        cost_estimate=cost(2 * width * cols * patches, 4 << 20),
        name="out_grad",
    )(member, att, cot, owner)


def out_sum_kernel(got_ref, out_ref):
    sources, rows, lanes = got_ref.shape
    slabs = out_ref.shape[1] // lanes
    count = out_ref.shape[0]
    for at in range(slabs):
        total = jnp.zeros((count, lanes), F32)
        for source in range(sources):
            scale = unit(got_ref[source, slabs * count:, :])[at:at + 1]
            total = total + from_i16(got_ref[source, at * count:(at + 1) * count, :]) * scale
        out_ref[:, at * lanes:(at + 1) * lanes] = total.astype(BF16)


def out_sum(got, cols):
    slabs = cols // LANES
    count = (got.shape[1] - 16) // slabs
    return pl.pallas_call(
        out_sum_kernel,
        in_specs=[pl.BlockSpec(memory_space=pltpu.VMEM)],
        out_specs=pl.BlockSpec(memory_space=pltpu.VMEM),
        out_shape=jax.ShapeDtypeStruct((count, cols), BF16),
        compiler_params=params(),
        cost_estimate=cost(1 << 20, 2 << 20),
        name="out_sum",
    )(got)


def qkv_sum_kernel(got_ref, out_ref):
    sources, rows, lanes = got_ref.shape
    groups = out_ref.shape[0]
    count = (rows - 16) // 3
    totals = []
    for k in range(3):
        total = jnp.zeros((count, lanes), F32)
        for source in range(sources):
            scale = unit(got_ref[source, 3 * count:, :])[k:k + 1]
            total = total + from_i16(got_ref[source, k * count:(k + 1) * count, :]) * scale
        totals.append(total)
    spare = jnp.zeros((8, lanes), F32)
    for group in range(groups):
        rows = [total[group * 8:(group + 1) * 8] for total in totals] + [spare]
        out_ref[group] = jnp.concatenate(rows, axis=0).astype(BF16)


def qkv_sum(got, groups):
    return pl.pallas_call(
        qkv_sum_kernel,
        in_specs=[pl.BlockSpec(memory_space=pltpu.VMEM)],
        out_specs=pl.BlockSpec(memory_space=pltpu.VMEM),
        out_shape=jax.ShapeDtypeStruct((groups, 32, LANES), BF16),
        compiler_params=params(),
        cost_estimate=cost(1 << 20, 2 << 20),
        name="qkv_sum",
    )(got)


def bytes_kernel(
    member, bounds, factor_ref, query_ref, wk_own, wv_own, wq_own, row_ref,
    out_ref, head_ref, tail_ref,
    lhs, shares, d_kv, w_own, start_ref, end_ref,
):
    groups, rows, patches = factor_ref.shape
    own, width = wq_own.shape
    dim = 64
    heads = own // dim
    blocks = patches // LANES
    total = shares.shape[2]
    s_dev = out_ref.shape[0]
    rim = total - s_dev
    columns_of(row_ref, start_ref, end_ref)
    lhs[:width, :] = query_ref[...]
    lhs[width:2 * width, :] = factor_ref[:, :own, :].reshape(width, patches)
    d_query = factor_ref[:, own:2 * own, :].reshape(width, patches)
    length = (row_ref[8:9, :] - row_ref[0:1, :]).astype(F32)
    lhs[2 * width:, :] = split2(dot(wq_own[...], d_query) * (1.0 / length))
    w_own[:, :width] = wk_own[...]
    w_own[:, width:] = wv_own[...]
    for group in range(groups):
        table = factor_ref[group, 2 * own:, :].astype(F32)
        for at in range(s_dev // patches):
            shares[group, :, at * patches:(at + 1) * patches] = table[8 * at:8 * at + 8]
        at = s_dev // patches
        shares[group, :, s_dev:] = table[8 * at:8 * at + 8, :rim]

    def tile_grad(base, span, first, count, slot):
        inside = patch_major(start_ref, end_ref, first, count, base, span)
        at = pl.ds(base, span)
        patch = pl.ds(first, count)
        for group in range(groups):
            share = shares[group, :, at]
            for kind in range(2):
                top = kind * width + group * own
                wide = dot(lhs[top:top + own, patch], inside)
                part = head_rows(share[kind * heads:(kind + 1) * heads], dim)
                d_kv[slot, top:top + own, :span] = (part * wide).astype(BF16)
        grad = dot(w_own[...], d_kv[slot, :, :span])
        pool = dot(lhs[2 * width:, patch], inside)
        return (grad + (pool[:own] + pool[own:])).T

    def tiles(span, first_of, count):
        def go(i, carry):
            for slot in range(2):
                base = pl.multiple_of((2 * i + slot) * span, span)
                out_ref[pl.ds(base, span), :] = tile_grad(base, span, first_of(base), count, slot).astype(BF16)
            return carry

        lax.fori_loop(0, s_dev // (2 * span), go, 0)

    def first_of(base):
        return pl.multiple_of(window(bounds, blocks, base) * LANES, LANES)

    @pl.when(bounds[blocks + 1] > 0)
    def _():
        tiles(LANES, first_of, 2 * LANES)

    @pl.when(bounds[blocks + 1] == 0)
    def _():
        tiles(TILE, first_of, 2 * LANES)

    head_ref[...] = tile_grad(0, LANES, 0, 2 * LANES, 0)[:16]
    tail_ref[...] = tile_grad(s_dev, rim, patches - 2 * LANES, 2 * LANES, 1)[:16]


def byte_grads(member, bounds, factors, query, w_query, w_key, w_value, row, s_dev):
    groups, rows, patches = factors.shape
    width = w_query.shape[0]
    own = width // groups
    rim = LANES
    mine = pl.BlockSpec((own, width), lambda i, member, bounds: (member[0], 0))
    return pl.pallas_call(
        bytes_kernel,
        grid_spec=pltpu.PrefetchScalarGridSpec(
            num_scalar_prefetch=2,
            grid=(1,),
            in_specs=[whole(factors.shape), whole(query.shape), mine, mine, mine, whole(row.shape)],
            out_specs=[whole((s_dev, own)), whole((16, own)), whole((16, own))],
            scratch_shapes=[
                pltpu.VMEM((2 * width + 2 * own, patches), BF16),
                pltpu.VMEM((groups, 8, s_dev + rim), F32),
                pltpu.VMEM((2, 2 * width, TILE), BF16),
                pltpu.VMEM((own, 2 * width), BF16),
                pltpu.VMEM((patches, LANES), I32),
                pltpu.VMEM((patches, LANES), I32),
            ],
        ),
        out_shape=[
            jax.ShapeDtypeStruct((s_dev, own), BF16),
            jax.ShapeDtypeStruct((16, own), F32),
            jax.ShapeDtypeStruct((16, own), F32),
        ],
        compiler_params=params(),
        cost_estimate=cost(8 << 30, 8 << 20),
        name="byte_grads",
    )(member, bounds, factors, query, w_key, w_value, w_query, row)


def shifted(value, axis, steps):
    count = lax.axis_size(axis)
    first, last = (max(0, -steps), min(count, count - steps))
    return lax.ppermute(value, axis, [(source, source + steps) for source in range(first, last)])


def swap(value, axis):
    return lax.all_to_all(value, axis, split_axis=0, concat_axis=0, tiled=True)


def collect(value, axis):
    count = lax.axis_size(axis)
    return swap(jnp.broadcast_to(value[None], (count,) + value.shape), axis)


def local(byte_states, patch_len, shard_offset, owner, cotangent, w_query, w_key, w_value, w_out):
    s_dev, width = byte_states.shape
    groups = lax.axis_size("patch")
    parts = lax.axis_size("seq")
    member = lax.axis_index("patch").astype(I32).reshape(1)
    following = shifted(byte_states[:MAXP], "seq", -1)
    rim = jnp.pad(following, ((0, LANES - MAXP), (0, 0)))

    coded_att, rim = lax.optimization_barrier((att_grad(w_out, cotangent, groups), rim))
    got_att = swap(coded_att, "patch")
    kv, pooled, att, query, probs, geo, row, bounds = forward(
        member, shard_offset, patch_len, byte_states, rim, w_key, w_value, w_query, groups
    )
    all_att = swap(att, "patch")
    grads, factor = backward(bounds, byte_states, kv, pooled, rim, got_att, query, probs, geo, row, parts)
    got_qkv = swap(grads, "seq")
    factors = swap(factor, "patch")
    all_att, _ = lax.optimization_barrier((all_att, grads))
    coded_out, patch_rows = out_grad(member, all_att, cotangent, owner, parts)
    got_out = swap(coded_out, "seq")
    all_query = queries(pooled, w_query)
    own_qkv = swap(qkv_sum(got_qkv, groups), "patch")
    all_out = collect(out_sum(got_out, cotangent.shape[1]), "seq")
    all_qkv = collect(own_qkv, "seq")
    d_bytes, head, tail = byte_grads(
        member, bounds, factors, all_query, w_query, w_key, w_value, row, s_dev
    )
    first = (head + shifted(tail, "seq", 1)).astype(BF16)
    d_bytes = lax.dynamic_update_slice(d_bytes, first, (0, 0))
    d_wout = all_out.reshape(width, -1).astype(F32)
    all_qkv = all_qkv[:, :, :24].reshape(parts, groups, 3, 8, -1)
    d_qkv = all_qkv.transpose(2, 0, 3, 1, 4).reshape(3, width // groups, width).astype(F32)
    return (d_bytes, d_qkv, d_wout, patch_rows)


def solution(mesh):
    return jax.shard_map(
        local,
        mesh=mesh,
        in_specs=(
            P("seq", None), P("seq", None), P("seq"), P("seq", None), P("seq", "patch"),
            P(), P(), P(), P(None, "patch"),
        ),
        out_specs=(P("seq", "patch"), P(None, "patch", None), P(None, "patch"), P(("seq", "patch"), None)),
        check_vma=False,
    )
```

```python
import jax
import jax.numpy as jnp
from jax import lax
from jax.experimental import pallas as pl
from jax.experimental.pallas import tpu as pltpu
from jax.sharding import PartitionSpec as P

HEADS = 16
MAXP = 16
LANES = 128
TILE = 256
UNROLL = 4
F32, BF16, I16, I32 = jnp.float32, jnp.bfloat16, jnp.int16, jnp.int32
NT = (((1,), (1,)), ((), ()))
VMEM_BYTES = 56 * 1024 * 1024


def params():
    return pltpu.CompilerParams(vmem_limit_bytes=VMEM_BYTES)


def cost(flops, moved):
    return pl.CostEstimate(flops=flops, bytes_accessed=moved, transcendentals=0)


def whole(shape):
    return pl.BlockSpec(shape, lambda *_: (0,) * len(shape))


def smem():
    return pl.BlockSpec(memory_space=pltpu.SMEM)


def dot(a, b):
    return jnp.dot(a, b, preferred_element_type=F32)


def dot_nt(a, b):
    return lax.dot_general(a, b, NT, preferred_element_type=F32)


def coded(value):
    peak = jnp.max(jnp.abs(value), axis=0, keepdims=True)
    power = jnp.ceil(jnp.log2(jnp.maximum(peak, 1e-30)))
    return jnp.round(value * (32767.0 * jnp.exp2(-power))), power


def to_i16(value):
    return value.astype(I32).astype(I16)


def from_i16(value):
    return value.astype(I32).astype(F32)


def unit(power):
    return jnp.exp2(from_i16(power)) * (1.0 / 32767.0)


def padded_rows(row_list, count):
    width = row_list[0].shape[1]
    at = lax.broadcasted_iota(I32, (count, width), 0)
    out = jnp.zeros((count, width), F32)
    for i, row in enumerate(row_list):
        out = jnp.where(at == i, jnp.broadcast_to(row, (count, width)), out)
    return out


def window(bounds, blocks, base):
    block = jnp.int32(0)
    for at in range(1, blocks - 1):
        block = block + (bounds[at] <= base).astype(I32)
    return block


def patch_major(start_ref, end_ref, first, count, base, width):
    rows = pl.ds(pl.multiple_of(first, LANES), count)
    start, end = start_ref[rows, :], end_ref[rows, :]
    parts = []
    for at in range(0, width, LANES):
        byte = base + at + lax.broadcasted_iota(I32, (count, LANES), 1)
        parts.append(jnp.where((byte >= start) & (byte < end), 1.0, 0.0).astype(BF16))
    return parts[0] if len(parts) == 1 else jnp.concatenate(parts, axis=1)


def byte_major(row_ref, first, count, base, width):
    lanes = pl.ds(pl.multiple_of(first, LANES), count)
    byte = base + lax.broadcasted_iota(I32, (width, count), 0)
    inside = (byte >= row_ref[0:1, lanes]) & (byte < row_ref[8:9, lanes])
    return jnp.where(inside, 1.0, 0.0).astype(BF16)


def over_tiles(bounds, blocks, s_dev, rim, body):
    def loop(width, unroll):
        def go(i, carry):
            for at in range(unroll):
                body(pl.multiple_of((i * unroll + at) * width, width), width)
            return carry

        lax.fori_loop(0, s_dev // (unroll * width), go, 0)

    @pl.when(bounds[blocks + 1] == 0)
    def _():
        loop(TILE, UNROLL)

    @pl.when(bounds[blocks + 1] > 0)
    def _():
        loop(LANES, 1)

    body(s_dev, rim)


def fill_rim(rim_ref, rim_rows):
    rim_rows[...] = jnp.zeros_like(rim_rows)
    rim_rows[:rim_ref.shape[0], :] = rim_ref[...]


def columns_of(row_ref, start_ref, end_ref):
    patches = row_ref.shape[1]
    start_ref[...] = jnp.broadcast_to(row_ref[0:1, :], (LANES, patches)).T
    end_ref[...] = jnp.broadcast_to(row_ref[8:9, :], (LANES, patches)).T


def send_copies(source, target, sems):
    copies = [pltpu.make_async_copy(source, target.at[i], sems.at[i]) for i in range(target.shape[0])]
    for copy in copies:
        copy.start()
    return copies


def over_segment(value, place, left, op):
    size = value.shape[1]
    before, after = value, value
    for step in (1, 2, 4, 8):
        before = jnp.where(place >= step, op(before, pltpu.roll(before, step, 1)), before)
        after = jnp.where(left >= step, op(after, pltpu.roll(after, size - step, 1)), after)
    return before, after


def head_rows(rows, dim):
    count, width = rows.shape
    return jnp.concatenate(
        [jnp.broadcast_to(rows[i:i + 1], (dim, width)) for i in range(count)], axis=0
    )


def split2(value):
    high = value.astype(BF16)
    return jnp.concatenate([high, (value - high.astype(F32)).astype(BF16)], axis=0)


def att_grad_kernel(w_ref, cot_ref, out_ref, cot_t):
    groups = out_ref.shape[0]
    own = w_ref.shape[0] // groups
    cot_t[...] = cot_ref[...].astype(F32).T.astype(BF16)
    for group in range(groups):
        codes, power = coded(dot(w_ref[group * own:(group + 1) * own, :], cot_t[...]))
        out_ref[group, :own, :] = to_i16(codes)
        out_ref[group, own:, :] = to_i16(jnp.broadcast_to(power, (16, power.shape[1])))


def att_grad(w_out, cot, groups):
    width, cols = w_out.shape
    rows = cot.shape[0]
    own = width // groups
    return pl.pallas_call(
        att_grad_kernel,
        in_specs=[pl.BlockSpec(memory_space=pltpu.VMEM)] * 2,
        out_specs=pl.BlockSpec(memory_space=pltpu.VMEM),
        out_shape=jax.ShapeDtypeStruct((groups, own + 16, rows), I16),
        scratch_shapes=[pltpu.VMEM((cols, rows), BF16)],
        compiler_params=params(),
        cost_estimate=cost(2 * width * cols * rows, 4 << 20),
        name="att_grad",
    )(w_out, cot)


def forward_kernel(
    member, offset, len_ref, x_hbm, rim_ref, wk_ref, wv_ref, wq_ref,
    kv_hbm, pooled_hbm, att_hbm, query_ref, probs_ref, geo_ref, row_ref, bounds,
    rim_rows, x_ref, kv_ref, pooled_ref, att_ref, w_kv, wq_t, acc, lhs, start_ref, end_ref, inv_col, att_acc,
    x_sems, out_sems, att_sems,
):
    rim = rim_rows.shape[0]
    patches = len_ref.shape[1]
    blocks = patches // LANES
    own = wk_ref.shape[1]
    dim = 64
    heads = own // dim
    s_dev = x_hbm.shape[0]
    chunks = x_sems.shape[0]
    chunk = s_dev // chunks
    loads = []
    for i in range(chunks):
        at = slice(i * chunk, (i + 1) * chunk)
        loads.append(pltpu.make_async_copy(x_hbm.at[at, :], x_ref.at[at, :], x_sems.at[i]))
        loads[-1].start()

    length = len_ref[...].astype(F32)
    before = lax.broadcasted_iota(I32, (patches, patches), 0)
    after = lax.broadcasted_iota(I32, (patches, patches), 1)
    off = offset[0].astype(F32)
    eight = jnp.broadcast_to(length, (8, patches))
    upper = jnp.where(before < after, 1.0, 0.0).astype(BF16)
    start_row = (dot(eight.astype(BF16), upper) + off).astype(I32)
    row_ref[:8, :] = start_row
    row_ref[8:, :] = start_row + eight.astype(I32)
    columns_of(row_ref, start_ref, end_ref)
    inv_col[...] = 1.0 / jnp.broadcast_to(length, (LANES, patches)).T
    at = lax.broadcasted_iota(I32, (16, patches), 0)
    both = jnp.concatenate([start_row, start_row], axis=0)
    geo = jnp.where(at == 0, both >> 6, jnp.where(at == 1, both & 63, 0)).astype(F32)
    geo = jnp.where(at == 2, jnp.broadcast_to(length, (16, patches)), geo)
    lhs[own:own + 16, :] = geo.astype(BF16)
    lane = lax.broadcasted_iota(I32, (1, patches), 1)
    for block in range(blocks + 1):
        total = jnp.sum(jnp.where(lane < block * LANES, length, 0.0))
        bounds[block] = (total + off).astype(I32)

    def crowded(i, found):
        base = i * TILE
        third = window(bounds, blocks, base) + 2
        return found | ((third < blocks) & (bounds[third] < base + TILE)).astype(I32)

    bounds[blocks + 1] = lax.fori_loop(0, s_dev // TILE, crowded, jnp.int32(0))
    w_kv[:, :own] = wk_ref[...]
    w_kv[:, own:] = wv_ref[...]
    wq_t[...] = wq_ref[...].astype(F32).T.astype(BF16)
    acc[...] = jnp.zeros_like(acc)

    def project(rows, base, width):
        kv_ref[:, pl.ds(base, width)] = dot(rows, w_kv[...]).T.astype(BF16)
        first = pl.multiple_of(window(bounds, blocks, base) * LANES, LANES)
        at = pl.ds(first, 2 * LANES)
        acc[at, :] += dot(patch_major(start_ref, end_ref, first, 2 * LANES, base, width), rows)

    for i in range(chunks):
        loads[i].wait()
        for at in range(i * chunk, (i + 1) * chunk, TILE):
            project(x_ref[at:at + TILE, :], at, TILE)
    fill_rim(rim_ref, rim_rows)
    project(rim_rows[...], s_dev, rim)

    @pl.when(bounds[blocks + 1] > 0)
    def _():
        def rest(i, carry):
            base = pl.multiple_of(i * TILE, TILE)
            third = window(bounds, blocks, base) + 2

            @pl.when((third < blocks) & (bounds[third] < base + TILE))
            def _():
                first = pl.multiple_of(third * LANES, LANES)
                acc[pl.ds(first, LANES), :] += dot(
                    patch_major(start_ref, end_ref, first, LANES, base, TILE), x_ref[pl.ds(base, TILE), :]
                )

            return carry

        lax.fori_loop(0, s_dev // TILE, rest, 0)

    kv_copy = pltpu.make_async_copy(kv_ref, kv_hbm, out_sems.at[0])
    kv_copy.start()
    pooled = (acc[...] * inv_col[:, :1]).astype(BF16)
    pooled_ref[...] = pooled
    pooled_copy = pltpu.make_async_copy(pooled_ref, pooled_hbm, out_sems.at[1])
    pooled_copy.start()
    query = dot_nt(wq_t[...], pooled).astype(BF16)
    lhs[:own, :] = query
    query_ref[...] = query

    def score(base, width):
        first = pl.multiple_of(window(bounds, blocks, base) * LANES, LANES)
        exp = dot(
            lhs[:, pl.ds(first, 2 * LANES)],
            patch_major(start_ref, end_ref, first, 2 * LANES, base, width),
        )
        at = pl.ds(base, width)
        product = exp[:own] * kv_ref[:own, at].astype(F32)
        rows = [jnp.sum(product[h * dim:(h + 1) * dim], axis=0, keepdims=True) for h in range(heads)]
        probs_ref[:, at] = padded_rows(rows, 8) * (dim ** -0.5)
        geo = exp[own:own + 8]
        byte = (base + lax.broadcasted_iota(I32, (1, width), 1)).astype(F32)
        place = byte - (64.0 * geo[0:1] + geo[1:2])
        geo_ref[:, at] = padded_rows([place, geo[2:3] - 1.0 - place], 8)

    over_tiles(bounds, blocks, s_dev, rim, score)
    place, left = geo_ref[0:1, :], geo_ref[1:2, :]
    scores = probs_ref[...]
    before, after = over_segment(scores, place, left, jnp.maximum)
    expo = jnp.exp(scores - jnp.maximum(before, after))
    before, after = over_segment(expo, place, left, jnp.add)
    probs_ref[...] = jnp.where(left >= 0.0, expo / (before + (after - expo)), 0.0)
    att_acc[...] = jnp.zeros_like(att_acc)

    def attend(base, width):
        at = pl.ds(base, width)
        probs_b = probs_ref[:, at].astype(BF16).astype(F32)[:heads]
        both = split2(head_rows(probs_b, dim) * kv_ref[own:, at].astype(F32))
        first = pl.multiple_of(window(bounds, blocks, base) * LANES, LANES)
        att_acc[:, pl.ds(first, 2 * LANES)] += dot(
            both, byte_major(row_ref, first, 2 * LANES, base, width)
        )

    over_tiles(bounds, blocks, s_dev, rim, attend)
    att_ref[...] = (att_acc[:own, :] + att_acc[own:, :]).astype(BF16)
    for copy in send_copies(att_ref, att_hbm, att_sems) + [kv_copy, pooled_copy]:
        copy.wait()


def hbm():
    return pl.BlockSpec(memory_space=pl.ANY)


def forward(member, offset, lengths, x, rim, w_key, w_value, w_query, groups):
    s_dev, width = x.shape
    patches = lengths.shape[1]
    own = width // groups
    total = s_dev + LANES
    col = pl.BlockSpec((width, own), lambda i, member, offset: (0, member[0]))
    shape = jax.ShapeDtypeStruct
    small = [
        shape((own, patches), BF16), shape((8, total), F32), shape((8, total), F32), shape((16, patches), I32),
    ]
    return pl.pallas_call(
        forward_kernel,
        grid_spec=pltpu.PrefetchScalarGridSpec(
            num_scalar_prefetch=2,
            grid=(1,),
            in_specs=[whole(lengths.shape), hbm(), whole(rim.shape), col, col, col],
            out_specs=[hbm()] * 3 + [whole(s.shape) for s in small] + [smem()],
            scratch_shapes=[
                pltpu.VMEM((LANES, width), BF16),
                pltpu.VMEM((s_dev, width), BF16),
                pltpu.VMEM((2 * own, total), BF16),
                pltpu.VMEM((patches, width), BF16),
                pltpu.VMEM((own, patches), BF16),
                pltpu.VMEM((width, 2 * own), BF16),
                pltpu.VMEM((own, width), BF16),
                pltpu.VMEM((patches, width), F32),
                pltpu.VMEM((own + 16, patches), BF16),
                pltpu.VMEM((patches, LANES), I32),
                pltpu.VMEM((patches, LANES), I32),
                pltpu.VMEM((patches, LANES), F32),
                pltpu.VMEM((2 * own, patches), F32),
                pltpu.SemaphoreType.DMA((8,)),
                pltpu.SemaphoreType.DMA((2,)),
                pltpu.SemaphoreType.DMA((groups,)),
            ],
        ),
        out_shape=[shape((2 * own, total), BF16), shape((patches, width), BF16), shape((groups, own, patches), BF16)]
        + small + [shape((8,), I32)],
        compiler_params=params(),
        cost_estimate=cost(8 << 30, 12 << 20),
        name="forward",
    )(member, offset, lengths, x, rim, w_key, w_value, w_query)


def backward_kernel(
    bounds, x_hbm, kv_hbm, pooled_hbm, rim_ref, got_ref, query_ref, probs_ref, geo_ref, row_ref,
    grad_ref, factor_out,
    rim_rows, x_ref, kv_ref, pooled_ref, factor_ref, start_ref, end_ref, d_kv, lhs, d_probs, d_scores, dq_acc, acc,
    x_sems, in_sems,
):
    rim = rim_rows.shape[0]
    s_dev = x_hbm.shape[0]
    own, patches = query_ref.shape
    blocks = patches // LANES
    dim = 64
    heads = own // dim
    sources = got_ref.shape[0]
    kv_copy = pltpu.make_async_copy(kv_hbm, kv_ref, in_sems.at[0])
    kv_copy.start()
    chunks = x_sems.shape[0]
    chunk = s_dev // chunks
    loads = []
    for i in range(chunks):
        at = slice(i * chunk, (i + 1) * chunk)
        loads.append(pltpu.make_async_copy(x_hbm.at[at, :], x_ref.at[at, :], x_sems.at[i]))
        loads[-1].start()
    pooled_copy = pltpu.make_async_copy(pooled_hbm, pooled_ref, in_sems.at[1])
    pooled_copy.start()

    columns_of(row_ref, start_ref, end_ref)
    summed = jnp.zeros((own, patches), F32)
    for source in range(sources):
        summed = summed + from_i16(got_ref[source, :own, :]) * unit(got_ref[source, own:, :])[0:1]
    lhs[:own, :] = summed.astype(BF16)
    lhs[own:, :] = query_ref[...]
    factor_ref[:own, :] = summed.astype(BF16)
    kv_copy.wait()

    def first_pass(base, width):
        first = pl.multiple_of(window(bounds, blocks, base) * LANES, LANES)
        exp = dot(
            lhs[:, pl.ds(first, 2 * LANES)],
            patch_major(start_ref, end_ref, first, 2 * LANES, base, width),
        )
        d_out = exp[:own]
        at = pl.ds(base, width)
        product = d_out * kv_ref[own:, at].astype(F32)
        rows = [jnp.sum(product[h * dim:(h + 1) * dim], axis=0, keepdims=True) for h in range(heads)]
        d_probs[:, at] = padded_rows(rows, 8)
        probs_b = probs_ref[:, at].astype(BF16).astype(F32)[:heads]
        d_kv[own:, at] = (head_rows(probs_b, dim) * d_out).astype(BF16)
        d_kv[:own, at] = exp[own:].astype(BF16)

    over_tiles(bounds, blocks, s_dev, rim, first_pass)
    place, left = geo_ref[0:1, :], geo_ref[1:2, :]
    probs = probs_ref[...]
    weighted = probs * d_probs[...]
    before, after = over_segment(weighted, place, left, jnp.add)
    inner = before + (after - weighted)
    slope = jnp.where(left >= 0.0, probs * (d_probs[...] - inner) * (dim ** -0.5), 0.0)
    d_scores[...] = slope.astype(BF16).astype(F32)
    dq_acc[...] = jnp.zeros_like(dq_acc)

    def second_pass(base, width):
        at = pl.ds(base, width)
        wide = head_rows(d_scores[:, at][:heads], dim)
        d_kv[:own, at] = (wide * d_kv[:own, at].astype(F32)).astype(BF16)
        both = split2(wide * kv_ref[:own, at].astype(F32))
        first = pl.multiple_of(window(bounds, blocks, base) * LANES, LANES)
        dq_acc[:, pl.ds(first, 2 * LANES)] += dot(
            both, byte_major(row_ref, first, 2 * LANES, base, width)
        )

    over_tiles(bounds, blocks, s_dev, rim, second_pass)
    factor_ref[own:2 * own, :] = (dq_acc[:own, :] + dq_acc[own:, :]).astype(BF16)
    probs_b = probs.astype(BF16).astype(F32)
    rows = padded_rows(
        [d_scores[h:h + 1, :] for h in range(heads)] + [probs_b[h:h + 1, :] for h in range(heads)], 8
    )
    groups = [rows[:, at:at + patches] for at in range(0, s_dev, patches)]
    last = jnp.concatenate([rows[:, s_dev:], jnp.zeros((8, patches - rim), F32)], axis=1)
    spare = factor_ref.shape[0] - 2 * own - 8 * (len(groups) + 1)
    stack = groups + [last] + ([jnp.zeros((spare, patches), F32)] if spare else [])
    factor_ref[2 * own:, :] = jnp.concatenate(stack, axis=0).astype(BF16)
    factor_out[...] = factor_ref[...]

    fill_rim(rim_ref, rim_rows)
    acc[...] = dot(d_kv[:, s_dev:], rim_rows[...])
    for i in range(chunks):
        loads[i].wait()
    acc[...] += dot(d_kv[:, :s_dev], x_ref[...])
    pooled_copy.wait()
    grad_q = dot(factor_ref[own:2 * own, :], pooled_ref[...])
    powers = []
    parts = grad_ref.shape[0]
    for k, grad in enumerate((grad_q, acc[:own, :], acc[own:, :])):
        codes, power = coded(grad.T)
        powers.append(power)
        rows = codes.shape[0] // parts
        spread = codes.reshape(rows // 8, parts, 8, own)
        for part in range(parts):
            grad_ref[part, k * rows:(k + 1) * rows, :] = to_i16(spread[:, part].reshape(rows, own))
    tail = to_i16(padded_rows(powers, 16))
    for part in range(parts):
        grad_ref[part, 3 * rows:, :] = tail


def backward(bounds, x, kv, pooled, rim, got, query, probs, geo, row, parts):
    s_dev, width = x.shape
    own, patches = query.shape
    groups = got.shape[0]
    total = kv.shape[1]
    extra = -(-8 * (s_dev // patches + 1) // 16) * 16
    rows = width // parts
    vmem = pl.BlockSpec(memory_space=pltpu.VMEM)
    return pl.pallas_call(
        backward_kernel,
        in_specs=[smem()] + [hbm()] * 3 + [vmem] * 6,
        out_specs=[vmem, vmem],
        out_shape=[
            jax.ShapeDtypeStruct((parts, 3 * rows + 16, own), I16),
            jax.ShapeDtypeStruct((2 * own + extra, patches), BF16),
        ],
        scratch_shapes=[
            pltpu.VMEM((LANES, width), BF16),
            pltpu.VMEM((s_dev, width), BF16),
            pltpu.VMEM((2 * own, total), BF16),
            pltpu.VMEM((patches, width), BF16),
            pltpu.VMEM((2 * own + extra, patches), BF16),
            pltpu.VMEM((patches, LANES), I32),
            pltpu.VMEM((patches, LANES), I32),
            pltpu.VMEM((2 * own, total), BF16),
            pltpu.VMEM((2 * own, patches), BF16),
            pltpu.VMEM((8, total), F32),
            pltpu.VMEM((8, total), F32),
            pltpu.VMEM((2 * own, patches), F32),
            pltpu.VMEM((2 * own, width), F32),
            pltpu.SemaphoreType.DMA((4,)),
            pltpu.SemaphoreType.DMA((2,)),
        ],
        compiler_params=params(),
        cost_estimate=cost(6 << 30, 16 << 20),
        name="backward",
    )(bounds, x, kv, pooled, rim, got, query, probs, geo, row)


def queries_kernel(pooled_ref, wq_ref, out_ref):
    out_ref[...] = dot(pooled_ref[...], wq_ref[...]).T.astype(BF16)


def queries(pooled, w_query):
    patches, width = pooled.shape
    return pl.pallas_call(
        queries_kernel,
        in_specs=[pl.BlockSpec(memory_space=pltpu.VMEM)] * 2,
        out_specs=pl.BlockSpec(memory_space=pltpu.VMEM),
        out_shape=jax.ShapeDtypeStruct((width, patches), BF16),
        compiler_params=params(),
        cost_estimate=cost(1 << 30, 4 << 20),
        name="queries",
    )(pooled, w_query)


def out_grad_kernel(member, att_ref, cot_ref, owner_ref, out_ref, rows_ref):
    groups, own, patches = att_ref.shape
    att = att_ref[...].reshape(groups * own, patches)
    codes, power = coded(dot(att, cot_ref[...]))
    parts = out_ref.shape[0]
    rows = codes.shape[0] // parts
    slabs = codes.shape[1] // LANES
    tail = to_i16(padded_rows([power[:, at * LANES:(at + 1) * LANES] for at in range(slabs)], 16))
    for part in range(parts):
        for at in range(slabs):
            block = codes[part * rows:(part + 1) * rows, at * LANES:(at + 1) * LANES]
            out_ref[part, at * rows:(at + 1) * rows, :] = to_i16(block)
        out_ref[part, slabs * rows:, :] = tail
    count = rows_ref.shape[0]
    order = jnp.broadcast_to(owner_ref[...], (8, patches))
    order = pltpu.roll(order, lax.rem(patches - member[0] * count, patches), 1)[0:1, :LANES]
    pick = jnp.where(lax.broadcasted_iota(I32, (patches, LANES), 0) == order, 1.0, 0.0).astype(BF16)
    rows_ref[...] = dot(att, pick).T[:count].astype(BF16)


def out_grad(member, att, cot, owner, parts):
    groups, own, patches = att.shape
    width, cols = groups * own, cot.shape[1]
    rows = cols // LANES * (width // parts) + 16
    count = patches // groups
    return pl.pallas_call(
        out_grad_kernel,
        in_specs=[smem()] + [pl.BlockSpec(memory_space=pltpu.VMEM)] * 3,
        out_specs=[pl.BlockSpec(memory_space=pltpu.VMEM)] * 2,
        out_shape=[
            jax.ShapeDtypeStruct((parts, rows, LANES), I16),
            jax.ShapeDtypeStruct((count, width), BF16),
        ],
        compiler_params=params(),
        cost_estimate=cost(2 * width * cols * patches, 4 << 20),
        name="out_grad",
    )(member, att, cot, owner)


def decoded(got_ref, first, count, power_row):
    rows = got_ref.shape[1]
    total = jnp.zeros((count, got_ref.shape[2]), F32)
    for source in range(got_ref.shape[0]):
        scale = unit(got_ref[source, rows - 16:, :])[power_row:power_row + 1]
        total = total + from_i16(got_ref[source, first:first + count, :]) * scale
    return total


def qkv_sum_kernel(member, got_ref, *refs):
    outs, blocks = refs[:-1], refs[-1]
    count = (got_ref.shape[1] - 16) // 3
    totals = [decoded(got_ref, k * count, count, k) for k in range(3)]
    for group in range(len(outs)):
        rows = [total[group * 8:(group + 1) * 8] for total in totals]
        blocks[group] = jnp.concatenate(rows + [jnp.zeros_like(rows[0])], axis=0)
    for at, out in enumerate(outs):
        out[...] = blocks[member[0] ^ at].astype(BF16)


def qkv_sum(member, got, groups):
    vmem = pl.BlockSpec(memory_space=pltpu.VMEM)
    return pl.pallas_call(
        qkv_sum_kernel,
        in_specs=[smem(), vmem],
        out_specs=[vmem] * groups,
        out_shape=[jax.ShapeDtypeStruct((32, LANES), BF16)] * groups,
        scratch_shapes=[pltpu.VMEM((groups, 32, LANES), F32)],
        compiler_params=params(),
        cost_estimate=cost(1 << 20, 2 << 20),
        name="qkv_sum",
    )(member, got)


def pack_kernel(got_ref, *refs):
    blocks, out_hbm, pack, sems = refs[:-3], refs[-3], refs[-2], refs[-1]
    first = 24 * len(blocks)
    rows = [block[...].astype(F32)[:24] for block in blocks]
    pack[:first, :] = jnp.concatenate(rows, axis=0).astype(BF16)
    count = (pack.shape[0] - first) // 4
    for slab in range(4):
        total = decoded(got_ref, slab * count, count, slab)
        pack[first + slab * count:first + (slab + 1) * count, :] = total.astype(BF16)
    for copy in send_copies(pack, out_hbm, sems):
        copy.wait()


def pack_sums(got, blocks, parts):
    vmem = pl.BlockSpec(memory_space=pltpu.VMEM)
    rows = 24 * len(blocks) + got.shape[1] - 16
    return pl.pallas_call(
        pack_kernel,
        in_specs=[vmem] * (1 + len(blocks)),
        out_specs=hbm(),
        out_shape=jax.ShapeDtypeStruct((parts, rows, LANES), BF16),
        scratch_shapes=[pltpu.VMEM((rows, LANES), BF16), pltpu.SemaphoreType.DMA((parts,))],
        compiler_params=params(),
        cost_estimate=cost(1 << 20, 3 << 20),
        name="pack_sums",
    )(got, *blocks)


def unpack_kernel(member, got_ref, qkv_ref, wout_ref):
    parts, rows, lanes = got_ref.shape
    groups = qkv_ref.shape[2] // lanes
    first = 24 * groups
    count = wout_ref.shape[0] // parts
    for part in range(parts):
        for slab in range(wout_ref.shape[1] // lanes):
            block = got_ref[part, first + slab * count:first + (slab + 1) * count, :]
            wout_ref[part * count:(part + 1) * count, slab * lanes:(slab + 1) * lanes] = block.astype(F32)
        values = got_ref[part, :first, :].astype(F32)
        for at in range(groups):
            lane = pl.ds(pl.multiple_of((member[0] ^ at) * lanes, lanes), lanes)
            for k in range(3):
                top = at * 24 + k * 8
                qkv_ref[k, part * 8:(part + 1) * 8, lane] = values[top:top + 8]


def unpack_sums(member, got, width, cols, groups):
    parts, rows, lanes = got.shape
    steps = 4
    return pl.pallas_call(
        unpack_kernel,
        grid=(steps,),
        in_specs=[smem(), pl.BlockSpec((parts // steps, rows, lanes), lambda i: (i, 0, 0))],
        out_specs=[
            pl.BlockSpec((3, width // groups // steps, width), lambda i: (0, i, 0)),
            pl.BlockSpec((width // steps, cols), lambda i: (i, 0)),
        ],
        out_shape=[
            jax.ShapeDtypeStruct((3, width // groups, width), F32),
            jax.ShapeDtypeStruct((width, cols), F32),
        ],
        compiler_params=params(),
        cost_estimate=cost(1 << 20, 6 << 20),
        name="unpack_sums",
    )(member, got)


def bytes_kernel(
    member, bounds, mine_ref, other_ref, query_ref, wk_own, wv_own, wq_own, row_ref,
    out_ref, head_ref, tail_ref,
    lhs, d_query, shares, d_kv, w_own, start_ref, end_ref,
):
    chips, rows, patches = mine_ref.shape
    groups = 2 * chips
    own, width = wq_own.shape
    dim = 64
    heads = own // dim
    blocks = patches // LANES
    total = shares.shape[2]
    s_dev = out_ref.shape[0]
    rim = total - s_dev
    columns_of(row_ref, start_ref, end_ref)
    lhs[:width, :] = query_ref[...]
    chip, core = member[0] // 2, member[0] % 2
    for ref, ref_core in ((mine_ref, core), (other_ref, 1 - core)):
        for back in range(chips):
            group = 2 * lax.rem(chip + chips - back, chips) + ref_core
            at_rows = pl.multiple_of(group * own, own)
            lhs[pl.ds(width + at_rows, own), :] = ref[back, :own, :]
            d_query[pl.ds(at_rows, own), :] = ref[back, own:2 * own, :]
            table = ref[back, 2 * own:, :].astype(F32)
            for at in range(s_dev // patches):
                shares[group, :, at * patches:(at + 1) * patches] = table[8 * at:8 * at + 8]
            at = s_dev // patches
            shares[group, :, s_dev:] = table[8 * at:8 * at + 8, :rim]
    length = (row_ref[8:9, :] - row_ref[0:1, :]).astype(F32)
    lhs[2 * width:, :] = split2(dot(wq_own[...], d_query[...]) * (1.0 / length))
    w_own[:, :width] = wk_own[...]
    w_own[:, width:] = wv_own[...]

    def tile_grad(base, span, first, count, slot):
        inside = patch_major(start_ref, end_ref, first, count, base, span)
        at = pl.ds(base, span)
        patch = pl.ds(first, count)
        for group in range(groups):
            share = shares[group, :, at]
            for kind in range(2):
                top = kind * width + group * own
                wide = dot(lhs[top:top + own, patch], inside)
                part = head_rows(share[kind * heads:(kind + 1) * heads], dim)
                d_kv[slot, top:top + own, :span] = (part * wide).astype(BF16)
        grad = dot(w_own[...], d_kv[slot, :, :span])
        pool = dot(lhs[2 * width:, patch], inside)
        return (grad + (pool[:own] + pool[own:])).T

    def tiles(span, first_of, count):
        def go(i, carry):
            for slot in range(2):
                base = pl.multiple_of((2 * i + slot) * span, span)
                out_ref[pl.ds(base, span), :] = tile_grad(base, span, first_of(base), count, slot).astype(BF16)
            return carry

        lax.fori_loop(0, s_dev // (2 * span), go, 0)

    def first_of(base):
        return pl.multiple_of(window(bounds, blocks, base) * LANES, LANES)

    @pl.when(bounds[blocks + 1] > 0)
    def _():
        tiles(LANES, first_of, 2 * LANES)

    @pl.when(bounds[blocks + 1] == 0)
    def _():
        tiles(TILE, first_of, 2 * LANES)

    head_ref[...] = tile_grad(0, LANES, 0, 2 * LANES, 0)[:16]
    tail_ref[...] = tile_grad(s_dev, rim, patches - 2 * LANES, 2 * LANES, 1)[:16]


def byte_grads(member, bounds, mine_factors, other_factors, query, w_query, w_key, w_value, row, s_dev):
    chips, rows, patches = mine_factors.shape
    groups = 2 * chips
    width = w_query.shape[0]
    own = width // groups
    rim = LANES
    mine = pl.BlockSpec((own, width), lambda i, member, bounds: (member[0], 0))
    return pl.pallas_call(
        bytes_kernel,
        grid_spec=pltpu.PrefetchScalarGridSpec(
            num_scalar_prefetch=2,
            grid=(1,),
            in_specs=[whole(mine_factors.shape), whole(other_factors.shape), whole(query.shape), mine, mine, mine, whole(row.shape)],
            out_specs=[whole((s_dev, own)), whole((16, own)), whole((16, own))],
            scratch_shapes=[
                pltpu.VMEM((2 * width + 2 * own, patches), BF16),
                pltpu.VMEM((width, patches), BF16),
                pltpu.VMEM((groups, 8, s_dev + rim), F32),
                pltpu.VMEM((2, 2 * width, TILE), BF16),
                pltpu.VMEM((own, 2 * width), BF16),
                pltpu.VMEM((patches, LANES), I32),
                pltpu.VMEM((patches, LANES), I32),
            ],
        ),
        out_shape=[
            jax.ShapeDtypeStruct((s_dev, own), BF16),
            jax.ShapeDtypeStruct((16, own), F32),
            jax.ShapeDtypeStruct((16, own), F32),
        ],
        compiler_params=params(),
        cost_estimate=cost(8 << 30, 8 << 20),
        name="byte_grads",
    )(member, bounds, mine_factors, other_factors, query, w_key, w_value, w_query, row)


def shifted(value, axis, steps):
    count = lax.axis_size(axis)
    first, last = (max(0, -steps), min(count, count - steps))
    return lax.ppermute(value, axis, [(source, source + steps) for source in range(first, last)])


def swap(value, axis):
    return lax.all_to_all(value, axis, split_axis=0, concat_axis=0, tiled=True)


def over_chips(value):
    count = lax.axis_size("patch")
    blocks = [value]
    for step in range(1, count // 2):
        pairs = [(i, (i + 2 * step) % count) for i in range(count)]
        blocks.append(lax.ppermute(value, "patch", pairs))
    return blocks


def other_core(value):
    return lax.ppermute(value, "patch", [(i, i ^ 1) for i in range(lax.axis_size("patch"))])


def after(value, *others):
    return lax.optimization_barrier((value,) + others)[0]


def local(byte_states, patch_len, shard_offset, owner, cotangent, w_query, w_key, w_value, w_out):
    s_dev, width = byte_states.shape
    groups = lax.axis_size("patch")
    parts = lax.axis_size("seq")
    member = lax.axis_index("patch").astype(I32).reshape(1)
    rim = shifted(byte_states[:MAXP], "seq", -1)

    coded_att = after(att_grad(w_out, cotangent, groups), rim)
    got_att = swap(coded_att, "patch")
    kv, pooled, att, query, probs, geo, row, bounds = forward(
        member, shard_offset, patch_len, byte_states, rim, w_key, w_value, w_query, groups
    )
    all_att = swap(after(att, got_att), "patch")
    grads, factor = backward(bounds, byte_states, kv, pooled, rim, got_att, query, probs, geo, row, parts)
    got_qkv = swap(after(grads, all_att), "seq")
    columns = over_chips(factor)
    coded_out, patch_rows = out_grad(member, after(all_att, grads), cotangent, owner, parts)
    got_out = swap(after(coded_out, got_qkv, *columns), "seq")
    all_query = queries(after(pooled, got_qkv), w_query)
    mine = jnp.stack(columns)
    other = other_core(mine)
    blocks = qkv_sum(member, got_qkv, groups)
    blocks = [blocks[0]] + [
        lax.ppermute(block, "patch", [(i, i ^ at) for i in range(groups)])
        for at, block in enumerate(blocks) if at > 0
    ]
    sums = swap(pack_sums(after(got_out, all_query, other), blocks, parts), "seq")
    d_bytes, head, tail = byte_grads(
        member, bounds, mine, other, all_query, w_query, w_key, w_value, row, s_dev
    )
    first = (head + shifted(tail, "seq", 1)).astype(BF16)
    d_bytes = lax.dynamic_update_slice(d_bytes, first, (0, 0))
    d_qkv, d_wout = unpack_sums(member, sums, width, cotangent.shape[1], groups)
    return (d_bytes, d_qkv, d_wout, patch_rows)


def solution(mesh):
    return jax.shard_map(
        local,
        mesh=mesh,
        in_specs=(
            P("seq", None), P("seq", None), P("seq"), P("seq", None), P("seq", "patch"),
            P(), P(), P(), P(None, "patch"),
        ),
        out_specs=(P("seq", "patch"), P(None, "patch", None), P(None, "patch"), P(("seq", "patch"), None)),
        check_vma=False,
    )
```

```python
import jax
import jax.numpy as jnp
from jax import lax
from jax.experimental import pallas as pl
from jax.experimental.pallas import tpu as pltpu
from jax.sharding import PartitionSpec as P

HEADS = 16
MAXP = 16
LANES = 128
TILE = 256
UNROLL = 4
F32, BF16, I16, I32 = jnp.float32, jnp.bfloat16, jnp.int16, jnp.int32
NT = (((1,), (1,)), ((), ()))


def params(mebibytes):
    return pltpu.CompilerParams(vmem_limit_bytes=mebibytes * 1024 * 1024)


def cost(flops, moved):
    return pl.CostEstimate(flops=flops, bytes_accessed=moved, transcendentals=0)


def whole(shape):
    return pl.BlockSpec(shape, lambda *_: (0,) * len(shape))


def smem():
    return pl.BlockSpec(memory_space=pltpu.SMEM)


def dot(a, b):
    return jnp.dot(a, b, preferred_element_type=F32)


def dot_nt(a, b):
    return lax.dot_general(a, b, NT, preferred_element_type=F32)


def coded(value):
    peak = jnp.max(jnp.abs(value), axis=0, keepdims=True)
    power = jnp.ceil(jnp.log2(jnp.maximum(peak, 1e-30)))
    return jnp.round(value * (32767.0 * jnp.exp2(-power))), power


def to_i16(value):
    return value.astype(I32).astype(I16)


def from_i16(value):
    return value.astype(I32).astype(F32)


def unit(power):
    return jnp.exp2(from_i16(power)) * (1.0 / 32767.0)


def padded_rows(row_list, count):
    width = row_list[0].shape[1]
    at = lax.broadcasted_iota(I32, (count, width), 0)
    out = jnp.zeros((count, width), F32)
    for i, row in enumerate(row_list):
        out = jnp.where(at == i, jnp.broadcast_to(row, (count, width)), out)
    return out


def window(bounds, blocks, base):
    block = jnp.int32(0)
    for at in range(1, blocks - 1):
        block = block + (bounds[at] <= base).astype(I32)
    return block


def patch_major(start_ref, end_ref, first, count, base, width):
    rows = pl.ds(pl.multiple_of(first, LANES), count)
    start, end = start_ref[rows, :], end_ref[rows, :]
    parts = []
    for at in range(0, width, LANES):
        byte = base + at + lax.broadcasted_iota(I32, (count, LANES), 1)
        parts.append(jnp.where((byte >= start) & (byte < end), 1.0, 0.0).astype(BF16))
    return parts[0] if len(parts) == 1 else jnp.concatenate(parts, axis=1)


def byte_major(row_ref, first, count, base, width):
    lanes = pl.ds(pl.multiple_of(first, LANES), count)
    byte = base + lax.broadcasted_iota(I32, (width, count), 0)
    inside = (byte >= row_ref[0:1, lanes]) & (byte < row_ref[8:9, lanes])
    return jnp.where(inside, 1.0, 0.0).astype(BF16)


def over_tiles(bounds, blocks, s_dev, rim, body):
    def loop(width, unroll):
        def go(i, carry):
            for at in range(unroll):
                body(pl.multiple_of((i * unroll + at) * width, width), width)
            return carry

        lax.fori_loop(0, s_dev // (unroll * width), go, 0)

    @pl.when(bounds[blocks + 1] == 0)
    def _():
        loop(TILE, UNROLL)

    @pl.when(bounds[blocks + 1] > 0)
    def _():
        loop(LANES, 1)

    body(s_dev, rim)


def fill_rim(rim_ref, rim_rows):
    rim_rows[...] = jnp.zeros_like(rim_rows)
    rim_rows[:rim_ref.shape[0], :] = rim_ref[...]


def columns_of(row_ref, start_ref, end_ref):
    patches = row_ref.shape[1]
    start_ref[...] = jnp.broadcast_to(row_ref[0:1, :], (LANES, patches)).T
    end_ref[...] = jnp.broadcast_to(row_ref[8:9, :], (LANES, patches)).T


def send_copies(source, target, sems):
    copies = [pltpu.make_async_copy(source, target.at[i], sems.at[i]) for i in range(target.shape[0])]
    for copy in copies:
        copy.start()
    return copies


def over_segment(value, place, left, op):
    size = value.shape[1]
    before, after = value, value
    for step in (1, 2, 4, 8):
        before = jnp.where(place >= step, op(before, pltpu.roll(before, step, 1)), before)
        after = jnp.where(left >= step, op(after, pltpu.roll(after, size - step, 1)), after)
    return before, after


def head_rows(rows, dim):
    count, width = rows.shape
    return jnp.concatenate(
        [jnp.broadcast_to(rows[i:i + 1], (dim, width)) for i in range(count)], axis=0
    )


def split2(value):
    high = value.astype(BF16)
    return jnp.concatenate([high, (value - high.astype(F32)).astype(BF16)], axis=0)


def att_grad_kernel(w_ref, cot_ref, out_ref, cot_t):
    groups = out_ref.shape[0]
    own = w_ref.shape[0] // groups
    cot_t[...] = cot_ref[...].astype(F32).T.astype(BF16)
    for group in range(groups):
        codes, power = coded(dot(w_ref[group * own:(group + 1) * own, :], cot_t[...]))
        out_ref[group, :own, :] = to_i16(codes)
        out_ref[group, own:, :] = to_i16(jnp.broadcast_to(power, (16, power.shape[1])))


def att_grad(w_out, cot, groups):
    width, cols = w_out.shape
    rows = cot.shape[0]
    own = width // groups
    return pl.pallas_call(
        att_grad_kernel,
        in_specs=[pl.BlockSpec(memory_space=pltpu.VMEM)] * 2,
        out_specs=pl.BlockSpec(memory_space=pltpu.VMEM),
        out_shape=jax.ShapeDtypeStruct((groups, own + 16, rows), I16),
        scratch_shapes=[pltpu.VMEM((cols, rows), BF16)],
        compiler_params=params(56),
        cost_estimate=cost(2 * width * cols * rows, 4 << 20),
        name="att_grad",
    )(w_out, cot)


def forward_kernel(
    member, offset, len_ref, x_hbm, rim_ref, wk_ref, wv_ref, wq_ref,
    kv_hbm, pooled_hbm, att_hbm, query_ref, probs_ref, geo_ref, row_ref, bounds,
    rim_rows, x_ref, kv_ref, pooled_ref, att_ref, w_kv, wq_t, acc, lhs, start_ref, end_ref, inv_col, att_acc,
    x_sems, out_sems, att_sems,
):
    rim = rim_rows.shape[0]
    patches = len_ref.shape[1]
    blocks = patches // LANES
    own = wk_ref.shape[1]
    dim = 64
    heads = own // dim
    s_dev = x_hbm.shape[0]
    chunks = x_sems.shape[0]
    chunk = s_dev // chunks
    loads = []
    for i in range(chunks):
        at = slice(i * chunk, (i + 1) * chunk)
        loads.append(pltpu.make_async_copy(x_hbm.at[at, :], x_ref.at[at, :], x_sems.at[i]))
        loads[-1].start()

    length = len_ref[...].astype(F32)
    before = lax.broadcasted_iota(I32, (patches, patches), 0)
    after = lax.broadcasted_iota(I32, (patches, patches), 1)
    off = offset[0].astype(F32)
    eight = jnp.broadcast_to(length, (8, patches))
    upper = jnp.where(before < after, 1.0, 0.0).astype(BF16)
    start_row = (dot(eight.astype(BF16), upper) + off).astype(I32)
    row_ref[:8, :] = start_row
    row_ref[8:, :] = start_row + eight.astype(I32)
    columns_of(row_ref, start_ref, end_ref)
    inv_col[...] = 1.0 / jnp.broadcast_to(length, (LANES, patches)).T
    at = lax.broadcasted_iota(I32, (16, patches), 0)
    both = jnp.concatenate([start_row, start_row], axis=0)
    geo = jnp.where(at == 0, both >> 6, jnp.where(at == 1, both & 63, 0)).astype(F32)
    geo = jnp.where(at == 2, jnp.broadcast_to(length, (16, patches)), geo)
    lhs[own:own + 16, :] = geo.astype(BF16)
    lane = lax.broadcasted_iota(I32, (1, patches), 1)
    for block in range(blocks + 1):
        total = jnp.sum(jnp.where(lane < block * LANES, length, 0.0))
        bounds[block] = (total + off).astype(I32)

    def crowded(i, found):
        base = i * TILE
        third = window(bounds, blocks, base) + 2
        return found | ((third < blocks) & (bounds[third] < base + TILE)).astype(I32)

    bounds[blocks + 1] = lax.fori_loop(0, s_dev // TILE, crowded, jnp.int32(0))
    w_kv[:, :own] = wk_ref[...]
    w_kv[:, own:] = wv_ref[...]
    wq_t[...] = wq_ref[...].astype(F32).T.astype(BF16)
    acc[...] = jnp.zeros_like(acc)

    def project(rows, base, width):
        kv_ref[:, pl.ds(base, width)] = dot(rows, w_kv[...]).T.astype(BF16)
        first = pl.multiple_of(window(bounds, blocks, base) * LANES, LANES)
        at = pl.ds(first, 2 * LANES)
        acc[at, :] += dot(patch_major(start_ref, end_ref, first, 2 * LANES, base, width), rows)

    for i in range(chunks):
        loads[i].wait()
        for at in range(i * chunk, (i + 1) * chunk, TILE):
            project(x_ref[at:at + TILE, :], at, TILE)
    fill_rim(rim_ref, rim_rows)
    project(rim_rows[...], s_dev, rim)

    @pl.when(bounds[blocks + 1] > 0)
    def _():
        def rest(i, carry):
            base = pl.multiple_of(i * TILE, TILE)
            third = window(bounds, blocks, base) + 2

            @pl.when((third < blocks) & (bounds[third] < base + TILE))
            def _():
                first = pl.multiple_of(third * LANES, LANES)
                acc[pl.ds(first, LANES), :] += dot(
                    patch_major(start_ref, end_ref, first, LANES, base, TILE), x_ref[pl.ds(base, TILE), :]
                )

            return carry

        lax.fori_loop(0, s_dev // TILE, rest, 0)

    kv_copy = pltpu.make_async_copy(kv_ref, kv_hbm, out_sems.at[0])
    kv_copy.start()
    pooled = (acc[...] * inv_col[:, :1]).astype(BF16)
    pooled_ref[...] = pooled
    pooled_copy = pltpu.make_async_copy(pooled_ref, pooled_hbm, out_sems.at[1])
    pooled_copy.start()
    query = dot_nt(wq_t[...], pooled).astype(BF16)
    lhs[:own, :] = query
    query_ref[...] = query

    def score(base, width):
        first = pl.multiple_of(window(bounds, blocks, base) * LANES, LANES)
        exp = dot(
            lhs[:, pl.ds(first, 2 * LANES)],
            patch_major(start_ref, end_ref, first, 2 * LANES, base, width),
        )
        at = pl.ds(base, width)
        product = exp[:own] * kv_ref[:own, at].astype(F32)
        rows = [jnp.sum(product[h * dim:(h + 1) * dim], axis=0, keepdims=True) for h in range(heads)]
        probs_ref[:, at] = padded_rows(rows, 8) * (dim ** -0.5)
        geo = exp[own:own + 8]
        byte = (base + lax.broadcasted_iota(I32, (1, width), 1)).astype(F32)
        place = byte - (64.0 * geo[0:1] + geo[1:2])
        geo_ref[:, at] = padded_rows([place, geo[2:3] - 1.0 - place], 8)

    over_tiles(bounds, blocks, s_dev, rim, score)
    place, left = geo_ref[0:1, :], geo_ref[1:2, :]
    scores = probs_ref[...]
    before, after = over_segment(scores, place, left, jnp.maximum)
    expo = jnp.exp(scores - jnp.maximum(before, after))
    before, after = over_segment(expo, place, left, jnp.add)
    probs_ref[...] = jnp.where(left >= 0.0, expo / (before + (after - expo)), 0.0)
    att_acc[...] = jnp.zeros_like(att_acc)

    def attend(base, width):
        at = pl.ds(base, width)
        probs_b = probs_ref[:, at].astype(BF16).astype(F32)[:heads]
        both = split2(head_rows(probs_b, dim) * kv_ref[own:, at].astype(F32))
        first = pl.multiple_of(window(bounds, blocks, base) * LANES, LANES)
        att_acc[:, pl.ds(first, 2 * LANES)] += dot(
            both, byte_major(row_ref, first, 2 * LANES, base, width)
        )

    over_tiles(bounds, blocks, s_dev, rim, attend)
    att_ref[...] = (att_acc[:own, :] + att_acc[own:, :]).astype(BF16)
    for copy in send_copies(att_ref, att_hbm, att_sems) + [kv_copy, pooled_copy]:
        copy.wait()


def hbm():
    return pl.BlockSpec(memory_space=pltpu.HBM)


def near():
    return pl.BlockSpec(memory_space=pl.ANY)


def forward(member, offset, lengths, x, rim, w_key, w_value, w_query, groups):
    s_dev, width = x.shape
    patches = lengths.shape[1]
    own = width // groups
    total = s_dev + LANES
    col = pl.BlockSpec((width, own), lambda i, member, offset: (0, member[0]))
    shape = jax.ShapeDtypeStruct
    small = [
        shape((own, patches), BF16), shape((8, total), F32), shape((8, total), F32), shape((16, patches), I32),
    ]
    return pl.pallas_call(
        forward_kernel,
        grid_spec=pltpu.PrefetchScalarGridSpec(
            num_scalar_prefetch=2,
            grid=(1,),
            in_specs=[whole(lengths.shape), hbm(), whole(rim.shape), col, col, col],
            out_specs=[hbm()] * 3 + [whole(s.shape) for s in small] + [smem()],
            scratch_shapes=[
                pltpu.VMEM((LANES, width), BF16),
                pltpu.VMEM((s_dev, width), BF16),
                pltpu.VMEM((2 * own, total), BF16),
                pltpu.VMEM((patches, width), BF16),
                pltpu.VMEM((own, patches), BF16),
                pltpu.VMEM((width, 2 * own), BF16),
                pltpu.VMEM((own, width), BF16),
                pltpu.VMEM((patches, width), F32),
                pltpu.VMEM((own + 16, patches), BF16),
                pltpu.VMEM((patches, LANES), I32),
                pltpu.VMEM((patches, LANES), I32),
                pltpu.VMEM((patches, LANES), F32),
                pltpu.VMEM((2 * own, patches), F32),
                pltpu.SemaphoreType.DMA((8,)),
                pltpu.SemaphoreType.DMA((2,)),
                pltpu.SemaphoreType.DMA((groups,)),
            ],
        ),
        out_shape=[shape((2 * own, total), BF16), shape((patches, width), BF16), shape((groups, own, patches), BF16)]
        + small + [shape((8,), I32)],
        compiler_params=params(56),
        cost_estimate=cost(8 << 30, 12 << 20),
        name="forward",
    )(member, offset, lengths, x, rim, w_key, w_value, w_query)


def backward_kernel(
    bounds, x_hbm, kv_hbm, pooled_hbm, rim_ref, got_ref, query_ref, probs_ref, geo_ref, row_ref,
    grad_ref, factor_out,
    rim_rows, x_ref, kv_ref, pooled_ref, factor_ref, start_ref, end_ref, d_kv, lhs, d_probs, d_scores, dq_acc, acc,
    x_sems, in_sems,
):
    rim = rim_rows.shape[0]
    s_dev = x_hbm.shape[0]
    own, patches = query_ref.shape
    blocks = patches // LANES
    dim = 64
    heads = own // dim
    sources = got_ref.shape[0]
    kv_copy = pltpu.make_async_copy(kv_hbm, kv_ref, in_sems.at[0])
    kv_copy.start()
    chunks = x_sems.shape[0]
    chunk = s_dev // chunks
    loads = []
    for i in range(chunks):
        at = slice(i * chunk, (i + 1) * chunk)
        loads.append(pltpu.make_async_copy(x_hbm.at[at, :], x_ref.at[at, :], x_sems.at[i]))
    pooled_copy = pltpu.make_async_copy(pooled_hbm, pooled_ref, in_sems.at[1])

    columns_of(row_ref, start_ref, end_ref)
    summed = jnp.zeros((own, patches), F32)
    for source in range(sources):
        summed = summed + from_i16(got_ref[source, :own, :]) * unit(got_ref[source, own:, :])[0:1]
    lhs[:own, :] = summed.astype(BF16)
    lhs[own:, :] = query_ref[...]
    factor_ref[:own, :] = summed.astype(BF16)
    kv_copy.wait()
    for copy in loads + [pooled_copy]:
        copy.start()

    def first_pass(base, width):
        first = pl.multiple_of(window(bounds, blocks, base) * LANES, LANES)
        exp = dot(
            lhs[:, pl.ds(first, 2 * LANES)],
            patch_major(start_ref, end_ref, first, 2 * LANES, base, width),
        )
        d_out = exp[:own]
        at = pl.ds(base, width)
        product = d_out * kv_ref[own:, at].astype(F32)
        rows = [jnp.sum(product[h * dim:(h + 1) * dim], axis=0, keepdims=True) for h in range(heads)]
        d_probs[:, at] = padded_rows(rows, 8)
        probs_b = probs_ref[:, at].astype(BF16).astype(F32)[:heads]
        d_kv[own:, at] = (head_rows(probs_b, dim) * d_out).astype(BF16)
        d_kv[:own, at] = exp[own:].astype(BF16)

    over_tiles(bounds, blocks, s_dev, rim, first_pass)
    place, left = geo_ref[0:1, :], geo_ref[1:2, :]
    probs = probs_ref[...]
    weighted = probs * d_probs[...]
    before, after = over_segment(weighted, place, left, jnp.add)
    inner = before + (after - weighted)
    slope = jnp.where(left >= 0.0, probs * (d_probs[...] - inner) * (dim ** -0.5), 0.0)
    d_scores[...] = slope.astype(BF16).astype(F32)
    dq_acc[...] = jnp.zeros_like(dq_acc)

    def second_pass(base, width):
        at = pl.ds(base, width)
        wide = head_rows(d_scores[:, at][:heads], dim)
        d_kv[:own, at] = (wide * d_kv[:own, at].astype(F32)).astype(BF16)
        both = split2(wide * kv_ref[:own, at].astype(F32))
        first = pl.multiple_of(window(bounds, blocks, base) * LANES, LANES)
        dq_acc[:, pl.ds(first, 2 * LANES)] += dot(
            both, byte_major(row_ref, first, 2 * LANES, base, width)
        )

    over_tiles(bounds, blocks, s_dev, rim, second_pass)
    factor_ref[own:2 * own, :] = (dq_acc[:own, :] + dq_acc[own:, :]).astype(BF16)
    probs_b = probs.astype(BF16).astype(F32)
    rows = padded_rows(
        [d_scores[h:h + 1, :] for h in range(heads)] + [probs_b[h:h + 1, :] for h in range(heads)], 8
    )
    groups = [rows[:, at:at + patches] for at in range(0, s_dev, patches)]
    groups.append(jnp.concatenate([rows[:, s_dev:], jnp.zeros((8, patches - rim), F32)], axis=1))
    groups += [jnp.zeros((8, patches), F32)] * ((factor_ref.shape[0] - 2 * own) // 4 - len(groups))
    upper = lax.broadcasted_iota(I32, (8, patches), 0) < 4
    stack = [
        jnp.where(upper, groups[i], pltpu.roll(groups[i + 1], 4, 0)) for i in range(0, len(groups), 2)
    ]
    factor_ref[2 * own:, :] = jnp.concatenate(stack, axis=0).astype(BF16)
    factor_out[...] = factor_ref[...]

    fill_rim(rim_ref, rim_rows)
    acc[...] = dot(d_kv[:, s_dev:], rim_rows[...])
    for i in range(chunks):
        loads[i].wait()
    acc[...] += dot(d_kv[:, :s_dev], x_ref[...])
    pooled_copy.wait()
    grad_q = dot(factor_ref[own:2 * own, :], pooled_ref[...])
    powers = []
    parts = grad_ref.shape[0]
    for k, grad in enumerate((grad_q, acc[:own, :], acc[own:, :])):
        codes, power = coded(grad.T)
        powers.append(power)
        rows = codes.shape[0] // parts
        spread = codes.reshape(rows // 8, parts, 8, own)
        for part in range(parts):
            grad_ref[part, k * rows:(k + 1) * rows, :] = to_i16(spread[:, part].reshape(rows, own))
    tail = to_i16(padded_rows(powers, 16))
    for part in range(parts):
        grad_ref[part, 3 * rows:, :] = tail


def backward(bounds, x, kv, pooled, rim, got, query, probs, geo, row, parts):
    s_dev, width = x.shape
    own, patches = query.shape
    groups = got.shape[0]
    total = kv.shape[1]
    extra = -(-4 * (s_dev // patches + 1) // 16) * 16
    rows = width // parts
    vmem = pl.BlockSpec(memory_space=pltpu.VMEM)
    return pl.pallas_call(
        backward_kernel,
        in_specs=[smem()] + [hbm()] * 3 + [vmem] * 6,
        out_specs=[vmem, vmem],
        out_shape=[
            jax.ShapeDtypeStruct((parts, 3 * rows + 16, own), I16),
            jax.ShapeDtypeStruct((2 * own + extra, patches), BF16),
        ],
        scratch_shapes=[
            pltpu.VMEM((LANES, width), BF16),
            pltpu.VMEM((s_dev, width), BF16),
            pltpu.VMEM((2 * own, total), BF16),
            pltpu.VMEM((patches, width), BF16),
            pltpu.VMEM((2 * own + extra, patches), BF16),
            pltpu.VMEM((patches, LANES), I32),
            pltpu.VMEM((patches, LANES), I32),
            pltpu.VMEM((2 * own, total), BF16),
            pltpu.VMEM((2 * own, patches), BF16),
            pltpu.VMEM((8, total), F32),
            pltpu.VMEM((8, total), F32),
            pltpu.VMEM((2 * own, patches), F32),
            pltpu.VMEM((2 * own, width), F32),
            pltpu.SemaphoreType.DMA((4,)),
            pltpu.SemaphoreType.DMA((2,)),
        ],
        compiler_params=params(56),
        cost_estimate=cost(6 << 30, 16 << 20),
        name="backward",
    )(bounds, x, kv, pooled, rim, got, query, probs, geo, row)


def queries_kernel(pooled_ref, wq_ref, out_ref):
    out_ref[...] = dot(pooled_ref[...], wq_ref[...]).T.astype(BF16)


def queries(pooled, w_query):
    patches, width = pooled.shape
    return pl.pallas_call(
        queries_kernel,
        in_specs=[pl.BlockSpec(memory_space=pltpu.VMEM)] * 2,
        out_specs=pl.BlockSpec(memory_space=pltpu.VMEM),
        out_shape=jax.ShapeDtypeStruct((width, patches), BF16),
        compiler_params=params(16),
        cost_estimate=cost(1 << 30, 4 << 20),
        name="queries",
    )(pooled, w_query)


def out_grad_kernel(member, att_ref, cot_ref, owner_ref, out_ref, rows_ref):
    groups, own, patches = att_ref.shape
    att = att_ref[...].reshape(groups * own, patches)
    codes, power = coded(dot(att, cot_ref[...]))
    parts = out_ref.shape[0]
    rows = codes.shape[0] // parts
    slabs = codes.shape[1] // LANES
    tail = to_i16(padded_rows([power[:, at * LANES:(at + 1) * LANES] for at in range(slabs)], 16))
    for part in range(parts):
        for at in range(slabs):
            block = codes[part * rows:(part + 1) * rows, at * LANES:(at + 1) * LANES]
            out_ref[part, at * rows:(at + 1) * rows, :] = to_i16(block)
        out_ref[part, slabs * rows:, :] = tail
    count = rows_ref.shape[0]
    order = jnp.broadcast_to(owner_ref[...], (8, patches))
    order = pltpu.roll(order, lax.rem(patches - member[0] * count, patches), 1)[0:1, :LANES]
    pick = jnp.where(lax.broadcasted_iota(I32, (patches, LANES), 0) == order, 1.0, 0.0).astype(BF16)
    rows_ref[...] = dot(att, pick).T[:count].astype(BF16)


def out_grad(member, att, cot, owner, parts):
    groups, own, patches = att.shape
    width, cols = groups * own, cot.shape[1]
    rows = cols // LANES * (width // parts) + 16
    count = patches // groups
    return pl.pallas_call(
        out_grad_kernel,
        in_specs=[smem()] + [pl.BlockSpec(memory_space=pltpu.VMEM)] * 3,
        out_specs=[pl.BlockSpec(memory_space=pltpu.VMEM)] * 2,
        out_shape=[
            jax.ShapeDtypeStruct((parts, rows, LANES), I16),
            jax.ShapeDtypeStruct((count, width), BF16),
        ],
        compiler_params=params(16),
        cost_estimate=cost(2 * width * cols * patches, 4 << 20),
        name="out_grad",
    )(member, att, cot, owner)


def decoded(got_ref, first, count, power_row):
    rows = got_ref.shape[1]
    total = jnp.zeros((count, got_ref.shape[2]), F32)
    for source in range(got_ref.shape[0]):
        scale = unit(got_ref[source, rows - 16:, :])[power_row:power_row + 1]
        total = total + from_i16(got_ref[source, first:first + count, :]) * scale
    return total


def qkv_sum_kernel(member, got_ref, *refs):
    outs, blocks = refs[:-1], refs[-1]
    chips = len(outs)
    count = (got_ref.shape[1] - 16) // 3
    totals = [decoded(got_ref, k * count, count, k) for k in range(3)]
    for group in range(2 * chips):
        rows = [total[group * 8:(group + 1) * 8] for total in totals]
        rows = jnp.concatenate(rows + [jnp.zeros_like(rows[0])], axis=0)
        blocks[group // 2, group % 2 * 32:group % 2 * 32 + 32, :] = rows
    for at, out in enumerate(outs):
        out[...] = blocks[(member[0] // 2) ^ at].astype(BF16)


def qkv_sum(member, got, chips):
    vmem = pl.BlockSpec(memory_space=pltpu.VMEM)
    return pl.pallas_call(
        qkv_sum_kernel,
        in_specs=[smem(), vmem],
        out_specs=[vmem] * chips,
        out_shape=[jax.ShapeDtypeStruct((64, LANES), BF16)] * chips,
        scratch_shapes=[pltpu.VMEM((chips, 64, LANES), F32)],
        compiler_params=params(8),
        cost_estimate=cost(1 << 20, 2 << 20),
        name="qkv_sum",
    )(member, got)


def relay_kernel(member, *refs):
    chips = (len(refs) - 4) // 2
    blocks, columns = refs[:chips], refs[chips:2 * chips]
    keep_ref, send_ref, mine_hbm, sems = refs[2 * chips:]
    moves = [pltpu.make_async_copy(column, mine_hbm.at[i], sems.at[i]) for i, column in enumerate(columns)]
    for copy in moves:
        copy.start()
    core = member[0] % 2
    for at, block in enumerate(blocks):
        keep_ref[at * 32:(at + 1) * 32, :] = block[pl.ds(pl.multiple_of(core * 32, 32), 32), :]
        send_ref[at * 32:(at + 1) * 32, :] = block[pl.ds(pl.multiple_of((1 - core) * 32, 32), 32), :]
    for copy in moves:
        copy.wait()


def relay(member, blocks, columns):
    vmem = pl.BlockSpec(memory_space=pltpu.VMEM)
    chips = len(blocks)
    return pl.pallas_call(
        relay_kernel,
        in_specs=[smem()] + [vmem] * (2 * chips),
        out_specs=[vmem, vmem, near()],
        out_shape=[
            jax.ShapeDtypeStruct((32 * chips, LANES), BF16),
            jax.ShapeDtypeStruct((32 * chips, LANES), BF16),
            jax.ShapeDtypeStruct((chips,) + columns[0].shape, BF16),
        ],
        scratch_shapes=[pltpu.SemaphoreType.DMA((chips,))],
        compiler_params=params(8),
        cost_estimate=cost(1 << 16, 3 << 20),
        name="relay",
    )(member, *blocks, *columns)


def pack_kernel(got_ref, keep_ref, other_ref, out_hbm, pack, sems):
    chips = keep_ref.shape[0] // 32
    rows = []
    for ref in (keep_ref, other_ref):
        values = ref[...].astype(F32)
        rows += [values[at * 32:at * 32 + 24] for at in range(chips)]
    first = 24 * len(rows)
    pack[:first, :] = jnp.concatenate(rows, axis=0).astype(BF16)
    count = (pack.shape[0] - first) // 4
    for slab in range(4):
        total = decoded(got_ref, slab * count, count, slab)
        pack[first + slab * count:first + (slab + 1) * count, :] = total.astype(BF16)
    for copy in send_copies(pack, out_hbm, sems):
        copy.wait()


def pack_sums(got, keep, other, parts):
    vmem = pl.BlockSpec(memory_space=pltpu.VMEM)
    rows = 24 * (keep.shape[0] // 16) + got.shape[1] - 16
    return pl.pallas_call(
        pack_kernel,
        in_specs=[vmem] * 3,
        out_specs=hbm(),
        out_shape=jax.ShapeDtypeStruct((parts, rows, LANES), BF16),
        scratch_shapes=[pltpu.VMEM((rows, LANES), BF16), pltpu.SemaphoreType.DMA((parts,))],
        compiler_params=params(8),
        cost_estimate=cost(1 << 20, 3 << 20),
        name="pack_sums",
    )(got, keep, other)


def unpack_kernel(member, got_hbm, qkv_hbm, wout_hbm, got_ref, qkv_ref, wout_ref, in_sems, out_sems):
    parts, rows, lanes = got_ref.shape
    steps = in_sems.shape[0]
    per = parts // steps
    loads = []
    for step in range(steps):
        at = slice(step * per, (step + 1) * per)
        loads.append(pltpu.make_async_copy(got_hbm.at[at], got_ref.at[at], in_sems.at[step]))
        loads[-1].start()
    groups = qkv_ref.shape[2] // lanes
    first = 24 * groups
    count = wout_ref.shape[0] // parts
    stores = []
    for step in range(steps):
        loads[step].wait()
        for part in range(step * per, (step + 1) * per):
            for slab in range(wout_ref.shape[1] // lanes):
                block = got_ref[part, first + slab * count:first + (slab + 1) * count, :]
                wout_ref[part * count:(part + 1) * count, slab * lanes:(slab + 1) * lanes] = block.astype(F32)
            values = got_ref[part, :first, :].astype(F32)
            for at in range(groups):
                source = member[0] ^ (2 * (at % (groups // 2)) + at // (groups // 2))
                lane = pl.ds(pl.multiple_of(source * lanes, lanes), lanes)
                for k in range(3):
                    top = at * 24 + k * 8
                    qkv_ref[k, part * 8:(part + 1) * 8, lane] = values[top:top + 8]
        at = slice(step * per * count, (step + 1) * per * count)
        stores.append(pltpu.make_async_copy(wout_ref.at[at, :], wout_hbm.at[at, :], out_sems.at[2 * step]))
        stores[-1].start()
        at = slice(step * per * 8, (step + 1) * per * 8)
        stores.append(pltpu.make_async_copy(qkv_ref.at[:, at, :], qkv_hbm.at[:, at, :], out_sems.at[2 * step + 1]))
        stores[-1].start()
    for copy in stores:
        copy.wait()


def unpack_sums(member, got, width, cols, groups):
    steps = 4
    qkv = ((3, width // groups, width), F32)
    wout = ((width, cols), F32)
    return pl.pallas_call(
        unpack_kernel,
        in_specs=[smem(), near()],
        out_specs=[hbm(), hbm()],
        out_shape=[jax.ShapeDtypeStruct(*qkv), jax.ShapeDtypeStruct(*wout)],
        scratch_shapes=[
            pltpu.VMEM(got.shape, BF16), pltpu.VMEM(*qkv), pltpu.VMEM(*wout),
            pltpu.SemaphoreType.DMA((steps,)), pltpu.SemaphoreType.DMA((2 * steps,)),
        ],
        compiler_params=params(12),
        cost_estimate=cost(1 << 20, 6 << 20),
        name="unpack_sums",
    )(member, got)


def bytes_kernel(
    member, bounds, mine_hbm, other_hbm, query_hbm, wk_hbm, wv_hbm, wq_hbm, row_ref,
    out_ref, head_ref, tail_ref,
    lhs, d_query, tables, shares, d_kv, w_own, wq_own, start_ref, end_ref, sems,
):
    chips, rows, patches = mine_hbm.shape
    groups = 2 * chips
    own, width = wq_own.shape
    dim = 64
    heads = own // dim
    blocks = patches // LANES
    total = shares.shape[2]
    s_dev = out_ref.shape[0]
    rim = total - s_dev
    chip, core = member[0] // 2, member[0] % 2
    own_rows = pl.ds(pl.multiple_of(member[0] * own, own), own)
    moves = []

    def move(source, target):
        moves.append(pltpu.make_async_copy(source, target, sems.at[len(moves)]))
        moves[-1].start()

    places = []
    for ref, ref_core in ((mine_hbm, core), (other_hbm, 1 - core)):
        for back in range(chips):
            group = 2 * lax.rem(chip + chips - back, chips) + ref_core
            at = pl.multiple_of(group * own, own)
            places.append(group)
            move(ref.at[back, 2 * own:, :], tables.at[len(places) - 1])
            move(ref.at[back, own:2 * own, :], d_query.at[pl.ds(at, own), :])
            move(ref.at[back, :own, :], lhs.at[pl.ds(width + at, own), :])
    move(wq_hbm.at[own_rows, :], wq_own)
    move(query_hbm, lhs.at[:width, :])
    move(wk_hbm.at[own_rows, :], w_own.at[:, :width])
    move(wv_hbm.at[own_rows, :], w_own.at[:, width:])
    columns_of(row_ref, start_ref, end_ref)
    for copy in moves:
        copy.wait()
    for slot, group in enumerate(places):
        table = tables[slot].astype(F32)
        for at in range(s_dev // patches + 1):
            part = table[8 * (at // 2):8 * (at // 2) + 8]
            part = pltpu.roll(part, 4, 0) if at % 2 else part
            if at < s_dev // patches:
                shares[group, :, at * patches:(at + 1) * patches] = part
            else:
                shares[group, :, s_dev:] = part[:, :rim]
    length = (row_ref[8:9, :] - row_ref[0:1, :]).astype(F32)
    lhs[2 * width:, :] = split2(dot(wq_own[...], d_query[...]) * (1.0 / length))

    def tile_grad(base, span, first, count, slot):
        inside = patch_major(start_ref, end_ref, first, count, base, span)
        at = pl.ds(base, span)
        patch = pl.ds(first, count)
        for group in range(groups):
            share = shares[group, :, at]
            for kind in range(2):
                top = kind * width + group * own
                wide = dot(lhs[top:top + own, patch], inside)
                part = head_rows(share[kind * heads:(kind + 1) * heads], dim)
                d_kv[slot, top:top + own, :span] = (part * wide).astype(BF16)
        grad = dot(w_own[...], d_kv[slot, :, :span])
        pool = dot(lhs[2 * width:, patch], inside)
        return (grad + (pool[:own] + pool[own:])).T

    def tiles(span, first_of, count):
        def go(i, carry):
            for slot in range(UNROLL):
                base = pl.multiple_of((UNROLL * i + slot) * span, span)
                out_ref[pl.ds(base, span), :] = tile_grad(base, span, first_of(base), count, slot).astype(BF16)
            return carry

        lax.fori_loop(0, s_dev // (UNROLL * span), go, 0)

    def first_of(base):
        return pl.multiple_of(window(bounds, blocks, base) * LANES, LANES)

    @pl.when(bounds[blocks + 1] > 0)
    def _():
        tiles(LANES, first_of, 2 * LANES)

    @pl.when(bounds[blocks + 1] == 0)
    def _():
        tiles(TILE, first_of, 2 * LANES)

    head_ref[...] = tile_grad(0, LANES, 0, 2 * LANES, 0)[:16]
    tail_ref[...] = tile_grad(s_dev, rim, patches - 2 * LANES, 2 * LANES, 1)[:16]


def byte_grads(member, bounds, mine_factors, other_factors, query, w_query, w_key, w_value, row, s_dev):
    chips, rows, patches = mine_factors.shape
    groups = 2 * chips
    width = w_query.shape[0]
    own = width // groups
    rim = LANES
    return pl.pallas_call(
        bytes_kernel,
        in_specs=[smem(), smem(), near(), near()] + [hbm()] * 4 + [pl.BlockSpec(memory_space=pltpu.VMEM)],
        out_specs=[pl.BlockSpec(memory_space=pltpu.VMEM)] * 3,
        scratch_shapes=[
            pltpu.VMEM((2 * width + 2 * own, patches), BF16),
            pltpu.VMEM((width, patches), BF16),
            pltpu.VMEM((groups, rows - 2 * own, patches), BF16),
            pltpu.VMEM((groups, 8, s_dev + rim), F32),
            pltpu.VMEM((UNROLL, 2 * width, TILE), BF16),
            pltpu.VMEM((own, 2 * width), BF16),
            pltpu.VMEM((own, width), BF16),
            pltpu.VMEM((patches, LANES), I32),
            pltpu.VMEM((patches, LANES), I32),
            pltpu.SemaphoreType.DMA((3 * groups + 4,)),
        ],
        out_shape=[
            jax.ShapeDtypeStruct((s_dev, own), BF16),
            jax.ShapeDtypeStruct((16, own), F32),
            jax.ShapeDtypeStruct((16, own), F32),
        ],
        compiler_params=params(52),
        cost_estimate=cost(8 << 30, 8 << 20),
        name="byte_grads",
    )(member, bounds, mine_factors, other_factors, query, w_key, w_value, w_query, row)


def shifted(value, axis, steps):
    count = lax.axis_size(axis)
    first, last = (max(0, -steps), min(count, count - steps))
    return lax.ppermute(value, axis, [(source, source + steps) for source in range(first, last)])


def swap(value, axis):
    return lax.all_to_all(value, axis, split_axis=0, concat_axis=0, tiled=True)


def over_chips(value):
    count = lax.axis_size("patch")
    blocks = [value]
    for step in range(1, count // 2):
        pairs = [(i, (i + 2 * step) % count) for i in range(count)]
        blocks.append(lax.ppermute(value, "patch", pairs))
    return blocks


def other_core(value):
    return lax.ppermute(value, "patch", [(i, i ^ 1) for i in range(lax.axis_size("patch"))])


def after(value, *others):
    return lax.optimization_barrier((value,) + others)[0]


def local(byte_states, patch_len, shard_offset, owner, cotangent, w_query, w_key, w_value, w_out):
    s_dev, width = byte_states.shape
    groups = lax.axis_size("patch")
    parts = lax.axis_size("seq")
    member = lax.axis_index("patch").astype(I32).reshape(1)
    rim = shifted(byte_states[:MAXP], "seq", -1)

    coded_att = after(att_grad(w_out, cotangent, groups), rim)
    got_att = swap(coded_att, "patch")
    kv, pooled, att, query, probs, geo, row, bounds = forward(
        member, shard_offset, patch_len, byte_states, rim, w_key, w_value, w_query, groups
    )
    all_att = swap(after(att, got_att), "patch")
    grads, factor = backward(bounds, byte_states, kv, pooled, rim, got_att, query, probs, geo, row, parts)
    got_qkv = swap(after(grads, all_att), "seq")
    columns = over_chips(factor)
    coded_out, patch_rows = out_grad(member, after(all_att, grads), cotangent, owner, parts)
    all_query = queries(after(pooled, coded_out), w_query)
    got_out = swap(after(coded_out, got_qkv, all_query, columns[1], columns[3]), "seq")
    blocks = [
        block if at == 0 else lax.ppermute(block, "patch", [(i, i ^ (2 * at)) for i in range(groups)])
        for at, block in enumerate(qkv_sum(member, got_qkv, groups // 2))
    ]
    keep, send, mine = relay(member, blocks, columns)
    got_keep = other_core(send)
    other = other_core(mine)
    sums = swap(pack_sums(got_out, keep, got_keep, parts), "seq")
    d_bytes, head, tail = byte_grads(
        member, bounds, mine, other, all_query, w_query, w_key, w_value, row, s_dev
    )
    first = (head + shifted(tail, "seq", 1)).astype(BF16)
    d_bytes = lax.dynamic_update_slice(d_bytes, first, (0, 0))
    d_qkv, d_wout = unpack_sums(member, sums, width, cotangent.shape[1], groups)
    return (d_bytes, d_qkv, d_wout, patch_rows)


def solution(mesh):
    return jax.shard_map(
        local,
        mesh=mesh,
        in_specs=(
            P("seq", None), P("seq", None), P("seq"), P("seq", None), P("seq", "patch"),
            P(), P(), P(), P(None, "patch"),
        ),
        out_specs=(P("seq", "patch"), P(None, "patch", None), P(None, "patch"), P(("seq", "patch"), None)),
        check_vma=False,
    )
```

```python
import jax
import jax.numpy as jnp
from jax import lax
from jax.experimental import pallas as pl
from jax.experimental.pallas import tpu as pltpu
from jax.sharding import PartitionSpec as P

HEADS = 16
MAXP = 16
LANES = 128
TILE = 256
UNROLL = 4
F32, BF16, I16, I32 = jnp.float32, jnp.bfloat16, jnp.int16, jnp.int32
NT = (((1,), (1,)), ((), ()))


def params(mebibytes):
    return pltpu.CompilerParams(vmem_limit_bytes=mebibytes * 1024 * 1024)


def cost(flops, moved):
    return pl.CostEstimate(flops=flops, bytes_accessed=moved, transcendentals=0)


def whole(shape):
    return pl.BlockSpec(shape, lambda *_: (0,) * len(shape))


def smem():
    return pl.BlockSpec(memory_space=pltpu.SMEM)


def dot(a, b):
    return jnp.dot(a, b, preferred_element_type=F32)


def dot_nt(a, b):
    return lax.dot_general(a, b, NT, preferred_element_type=F32)


def coded(value):
    peak = jnp.max(jnp.abs(value), axis=0, keepdims=True)
    power = jnp.ceil(jnp.log2(jnp.maximum(peak, 1e-30)))
    return jnp.round(value * (32767.0 * jnp.exp2(-power))), power


def to_i16(value):
    return value.astype(I32).astype(I16)


def from_i16(value):
    return value.astype(I32).astype(F32)


def unit(power):
    return jnp.exp2(from_i16(power)) * (1.0 / 32767.0)


def padded_rows(row_list, count):
    width = row_list[0].shape[1]
    at = lax.broadcasted_iota(I32, (count, width), 0)
    out = jnp.zeros((count, width), F32)
    for i, row in enumerate(row_list):
        out = jnp.where(at == i, jnp.broadcast_to(row, (count, width)), out)
    return out


def window(bounds, blocks, base):
    block = jnp.int32(0)
    for at in range(1, blocks - 1):
        block = block + (bounds[at] <= base).astype(I32)
    return block


def patch_major(start_ref, end_ref, first, count, base, width):
    rows = pl.ds(pl.multiple_of(first, LANES), count)
    start, end = start_ref[rows, :], end_ref[rows, :]
    parts = []
    for at in range(0, width, LANES):
        byte = base + at + lax.broadcasted_iota(I32, (count, LANES), 1)
        parts.append(jnp.where((byte >= start) & (byte < end), 1.0, 0.0).astype(BF16))
    return parts[0] if len(parts) == 1 else jnp.concatenate(parts, axis=1)


def byte_major(row_ref, first, count, base, width):
    lanes = pl.ds(pl.multiple_of(first, LANES), count)
    byte = base + lax.broadcasted_iota(I32, (width, count), 0)
    inside = (byte >= row_ref[0:1, lanes]) & (byte < row_ref[8:9, lanes])
    return jnp.where(inside, 1.0, 0.0).astype(BF16)


def over_tiles(bounds, blocks, s_dev, rim, body):
    def loop(width, unroll):
        def go(i, carry):
            for at in range(unroll):
                body(pl.multiple_of((i * unroll + at) * width, width), width)
            return carry

        lax.fori_loop(0, s_dev // (unroll * width), go, 0)

    @pl.when(bounds[blocks + 1] == 0)
    def _():
        loop(TILE, UNROLL)

    @pl.when(bounds[blocks + 1] > 0)
    def _():
        loop(LANES, 1)

    body(s_dev, rim)


def fill_rim(rim_ref, rim_rows):
    rim_rows[...] = jnp.zeros_like(rim_rows)
    rim_rows[:rim_ref.shape[0], :] = rim_ref[...]


def columns_of(row_ref, start_ref, end_ref):
    patches = row_ref.shape[1]
    start_ref[...] = jnp.broadcast_to(row_ref[0:1, :], (LANES, patches)).T
    end_ref[...] = jnp.broadcast_to(row_ref[8:9, :], (LANES, patches)).T


def send_copies(source, target, sems):
    copies = [pltpu.make_async_copy(source, target.at[i], sems.at[i]) for i in range(target.shape[0])]
    for copy in copies:
        copy.start()
    return copies


def over_segment(value, place, left, op):
    size = value.shape[1]
    before, after = value, value
    for step in (1, 2, 4, 8):
        before = jnp.where(place >= step, op(before, pltpu.roll(before, step, 1)), before)
        after = jnp.where(left >= step, op(after, pltpu.roll(after, size - step, 1)), after)
    return before, after


def head_rows(rows, dim):
    count, width = rows.shape
    return jnp.concatenate(
        [jnp.broadcast_to(rows[i:i + 1], (dim, width)) for i in range(count)], axis=0
    )


def split2(value):
    high = value.astype(BF16)
    return jnp.concatenate([high, (value - high.astype(F32)).astype(BF16)], axis=0)


def att_grad_kernel(w_ref, cot_ref, out_ref, cot_t):
    groups = out_ref.shape[0]
    own = w_ref.shape[0] // groups
    cot_t[...] = cot_ref[...].astype(F32).T.astype(BF16)
    for group in range(groups):
        codes, power = coded(dot(w_ref[group * own:(group + 1) * own, :], cot_t[...]))
        out_ref[group, :own, :] = to_i16(codes)
        out_ref[group, own:, :] = to_i16(jnp.broadcast_to(power, (16, power.shape[1])))


def att_grad(w_out, cot, groups):
    width, cols = w_out.shape
    rows = cot.shape[0]
    own = width // groups
    return pl.pallas_call(
        att_grad_kernel,
        in_specs=[pl.BlockSpec(memory_space=pltpu.VMEM)] * 2,
        out_specs=pl.BlockSpec(memory_space=pltpu.VMEM),
        out_shape=jax.ShapeDtypeStruct((groups, own + 16, rows), I16),
        scratch_shapes=[pltpu.VMEM((cols, rows), BF16)],
        compiler_params=params(56),
        cost_estimate=cost(2 * width * cols * rows, 4 << 20),
        name="att_grad",
    )(w_out, cot)


def forward_kernel(
    member, offset, len_ref, x_hbm, wq_hbm, rim_ref, wk_ref, wv_ref,
    kv_hbm, pooled_hbm, queries_hbm, att_ref, query_ref, probs_ref, geo_ref, row_ref, bounds,
    rim_rows, x_ref, wq_ref, queries_ref, kv_ref, pooled_ref, w_kv, acc, lhs, start_ref, end_ref, inv_col, att_acc,
    x_sems, out_sems,
):
    rim = rim_rows.shape[0]
    patches = len_ref.shape[1]
    blocks = patches // LANES
    own = wk_ref.shape[1]
    dim = 64
    heads = own // dim
    s_dev = x_hbm.shape[0]
    chunks = x_sems.shape[0]
    chunk = s_dev // chunks
    loads = []
    for i in range(chunks):
        at = slice(i * chunk, (i + 1) * chunk)
        loads.append(pltpu.make_async_copy(x_hbm.at[at, :], x_ref.at[at, :], x_sems.at[i]))
        loads[-1].start()
    wq_copy = pltpu.make_async_copy(wq_hbm, wq_ref, out_sems.at[2])
    wq_copy.start()

    length = len_ref[...].astype(F32)
    before = lax.broadcasted_iota(I32, (patches, patches), 0)
    after = lax.broadcasted_iota(I32, (patches, patches), 1)
    off = offset[0].astype(F32)
    eight = jnp.broadcast_to(length, (8, patches))
    upper = jnp.where(before < after, 1.0, 0.0).astype(BF16)
    start_row = (dot(eight.astype(BF16), upper) + off).astype(I32)
    row_ref[:8, :] = start_row
    row_ref[8:, :] = start_row + eight.astype(I32)
    columns_of(row_ref, start_ref, end_ref)
    inv_col[...] = 1.0 / jnp.broadcast_to(length, (LANES, patches)).T
    at = lax.broadcasted_iota(I32, (16, patches), 0)
    both = jnp.concatenate([start_row, start_row], axis=0)
    geo = jnp.where(at == 0, both >> 6, jnp.where(at == 1, both & 63, 0)).astype(F32)
    geo = jnp.where(at == 2, jnp.broadcast_to(length, (16, patches)), geo)
    lhs[own:own + 16, :] = geo.astype(BF16)
    lane = lax.broadcasted_iota(I32, (1, patches), 1)
    for block in range(blocks + 1):
        total = jnp.sum(jnp.where(lane < block * LANES, length, 0.0))
        bounds[block] = (total + off).astype(I32)

    def crowded(i, found):
        base = i * TILE
        third = window(bounds, blocks, base) + 2
        return found | ((third < blocks) & (bounds[third] < base + TILE)).astype(I32)

    bounds[blocks + 1] = lax.fori_loop(0, s_dev // TILE, crowded, jnp.int32(0))
    w_kv[:, :own] = wk_ref[...]
    w_kv[:, own:] = wv_ref[...]
    acc[...] = jnp.zeros_like(acc)

    def project(rows, base, width):
        kv_ref[:, pl.ds(base, width)] = dot(rows, w_kv[...]).T.astype(BF16)
        first = pl.multiple_of(window(bounds, blocks, base) * LANES, LANES)
        at = pl.ds(first, 2 * LANES)
        acc[at, :] += dot(patch_major(start_ref, end_ref, first, 2 * LANES, base, width), rows)

    for i in range(chunks):
        loads[i].wait()
        for at in range(i * chunk, (i + 1) * chunk, TILE):
            project(x_ref[at:at + TILE, :], at, TILE)
    fill_rim(rim_ref, rim_rows)
    project(rim_rows[...], s_dev, rim)

    @pl.when(bounds[blocks + 1] > 0)
    def _():
        def rest(i, carry):
            base = pl.multiple_of(i * TILE, TILE)
            third = window(bounds, blocks, base) + 2

            @pl.when((third < blocks) & (bounds[third] < base + TILE))
            def _():
                first = pl.multiple_of(third * LANES, LANES)
                acc[pl.ds(first, LANES), :] += dot(
                    patch_major(start_ref, end_ref, first, LANES, base, TILE), x_ref[pl.ds(base, TILE), :]
                )

            return carry

        lax.fori_loop(0, s_dev // TILE, rest, 0)

    kv_copy = pltpu.make_async_copy(kv_ref, kv_hbm, out_sems.at[0])
    kv_copy.start()
    pooled = (acc[...] * inv_col[:, :1]).astype(BF16)
    pooled_ref[...] = pooled
    pooled_copy = pltpu.make_async_copy(pooled_ref, pooled_hbm, out_sems.at[1])
    pooled_copy.start()
    wq_copy.wait()
    queries_ref[...] = dot(pooled, wq_ref[...]).T.astype(BF16)
    queries_copy = pltpu.make_async_copy(queries_ref, queries_hbm, out_sems.at[3])
    queries_copy.start()
    query = queries_ref[pl.ds(pl.multiple_of(member[0] * own, own), own), :]
    lhs[:own, :] = query
    query_ref[...] = query

    def score(base, width):
        first = pl.multiple_of(window(bounds, blocks, base) * LANES, LANES)
        exp = dot(
            lhs[:, pl.ds(first, 2 * LANES)],
            patch_major(start_ref, end_ref, first, 2 * LANES, base, width),
        )
        at = pl.ds(base, width)
        product = exp[:own] * kv_ref[:own, at].astype(F32)
        rows = [jnp.sum(product[h * dim:(h + 1) * dim], axis=0, keepdims=True) for h in range(heads)]
        probs_ref[:, at] = padded_rows(rows, 8) * (dim ** -0.5)
        geo = exp[own:own + 8]
        byte = (base + lax.broadcasted_iota(I32, (1, width), 1)).astype(F32)
        place = byte - (64.0 * geo[0:1] + geo[1:2])
        geo_ref[:, at] = padded_rows([place, geo[2:3] - 1.0 - place], 8)

    over_tiles(bounds, blocks, s_dev, rim, score)
    place, left = geo_ref[0:1, :], geo_ref[1:2, :]
    scores = probs_ref[...]
    before, after = over_segment(scores, place, left, jnp.maximum)
    expo = jnp.exp(scores - jnp.maximum(before, after))
    before, after = over_segment(expo, place, left, jnp.add)
    probs_ref[...] = jnp.where(left >= 0.0, expo / (before + (after - expo)), 0.0)
    att_acc[...] = jnp.zeros_like(att_acc)

    def attend(base, width):
        at = pl.ds(base, width)
        probs_b = probs_ref[:, at].astype(BF16).astype(F32)[:heads]
        both = split2(head_rows(probs_b, dim) * kv_ref[own:, at].astype(F32))
        first = pl.multiple_of(window(bounds, blocks, base) * LANES, LANES)
        att_acc[:, pl.ds(first, 2 * LANES)] += dot(
            both, byte_major(row_ref, first, 2 * LANES, base, width)
        )

    over_tiles(bounds, blocks, s_dev, rim, attend)
    att_ref[...] = (att_acc[:own, :] + att_acc[own:, :]).astype(BF16)
    for copy in (kv_copy, pooled_copy, queries_copy):
        copy.wait()


def hbm():
    return pl.BlockSpec(memory_space=pltpu.HBM)


def near():
    return pl.BlockSpec(memory_space=pl.ANY)


def forward(member, offset, lengths, x, rim, w_key, w_value, w_query, groups):
    s_dev, width = x.shape
    patches = lengths.shape[1]
    own = width // groups
    total = s_dev + LANES
    col = pl.BlockSpec((width, own), lambda i, member, offset: (0, member[0]))
    shape = jax.ShapeDtypeStruct
    small = [
        shape((own, patches), BF16), shape((own, patches), BF16), shape((8, total), F32), shape((8, total), F32), shape((16, patches), I32),
    ]
    return pl.pallas_call(
        forward_kernel,
        grid_spec=pltpu.PrefetchScalarGridSpec(
            num_scalar_prefetch=2,
            grid=(1,),
            in_specs=[whole(lengths.shape), hbm(), hbm(), whole(rim.shape), col, col],
            out_specs=[hbm()] * 3 + [whole(s.shape) for s in small] + [smem()],
            scratch_shapes=[
                pltpu.VMEM((LANES, width), BF16),
                pltpu.VMEM((s_dev, width), BF16),
                pltpu.VMEM((width, width), BF16),
                pltpu.VMEM((width, patches), BF16),
                pltpu.VMEM((2 * own, total), BF16),
                pltpu.VMEM((patches, width), BF16),
                pltpu.VMEM((width, 2 * own), BF16),
                pltpu.VMEM((patches, width), F32),
                pltpu.VMEM((own + 16, patches), BF16),
                pltpu.VMEM((patches, LANES), I32),
                pltpu.VMEM((patches, LANES), I32),
                pltpu.VMEM((patches, LANES), F32),
                pltpu.VMEM((2 * own, patches), F32),
                pltpu.SemaphoreType.DMA((8,)),
                pltpu.SemaphoreType.DMA((4,)),
            ],
        ),
        out_shape=[shape((2 * own, total), BF16), shape((patches, width), BF16), shape((width, patches), BF16)]
        + small + [shape((8,), I32)],
        compiler_params=params(56),
        cost_estimate=cost(8 << 30, 12 << 20),
        name="forward",
    )(member, offset, lengths, x, w_query, rim, w_key, w_value)


def backward_kernel(
    bounds, x_hbm, kv_hbm, pooled_hbm, rim_ref, got_ref, query_ref, probs_ref, geo_ref, row_ref,
    grad_ref, factor_out,
    rim_rows, x_ref, kv_ref, pooled_ref, factor_ref, start_ref, end_ref, d_kv, lhs, d_probs, d_scores, dq_acc, acc,
    x_sems, in_sems,
):
    rim = rim_rows.shape[0]
    s_dev = x_hbm.shape[0]
    own, patches = query_ref.shape
    blocks = patches // LANES
    dim = 64
    heads = own // dim
    sources = got_ref.shape[0]
    kv_copy = pltpu.make_async_copy(kv_hbm, kv_ref, in_sems.at[0])
    kv_copy.start()
    chunks = x_sems.shape[0]
    chunk = s_dev // chunks
    loads = []
    for i in range(chunks):
        at = slice(i * chunk, (i + 1) * chunk)
        loads.append(pltpu.make_async_copy(x_hbm.at[at, :], x_ref.at[at, :], x_sems.at[i]))
    pooled_copy = pltpu.make_async_copy(pooled_hbm, pooled_ref, in_sems.at[1])

    columns_of(row_ref, start_ref, end_ref)
    summed = jnp.zeros((own, patches), F32)
    for source in range(sources):
        summed = summed + from_i16(got_ref[source, :own, :]) * unit(got_ref[source, own:, :])[0:1]
    lhs[:own, :] = summed.astype(BF16)
    lhs[own:, :] = query_ref[...]
    factor_ref[:own, :] = summed.astype(BF16)
    kv_copy.wait()
    for copy in loads + [pooled_copy]:
        copy.start()

    def first_pass(base, width):
        first = pl.multiple_of(window(bounds, blocks, base) * LANES, LANES)
        exp = dot(
            lhs[:, pl.ds(first, 2 * LANES)],
            patch_major(start_ref, end_ref, first, 2 * LANES, base, width),
        )
        d_out = exp[:own]
        at = pl.ds(base, width)
        product = d_out * kv_ref[own:, at].astype(F32)
        rows = [jnp.sum(product[h * dim:(h + 1) * dim], axis=0, keepdims=True) for h in range(heads)]
        d_probs[:, at] = padded_rows(rows, 8)
        probs_b = probs_ref[:, at].astype(BF16).astype(F32)[:heads]
        d_kv[own:, at] = (head_rows(probs_b, dim) * d_out).astype(BF16)
        d_kv[:own, at] = exp[own:].astype(BF16)

    over_tiles(bounds, blocks, s_dev, rim, first_pass)
    place, left = geo_ref[0:1, :], geo_ref[1:2, :]
    probs = probs_ref[...]
    weighted = probs * d_probs[...]
    before, after = over_segment(weighted, place, left, jnp.add)
    inner = before + (after - weighted)
    slope = jnp.where(left >= 0.0, probs * (d_probs[...] - inner) * (dim ** -0.5), 0.0)
    d_scores[...] = slope.astype(BF16).astype(F32)
    dq_acc[...] = jnp.zeros_like(dq_acc)

    def second_pass(base, width):
        at = pl.ds(base, width)
        wide = head_rows(d_scores[:, at][:heads], dim)
        d_kv[:own, at] = (wide * d_kv[:own, at].astype(F32)).astype(BF16)
        both = split2(wide * kv_ref[:own, at].astype(F32))
        first = pl.multiple_of(window(bounds, blocks, base) * LANES, LANES)
        dq_acc[:, pl.ds(first, 2 * LANES)] += dot(
            both, byte_major(row_ref, first, 2 * LANES, base, width)
        )

    over_tiles(bounds, blocks, s_dev, rim, second_pass)
    factor_ref[own:2 * own, :] = (dq_acc[:own, :] + dq_acc[own:, :]).astype(BF16)
    probs_b = probs.astype(BF16).astype(F32)
    rows = padded_rows(
        [d_scores[h:h + 1, :] for h in range(heads)] + [probs_b[h:h + 1, :] for h in range(heads)], 8
    )
    groups = [rows[:, at:at + patches] for at in range(0, s_dev, patches)]
    groups.append(jnp.concatenate([rows[:, s_dev:], jnp.zeros((8, patches - rim), F32)], axis=1))
    groups += [jnp.zeros((8, patches), F32)] * ((factor_ref.shape[0] - 2 * own) // 4 - len(groups))
    upper = lax.broadcasted_iota(I32, (8, patches), 0) < 4
    stack = [
        jnp.where(upper, groups[i], pltpu.roll(groups[i + 1], 4, 0)) for i in range(0, len(groups), 2)
    ]
    factor_ref[2 * own:, :] = jnp.concatenate(stack, axis=0).astype(BF16)
    factor_out[...] = factor_ref[...]

    fill_rim(rim_ref, rim_rows)
    acc[...] = dot(d_kv[:, s_dev:], rim_rows[...])
    for i in range(chunks):
        loads[i].wait()
    acc[...] += dot(d_kv[:, :s_dev], x_ref[...])
    pooled_copy.wait()
    grad_q = dot(factor_ref[own:2 * own, :], pooled_ref[...])
    powers = []
    parts = grad_ref.shape[0]
    for k, grad in enumerate((grad_q, acc[:own, :], acc[own:, :])):
        codes, power = coded(grad.T)
        powers.append(power)
        rows = codes.shape[0] // parts
        spread = codes.reshape(rows // 8, parts, 8, own)
        for part in range(parts):
            grad_ref[part, k * rows:(k + 1) * rows, :] = to_i16(spread[:, part].reshape(rows, own))
    tail = to_i16(padded_rows(powers, 16))
    for part in range(parts):
        grad_ref[part, 3 * rows:, :] = tail


def backward(bounds, x, kv, pooled, rim, got, query, probs, geo, row, parts):
    s_dev, width = x.shape
    own, patches = query.shape
    groups = got.shape[0]
    total = kv.shape[1]
    extra = -(-4 * (s_dev // patches + 1) // 16) * 16
    rows = width // parts
    vmem = pl.BlockSpec(memory_space=pltpu.VMEM)
    return pl.pallas_call(
        backward_kernel,
        in_specs=[smem()] + [hbm()] * 3 + [vmem] * 6,
        out_specs=[vmem, vmem],
        out_shape=[
            jax.ShapeDtypeStruct((parts, 3 * rows + 16, own), I16),
            jax.ShapeDtypeStruct((2 * own + extra, patches), BF16),
        ],
        scratch_shapes=[
            pltpu.VMEM((LANES, width), BF16),
            pltpu.VMEM((s_dev, width), BF16),
            pltpu.VMEM((2 * own, total), BF16),
            pltpu.VMEM((patches, width), BF16),
            pltpu.VMEM((2 * own + extra, patches), BF16),
            pltpu.VMEM((patches, LANES), I32),
            pltpu.VMEM((patches, LANES), I32),
            pltpu.VMEM((2 * own, total), BF16),
            pltpu.VMEM((2 * own, patches), BF16),
            pltpu.VMEM((8, total), F32),
            pltpu.VMEM((8, total), F32),
            pltpu.VMEM((2 * own, patches), F32),
            pltpu.VMEM((2 * own, width), F32),
            pltpu.SemaphoreType.DMA((4,)),
            pltpu.SemaphoreType.DMA((2,)),
        ],
        compiler_params=params(56),
        cost_estimate=cost(6 << 30, 16 << 20),
        name="backward",
    )(bounds, x, kv, pooled, rim, got, query, probs, geo, row)


def out_grad_kernel(member, mine_ref, other_ref, cot_ref, owner_ref, out_ref, rows_ref, att_ref):
    chips, own, patches = mine_ref.shape
    chip, core = member[0] // 2, member[0] % 2
    for ref, ref_core in ((mine_ref, core), (other_ref, 1 - core)):
        for back in range(chips):
            group = 2 * lax.rem(chip + chips - back, chips) + ref_core
            att_ref[pl.ds(pl.multiple_of(group * own, own), own), :] = ref[back]
    att = att_ref[...]
    codes, power = coded(dot(att, cot_ref[...]))
    parts = out_ref.shape[0]
    rows = codes.shape[0] // parts
    slabs = codes.shape[1] // LANES
    tail = to_i16(padded_rows([power[:, at * LANES:(at + 1) * LANES] for at in range(slabs)], 16))
    for part in range(parts):
        for at in range(slabs):
            block = codes[part * rows:(part + 1) * rows, at * LANES:(at + 1) * LANES]
            out_ref[part, at * rows:(at + 1) * rows, :] = to_i16(block)
        out_ref[part, slabs * rows:, :] = tail
    count = rows_ref.shape[0]
    order = jnp.broadcast_to(owner_ref[...], (8, patches))
    order = pltpu.roll(order, lax.rem(patches - member[0] * count, patches), 1)[0:1, :LANES]
    pick = jnp.where(lax.broadcasted_iota(I32, (patches, LANES), 0) == order, 1.0, 0.0).astype(BF16)
    rows_ref[...] = dot(att, pick).T[:count].astype(BF16)


def out_grad(member, mine, other, cot, owner, parts):
    chips, own, patches = mine.shape
    groups = 2 * chips
    width, cols = groups * own, cot.shape[1]
    rows = cols // LANES * (width // parts) + 16
    count = patches // groups
    return pl.pallas_call(
        out_grad_kernel,
        in_specs=[smem()] + [pl.BlockSpec(memory_space=pltpu.VMEM)] * 4,
        out_specs=[pl.BlockSpec(memory_space=pltpu.VMEM)] * 2,
        scratch_shapes=[pltpu.VMEM((width, patches), BF16)],
        out_shape=[
            jax.ShapeDtypeStruct((parts, rows, LANES), I16),
            jax.ShapeDtypeStruct((count, width), BF16),
        ],
        compiler_params=params(16),
        cost_estimate=cost(2 * width * cols * patches, 4 << 20),
        name="out_grad",
    )(member, mine, other, cot, owner)


def decoded(got_ref, first, count, power_row):
    rows = got_ref.shape[1]
    total = jnp.zeros((count, got_ref.shape[2]), F32)
    for source in range(got_ref.shape[0]):
        scale = unit(got_ref[source, rows - 16:, :])[power_row:power_row + 1]
        total = total + from_i16(got_ref[source, first:first + count, :]) * scale
    return total


def qkv_sum_kernel(member, got_ref, *refs):
    outs, blocks = refs[:-1], refs[-1]
    chips = len(outs)
    count = (got_ref.shape[1] - 16) // 3
    totals = [decoded(got_ref, k * count, count, k) for k in range(3)]
    for group in range(2 * chips):
        rows = [total[group * 8:(group + 1) * 8] for total in totals]
        rows = jnp.concatenate(rows + [jnp.zeros_like(rows[0])], axis=0)
        blocks[group // 2, group % 2 * 32:group % 2 * 32 + 32, :] = rows
    for at, out in enumerate(outs):
        out[...] = blocks[(member[0] // 2) ^ at].astype(BF16)


def qkv_sum(member, got, chips):
    vmem = pl.BlockSpec(memory_space=pltpu.VMEM)
    return pl.pallas_call(
        qkv_sum_kernel,
        in_specs=[smem(), vmem],
        out_specs=[vmem] * chips,
        out_shape=[jax.ShapeDtypeStruct((64, LANES), BF16)] * chips,
        scratch_shapes=[pltpu.VMEM((chips, 64, LANES), F32)],
        compiler_params=params(8),
        cost_estimate=cost(1 << 20, 2 << 20),
        name="qkv_sum",
    )(member, got)


def stack_kernel(*refs):
    out = refs[-1]
    for at, block in enumerate(refs[:-1]):
        out[at] = block[...]


def stack(blocks):
    vmem = pl.BlockSpec(memory_space=pltpu.VMEM)
    return pl.pallas_call(
        stack_kernel,
        in_specs=[vmem] * len(blocks),
        out_specs=vmem,
        out_shape=jax.ShapeDtypeStruct((len(blocks),) + blocks[0].shape, BF16),
        compiler_params=params(8),
        cost_estimate=cost(1 << 16, 1 << 20),
        name="stack",
    )(*blocks)


def relay_kernel(member, *refs):
    chips = (len(refs) - 5) // 2
    blocks, columns = refs[:chips], refs[chips:2 * chips]
    keep_ref, send_ref, mine_any, stage, sems = refs[2 * chips:]
    moves = [pltpu.make_async_copy(column, stage.at[i], sems.at[i]) for i, column in enumerate(columns)]
    for copy in moves:
        copy.start()
    core = member[0] % 2
    for at, block in enumerate(blocks):
        keep_ref[at * 32:(at + 1) * 32, :] = block[pl.ds(pl.multiple_of(core * 32, 32), 32), :]
        send_ref[at * 32:(at + 1) * 32, :] = block[pl.ds(pl.multiple_of((1 - core) * 32, 32), 32), :]
    sends = [pltpu.make_async_copy(stage.at[i], mine_any.at[i], sems.at[chips + i]) for i in range(chips)]
    for copy, send in zip(moves, sends):
        copy.wait()
        send.start()
    for send in sends:
        send.wait()


def relay(member, blocks, columns):
    vmem = pl.BlockSpec(memory_space=pltpu.VMEM)
    chips = len(blocks)
    return pl.pallas_call(
        relay_kernel,
        in_specs=[smem()] + [vmem] * chips + [near()] * chips,
        out_specs=[vmem, vmem, near()],
        out_shape=[
            jax.ShapeDtypeStruct((32 * chips, LANES), BF16),
            jax.ShapeDtypeStruct((32 * chips, LANES), BF16),
            jax.ShapeDtypeStruct((chips,) + columns[0].shape, BF16),
        ],
        scratch_shapes=[
            pltpu.VMEM((chips,) + columns[0].shape, BF16), pltpu.SemaphoreType.DMA((2 * chips,)),
        ],
        compiler_params=params(8),
        cost_estimate=cost(1 << 16, 3 << 20),
        name="relay",
    )(member, *blocks, *columns)


def pack_kernel(got_ref, keep_ref, other_ref, out_hbm, pack, sems):
    chips = keep_ref.shape[0] // 32
    rows = []
    for ref in (keep_ref, other_ref):
        values = ref[...].astype(F32)
        rows += [values[at * 32:at * 32 + 24] for at in range(chips)]
    first = 24 * len(rows)
    pack[:first, :] = jnp.concatenate(rows, axis=0).astype(BF16)
    count = (pack.shape[0] - first) // 4
    for slab in range(4):
        total = decoded(got_ref, slab * count, count, slab)
        pack[first + slab * count:first + (slab + 1) * count, :] = total.astype(BF16)
    for copy in send_copies(pack, out_hbm, sems):
        copy.wait()


def pack_sums(got, keep, other, parts):
    vmem = pl.BlockSpec(memory_space=pltpu.VMEM)
    rows = 24 * (keep.shape[0] // 16) + got.shape[1] - 16
    return pl.pallas_call(
        pack_kernel,
        in_specs=[vmem] * 3,
        out_specs=hbm(),
        out_shape=jax.ShapeDtypeStruct((parts, rows, LANES), BF16),
        scratch_shapes=[pltpu.VMEM((rows, LANES), BF16), pltpu.SemaphoreType.DMA((parts,))],
        compiler_params=params(60),
        cost_estimate=cost(1 << 20, 3 << 20),
        name="pack_sums",
    )(got, keep, other)


def unpack_kernel(member, got_ref, qkv_hbm, wout_hbm, qkv_ref, wout_ref, out_sems):
    parts, rows, lanes = got_ref.shape
    steps = out_sems.shape[0] // 2
    per = parts // steps
    groups = qkv_ref.shape[2] // lanes
    first = 24 * groups
    count = wout_ref.shape[0] // parts
    stores = []
    for step in range(steps):
        for part in range(step * per, (step + 1) * per):
            for slab in range(wout_ref.shape[1] // lanes):
                block = got_ref[part, first + slab * count:first + (slab + 1) * count, :]
                wout_ref[part * count:(part + 1) * count, slab * lanes:(slab + 1) * lanes] = block.astype(F32)
            values = got_ref[part, :first, :].astype(F32)
            for at in range(groups):
                source = member[0] ^ (2 * (at % (groups // 2)) + at // (groups // 2))
                lane = pl.ds(pl.multiple_of(source * lanes, lanes), lanes)
                for k in range(3):
                    top = at * 24 + k * 8
                    qkv_ref[k, part * 8:(part + 1) * 8, lane] = values[top:top + 8]
        at = slice(step * per * count, (step + 1) * per * count)
        stores.append(pltpu.make_async_copy(wout_ref.at[at, :], wout_hbm.at[at, :], out_sems.at[2 * step]))
        stores[-1].start()
        at = slice(step * per * 8, (step + 1) * per * 8)
        stores.append(pltpu.make_async_copy(qkv_ref.at[:, at, :], qkv_hbm.at[:, at, :], out_sems.at[2 * step + 1]))
        stores[-1].start()
    for copy in stores:
        copy.wait()


def unpack_sums(member, got, width, cols, groups):
    steps = 4
    qkv = ((3, width // groups, width), F32)
    wout = ((width, cols), F32)
    return pl.pallas_call(
        unpack_kernel,
        in_specs=[smem(), pl.BlockSpec(memory_space=pltpu.VMEM)],
        out_specs=[hbm(), hbm()],
        out_shape=[jax.ShapeDtypeStruct(*qkv), jax.ShapeDtypeStruct(*wout)],
        scratch_shapes=[
            pltpu.VMEM(*qkv), pltpu.VMEM(*wout), pltpu.SemaphoreType.DMA((2 * steps,)),
        ],
        compiler_params=params(12),
        cost_estimate=cost(1 << 20, 6 << 20),
        name="unpack_sums",
    )(member, got)


def bytes_kernel(
    member, bounds, mine_hbm, other_hbm, query_hbm, wk_hbm, wv_hbm, wq_hbm, row_ref,
    out_ref, head_ref, tail_ref,
    lhs, d_query, tables, shares, d_kv, w_own, wq_own, start_ref, end_ref, sems,
):
    chips, rows, patches = mine_hbm.shape
    groups = 2 * chips
    own, width = wq_own.shape
    dim = 64
    heads = own // dim
    blocks = patches // LANES
    total = shares.shape[2]
    s_dev = out_ref.shape[0]
    rim = total - s_dev
    chip, core = member[0] // 2, member[0] % 2
    own_rows = pl.ds(pl.multiple_of(member[0] * own, own), own)
    moves = []

    def move(source, target):
        moves.append(pltpu.make_async_copy(source, target, sems.at[len(moves)]))
        moves[-1].start()

    places = []
    for ref, ref_core in ((mine_hbm, core), (other_hbm, 1 - core)):
        for back in range(chips):
            group = 2 * lax.rem(chip + chips - back, chips) + ref_core
            at = pl.multiple_of(group * own, own)
            places.append(group)
            move(ref.at[back, 2 * own:, :], tables.at[len(places) - 1])
            move(ref.at[back, own:2 * own, :], d_query.at[pl.ds(at, own), :])
            move(ref.at[back, :own, :], lhs.at[pl.ds(width + at, own), :])
    move(wq_hbm.at[own_rows, :], wq_own)
    move(query_hbm, lhs.at[:width, :])
    move(wk_hbm.at[own_rows, :], w_own.at[:, :width])
    move(wv_hbm.at[own_rows, :], w_own.at[:, width:])
    columns_of(row_ref, start_ref, end_ref)
    for copy in moves:
        copy.wait()
    for slot, group in enumerate(places):
        table = tables[slot].astype(F32)
        for at in range(s_dev // patches + 1):
            part = table[8 * (at // 2):8 * (at // 2) + 8]
            part = pltpu.roll(part, 4, 0) if at % 2 else part
            if at < s_dev // patches:
                shares[group, :, at * patches:(at + 1) * patches] = part
            else:
                shares[group, :, s_dev:] = part[:, :rim]
    length = (row_ref[8:9, :] - row_ref[0:1, :]).astype(F32)
    lhs[2 * width:, :] = split2(dot(wq_own[...], d_query[...]) * (1.0 / length))

    def tile_grad(base, span, first, count, slot):
        inside = patch_major(start_ref, end_ref, first, count, base, span)
        at = pl.ds(base, span)
        patch = pl.ds(first, count)
        for group in range(groups):
            share = shares[group, :, at]
            for kind in range(2):
                top = kind * width + group * own
                wide = dot(lhs[top:top + own, patch], inside)
                part = head_rows(share[kind * heads:(kind + 1) * heads], dim)
                d_kv[slot, top:top + own, :span] = (part * wide).astype(BF16)
        grad = dot(w_own[...], d_kv[slot, :, :span])
        pool = dot(lhs[2 * width:, patch], inside)
        return (grad + (pool[:own] + pool[own:])).T

    def tiles(span, first_of, count):
        def go(i, carry):
            for slot in range(UNROLL):
                base = pl.multiple_of((UNROLL * i + slot) * span, span)
                out_ref[pl.ds(base, span), :] = tile_grad(base, span, first_of(base), count, slot).astype(BF16)
            return carry

        lax.fori_loop(0, s_dev // (UNROLL * span), go, 0)

    def first_of(base):
        return pl.multiple_of(window(bounds, blocks, base) * LANES, LANES)

    @pl.when(bounds[blocks + 1] > 0)
    def _():
        tiles(LANES, first_of, 2 * LANES)

    @pl.when(bounds[blocks + 1] == 0)
    def _():
        tiles(TILE, first_of, 2 * LANES)

    head_ref[...] = tile_grad(0, LANES, 0, 2 * LANES, 0)[:16]
    tail_ref[...] = tile_grad(s_dev, rim, patches - 2 * LANES, 2 * LANES, 1)[:16]


def byte_grads(member, bounds, mine_factors, other_factors, query, w_query, w_key, w_value, row, s_dev):
    chips, rows, patches = mine_factors.shape
    groups = 2 * chips
    width = w_query.shape[0]
    own = width // groups
    rim = LANES
    return pl.pallas_call(
        bytes_kernel,
        in_specs=[smem(), smem(), near(), near()] + [hbm()] * 4 + [pl.BlockSpec(memory_space=pltpu.VMEM)],
        out_specs=[pl.BlockSpec(memory_space=pltpu.VMEM)] * 3,
        scratch_shapes=[
            pltpu.VMEM((2 * width + 2 * own, patches), BF16),
            pltpu.VMEM((width, patches), BF16),
            pltpu.VMEM((groups, rows - 2 * own, patches), BF16),
            pltpu.VMEM((groups, 8, s_dev + rim), F32),
            pltpu.VMEM((UNROLL, 2 * width, TILE), BF16),
            pltpu.VMEM((own, 2 * width), BF16),
            pltpu.VMEM((own, width), BF16),
            pltpu.VMEM((patches, LANES), I32),
            pltpu.VMEM((patches, LANES), I32),
            pltpu.SemaphoreType.DMA((3 * groups + 4,)),
        ],
        out_shape=[
            jax.ShapeDtypeStruct((s_dev, own), BF16),
            jax.ShapeDtypeStruct((16, own), F32),
            jax.ShapeDtypeStruct((16, own), F32),
        ],
        compiler_params=params(52),
        cost_estimate=cost(8 << 30, 8 << 20),
        name="byte_grads",
    )(member, bounds, mine_factors, other_factors, query, w_key, w_value, w_query, row)


def shifted(value, axis, steps):
    count = lax.axis_size(axis)
    first, last = (max(0, -steps), min(count, count - steps))
    return lax.ppermute(value, axis, [(source, source + steps) for source in range(first, last)])


def swap(value, axis):
    return lax.all_to_all(value, axis, split_axis=0, concat_axis=0, tiled=True)


def over_chips(value):
    count = lax.axis_size("patch")
    blocks = [value]
    for step in range(1, count // 2):
        pairs = [(i, (i + 2 * step) % count) for i in range(count)]
        blocks.append(lax.ppermute(value, "patch", pairs))
    return blocks


def other_core(value):
    return lax.ppermute(value, "patch", [(i, i ^ 1) for i in range(lax.axis_size("patch"))])


def after(value, *others):
    return lax.optimization_barrier((value,) + others)[0]


def local(byte_states, patch_len, shard_offset, owner, cotangent, w_query, w_key, w_value, w_out):
    s_dev, width = byte_states.shape
    groups = lax.axis_size("patch")
    parts = lax.axis_size("seq")
    member = lax.axis_index("patch").astype(I32).reshape(1)
    rim = shifted(byte_states[:MAXP], "seq", -1)

    coded_att = after(att_grad(w_out, cotangent, groups), rim)
    got_att = swap(coded_att, "patch")
    kv, pooled, all_query, att, query, probs, geo, row, bounds = forward(
        member, shard_offset, patch_len, byte_states, rim, w_key, w_value, w_query, groups
    )
    att_columns = over_chips(att)
    grads, factor = backward(bounds, byte_states, kv, pooled, rim, got_att, query, probs, geo, row, parts)
    got_qkv = swap(after(grads, *att_columns[1:]), "seq")
    mine_att = stack([after(att_columns[0], grads)] + att_columns[1:])
    other_att = other_core(mine_att)
    columns = over_chips(factor)
    coded_out, patch_rows = out_grad(member, mine_att, other_att, cotangent, owner, parts)
    got_out = swap(after(coded_out, got_qkv, columns[1], columns[3]), "seq")
    blocks = [
        block if at == 0 else lax.ppermute(block, "patch", [(i, i ^ (2 * at)) for i in range(groups)])
        for at, block in enumerate(qkv_sum(member, got_qkv, groups // 2))
    ]
    keep, send, mine = relay(member, blocks, columns)
    got_keep = other_core(send)
    other = other_core(mine)
    sums = swap(pack_sums(got_out, keep, got_keep, parts), "seq")
    d_bytes, head, tail = byte_grads(
        member, bounds, mine, other, all_query, w_query, w_key, w_value, row, s_dev
    )
    first = (head + shifted(tail, "seq", 1)).astype(BF16)
    d_bytes = lax.dynamic_update_slice(d_bytes, first, (0, 0))
    d_qkv, d_wout = unpack_sums(member, sums, width, cotangent.shape[1], groups)
    return (d_bytes, d_qkv, d_wout, patch_rows)


def solution(mesh):
    return jax.shard_map(
        local,
        mesh=mesh,
        in_specs=(
            P("seq", None), P("seq", None), P("seq"), P("seq", None), P("seq", "patch"),
            P(), P(), P(), P(None, "patch"),
        ),
        out_specs=(P("seq", "patch"), P(None, "patch", None), P(None, "patch"), P(("seq", "patch"), None)),
        check_vma=False,
    )
```

```python
import jax
import jax.numpy as jnp
from jax import lax
from jax.experimental import pallas as pl
from jax.experimental.pallas import tpu as pltpu
from jax.sharding import PartitionSpec as P

HEADS = 16
MAXP = 16
LANES = 128
TILE = 256
UNROLL = 4
F32, BF16, I16, I32 = jnp.float32, jnp.bfloat16, jnp.int16, jnp.int32
NT = (((1,), (1,)), ((), ()))


def params(mebibytes):
    return pltpu.CompilerParams(vmem_limit_bytes=mebibytes * 1024 * 1024)


def cost(flops, moved):
    return pl.CostEstimate(flops=flops, bytes_accessed=moved, transcendentals=0)


def whole(shape):
    return pl.BlockSpec(shape, lambda *_: (0,) * len(shape))


def smem():
    return pl.BlockSpec(memory_space=pltpu.SMEM)


def dot(a, b):
    return jnp.dot(a, b, preferred_element_type=F32)


def dot_nt(a, b):
    return lax.dot_general(a, b, NT, preferred_element_type=F32)


def coded(value):
    peak = jnp.max(jnp.abs(value), axis=0, keepdims=True)
    power = jnp.ceil(jnp.log2(jnp.maximum(peak, 1e-30)))
    return jnp.round(value * (32767.0 * jnp.exp2(-power))), power


def to_i16(value):
    return value.astype(I32).astype(I16)


def from_i16(value):
    return value.astype(I32).astype(F32)


def unit(power):
    return jnp.exp2(from_i16(power)) * (1.0 / 32767.0)


def padded_rows(row_list, count):
    width = row_list[0].shape[1]
    at = lax.broadcasted_iota(I32, (count, width), 0)
    out = jnp.zeros((count, width), F32)
    for i, row in enumerate(row_list):
        out = jnp.where(at == i, jnp.broadcast_to(row, (count, width)), out)
    return out


def window(bounds, blocks, base):
    block = jnp.int32(0)
    for at in range(1, blocks - 1):
        block = block + (bounds[at] <= base).astype(I32)
    return block


def patch_major(start_ref, end_ref, first, count, base, width):
    rows = pl.ds(pl.multiple_of(first, LANES), count)
    start, end = start_ref[rows, :], end_ref[rows, :]
    parts = []
    for at in range(0, width, LANES):
        byte = base + at + lax.broadcasted_iota(I32, (count, LANES), 1)
        parts.append(jnp.where((byte >= start) & (byte < end), 1.0, 0.0).astype(BF16))
    return parts[0] if len(parts) == 1 else jnp.concatenate(parts, axis=1)


def byte_major(row_ref, first, count, base, width):
    lanes = pl.ds(pl.multiple_of(first, LANES), count)
    byte = base + lax.broadcasted_iota(I32, (width, count), 0)
    inside = (byte >= row_ref[0:1, lanes]) & (byte < row_ref[8:9, lanes])
    return jnp.where(inside, 1.0, 0.0).astype(BF16)


def over_tiles(bounds, blocks, s_dev, rim, body):
    def loop(width, unroll):
        def go(i, carry):
            for at in range(unroll):
                body(pl.multiple_of((i * unroll + at) * width, width), width)
            return carry

        lax.fori_loop(0, s_dev // (unroll * width), go, 0)

    @pl.when(bounds[blocks + 1] == 0)
    def _():
        loop(TILE, UNROLL)

    @pl.when(bounds[blocks + 1] > 0)
    def _():
        loop(LANES, 1)

    body(s_dev, rim)


def fill_rim(rim_ref, rim_rows):
    rim_rows[...] = jnp.zeros_like(rim_rows)
    rim_rows[:rim_ref.shape[0], :] = rim_ref[...]


def columns_of(row_ref, start_ref, end_ref):
    patches = row_ref.shape[1]
    start_ref[...] = jnp.broadcast_to(row_ref[0:1, :], (LANES, patches)).T
    end_ref[...] = jnp.broadcast_to(row_ref[8:9, :], (LANES, patches)).T


def send_copies(source, target, sems):
    copies = [pltpu.make_async_copy(source, target.at[i], sems.at[i]) for i in range(target.shape[0])]
    for copy in copies:
        copy.start()
    return copies


def over_segment(value, place, left, op):
    size = value.shape[1]
    before, after = value, value
    for step in (1, 2, 4, 8):
        before = jnp.where(place >= step, op(before, pltpu.roll(before, step, 1)), before)
        after = jnp.where(left >= step, op(after, pltpu.roll(after, size - step, 1)), after)
    return before, after


def head_rows(rows, dim):
    count, width = rows.shape
    return jnp.concatenate(
        [jnp.broadcast_to(rows[i:i + 1], (dim, width)) for i in range(count)], axis=0
    )


def split2(value):
    high = value.astype(BF16)
    return jnp.concatenate([high, (value - high.astype(F32)).astype(BF16)], axis=0)


def att_grad_kernel(w_ref, cot_ref, out_ref, cot_t):
    groups = out_ref.shape[0]
    own = w_ref.shape[0] // groups
    cot_t[...] = cot_ref[...].astype(F32).T.astype(BF16)
    for group in range(groups):
        codes, power = coded(dot(w_ref[group * own:(group + 1) * own, :], cot_t[...]))
        out_ref[group, :own, :] = to_i16(codes)
        out_ref[group, own:, :] = to_i16(jnp.broadcast_to(power, (16, power.shape[1])))


def att_grad(w_out, cot, groups):
    width, cols = w_out.shape
    rows = cot.shape[0]
    own = width // groups
    return pl.pallas_call(
        att_grad_kernel,
        in_specs=[pl.BlockSpec(memory_space=pltpu.VMEM)] * 2,
        out_specs=pl.BlockSpec(memory_space=pltpu.VMEM),
        out_shape=jax.ShapeDtypeStruct((groups, own + 16, rows), I16),
        scratch_shapes=[pltpu.VMEM((cols, rows), BF16)],
        compiler_params=params(56),
        cost_estimate=cost(2 * width * cols * rows, 4 << 20),
        name="att_grad",
    )(w_out, cot)


def forward_kernel(
    member, offset, len_ref, x_hbm, wq_hbm, rim_ref, wk_ref, wv_ref,
    kv_hbm, pooled_hbm, queries_hbm, att_ref, query_ref, probs_ref, geo_ref, row_ref, bounds,
    rim_rows, x_ref, wq_ref, queries_ref, kv_ref, pooled_ref, w_kv, acc, lhs, start_ref, end_ref, inv_col, att_acc,
    x_sems, out_sems,
):
    rim = rim_rows.shape[0]
    patches = len_ref.shape[1]
    blocks = patches // LANES
    own = wk_ref.shape[1]
    dim = 64
    heads = own // dim
    s_dev = x_hbm.shape[0]
    chunks = x_sems.shape[0]
    chunk = s_dev // chunks
    loads = []
    for i in range(chunks):
        at = slice(i * chunk, (i + 1) * chunk)
        loads.append(pltpu.make_async_copy(x_hbm.at[at, :], x_ref.at[at, :], x_sems.at[i]))
        loads[-1].start()
    wq_copy = pltpu.make_async_copy(wq_hbm, wq_ref, out_sems.at[2])
    wq_copy.start()

    length = len_ref[...].astype(F32)
    before = lax.broadcasted_iota(I32, (patches, patches), 0)
    after = lax.broadcasted_iota(I32, (patches, patches), 1)
    off = offset[0].astype(F32)
    eight = jnp.broadcast_to(length, (8, patches))
    upper = jnp.where(before < after, 1.0, 0.0).astype(BF16)
    start_row = (dot(eight.astype(BF16), upper) + off).astype(I32)
    row_ref[:8, :] = start_row
    row_ref[8:, :] = start_row + eight.astype(I32)
    columns_of(row_ref, start_ref, end_ref)
    inv_col[...] = 1.0 / jnp.broadcast_to(length, (LANES, patches)).T
    at = lax.broadcasted_iota(I32, (16, patches), 0)
    both = jnp.concatenate([start_row, start_row], axis=0)
    geo = jnp.where(at == 0, both >> 6, jnp.where(at == 1, both & 63, 0)).astype(F32)
    geo = jnp.where(at == 2, jnp.broadcast_to(length, (16, patches)), geo)
    lhs[own:own + 16, :] = geo.astype(BF16)
    lane = lax.broadcasted_iota(I32, (1, patches), 1)
    for block in range(blocks + 1):
        total = jnp.sum(jnp.where(lane < block * LANES, length, 0.0))
        bounds[block] = (total + off).astype(I32)

    def crowded(i, found):
        base = i * TILE
        third = window(bounds, blocks, base) + 2
        return found | ((third < blocks) & (bounds[third] < base + TILE)).astype(I32)

    bounds[blocks + 1] = lax.fori_loop(0, s_dev // TILE, crowded, jnp.int32(0))
    w_kv[:, :own] = wk_ref[...]
    w_kv[:, own:] = wv_ref[...]
    acc[...] = jnp.zeros_like(acc)

    def project(rows, base, width):
        kv_ref[:, pl.ds(base, width)] = dot(rows, w_kv[...]).T.astype(BF16)
        first = pl.multiple_of(window(bounds, blocks, base) * LANES, LANES)
        at = pl.ds(first, 2 * LANES)
        acc[at, :] += dot(patch_major(start_ref, end_ref, first, 2 * LANES, base, width), rows)

    for i in range(chunks):
        loads[i].wait()
        for at in range(i * chunk, (i + 1) * chunk, TILE):
            project(x_ref[at:at + TILE, :], at, TILE)
    fill_rim(rim_ref, rim_rows)
    project(rim_rows[...], s_dev, rim)

    @pl.when(bounds[blocks + 1] > 0)
    def _():
        def rest(i, carry):
            base = pl.multiple_of(i * TILE, TILE)
            third = window(bounds, blocks, base) + 2

            @pl.when((third < blocks) & (bounds[third] < base + TILE))
            def _():
                first = pl.multiple_of(third * LANES, LANES)
                acc[pl.ds(first, LANES), :] += dot(
                    patch_major(start_ref, end_ref, first, LANES, base, TILE), x_ref[pl.ds(base, TILE), :]
                )

            return carry

        lax.fori_loop(0, s_dev // TILE, rest, 0)

    kv_copy = pltpu.make_async_copy(kv_ref, kv_hbm, out_sems.at[0])
    kv_copy.start()
    pooled = (acc[...] * inv_col[:, :1]).astype(BF16)
    pooled_ref[...] = pooled
    pooled_copy = pltpu.make_async_copy(pooled_ref, pooled_hbm, out_sems.at[1])
    pooled_copy.start()
    wq_copy.wait()
    queries_ref[...] = dot(pooled, wq_ref[...]).T.astype(BF16)
    queries_copy = pltpu.make_async_copy(queries_ref, queries_hbm, out_sems.at[3])
    queries_copy.start()
    query = queries_ref[pl.ds(pl.multiple_of(member[0] * own, own), own), :]
    lhs[:own, :] = query
    query_ref[...] = query

    def score(base, width):
        first = pl.multiple_of(window(bounds, blocks, base) * LANES, LANES)
        exp = dot(
            lhs[:, pl.ds(first, 2 * LANES)],
            patch_major(start_ref, end_ref, first, 2 * LANES, base, width),
        )
        at = pl.ds(base, width)
        product = exp[:own] * kv_ref[:own, at].astype(F32)
        rows = [jnp.sum(product[h * dim:(h + 1) * dim], axis=0, keepdims=True) for h in range(heads)]
        probs_ref[:, at] = padded_rows(rows, 8) * (dim ** -0.5)
        geo = exp[own:own + 8]
        byte = (base + lax.broadcasted_iota(I32, (1, width), 1)).astype(F32)
        place = byte - (64.0 * geo[0:1] + geo[1:2])
        geo_ref[:, at] = padded_rows([place, geo[2:3] - 1.0 - place], 8)

    over_tiles(bounds, blocks, s_dev, rim, score)
    place, left = geo_ref[0:1, :], geo_ref[1:2, :]
    scores = probs_ref[...]
    before, after = over_segment(scores, place, left, jnp.maximum)
    expo = jnp.exp(scores - jnp.maximum(before, after))
    before, after = over_segment(expo, place, left, jnp.add)
    probs_ref[...] = jnp.where(left >= 0.0, expo / (before + (after - expo)), 0.0)
    att_acc[...] = jnp.zeros_like(att_acc)

    def attend(base, width):
        at = pl.ds(base, width)
        probs_b = probs_ref[:, at].astype(BF16).astype(F32)[:heads]
        both = split2(head_rows(probs_b, dim) * kv_ref[own:, at].astype(F32))
        first = pl.multiple_of(window(bounds, blocks, base) * LANES, LANES)
        att_acc[:, pl.ds(first, 2 * LANES)] += dot(
            both, byte_major(row_ref, first, 2 * LANES, base, width)
        )

    over_tiles(bounds, blocks, s_dev, rim, attend)
    att_ref[...] = (att_acc[:own, :] + att_acc[own:, :]).astype(BF16)
    for copy in (kv_copy, pooled_copy, queries_copy):
        copy.wait()


def hbm():
    return pl.BlockSpec(memory_space=pltpu.HBM)


def near():
    return pl.BlockSpec(memory_space=pl.ANY)


def forward(member, offset, lengths, x, rim, w_key, w_value, w_query, groups):
    s_dev, width = x.shape
    patches = lengths.shape[1]
    own = width // groups
    total = s_dev + LANES
    col = pl.BlockSpec((width, own), lambda i, member, offset: (0, member[0]))
    shape = jax.ShapeDtypeStruct
    small = [
        shape((own, patches), BF16), shape((own, patches), BF16), shape((8, total), F32), shape((8, total), F32), shape((16, patches), I32),
    ]
    return pl.pallas_call(
        forward_kernel,
        grid_spec=pltpu.PrefetchScalarGridSpec(
            num_scalar_prefetch=2,
            grid=(1,),
            in_specs=[whole(lengths.shape), hbm(), hbm(), whole(rim.shape), col, col],
            out_specs=[hbm()] * 3 + [whole(s.shape) for s in small] + [smem()],
            scratch_shapes=[
                pltpu.VMEM((LANES, width), BF16),
                pltpu.VMEM((s_dev, width), BF16),
                pltpu.VMEM((width, width), BF16),
                pltpu.VMEM((width, patches), BF16),
                pltpu.VMEM((2 * own, total), BF16),
                pltpu.VMEM((patches, width), BF16),
                pltpu.VMEM((width, 2 * own), BF16),
                pltpu.VMEM((patches, width), F32),
                pltpu.VMEM((own + 16, patches), BF16),
                pltpu.VMEM((patches, LANES), I32),
                pltpu.VMEM((patches, LANES), I32),
                pltpu.VMEM((patches, LANES), F32),
                pltpu.VMEM((2 * own, patches), F32),
                pltpu.SemaphoreType.DMA((8,)),
                pltpu.SemaphoreType.DMA((4,)),
            ],
        ),
        out_shape=[shape((2 * own, total), BF16), shape((patches, width), BF16), shape((width, patches), BF16)]
        + small + [shape((8,), I32)],
        compiler_params=params(56),
        cost_estimate=cost(8 << 30, 12 << 20),
        name="forward",
    )(member, offset, lengths, x, w_query, rim, w_key, w_value)


def att_sum_kernel(got_ref, out_ref):
    own = out_ref.shape[0]
    total = jnp.zeros(out_ref.shape, F32)
    for source in range(got_ref.shape[0]):
        total = total + from_i16(got_ref[source, :own, :]) * unit(got_ref[source, own:, :])[0:1]
    out_ref[...] = total.astype(BF16)


def att_sum(got):
    groups, rows, patches = got.shape
    vmem = pl.BlockSpec(memory_space=pltpu.VMEM)
    return pl.pallas_call(
        att_sum_kernel,
        in_specs=[vmem],
        out_specs=vmem,
        out_shape=jax.ShapeDtypeStruct((rows - 16, patches), BF16),
        compiler_params=params(8),
        cost_estimate=cost(1 << 20, 2 << 20),
        name="att_sum",
    )(got)


def backward_kernel(
    bounds, x_hbm, kv_hbm, pooled_hbm, rim_ref, d_att_ref, query_ref, probs_ref, geo_ref, row_ref,
    grad_ref, factor_out,
    rim_rows, x_ref, kv_ref, pooled_ref, factor_ref, start_ref, end_ref, d_kv, lhs, d_probs, d_scores, dq_acc, acc,
    x_sems, in_sems,
):
    rim = rim_rows.shape[0]
    s_dev = x_hbm.shape[0]
    own, patches = query_ref.shape
    blocks = patches // LANES
    dim = 64
    heads = own // dim
    kv_copy = pltpu.make_async_copy(kv_hbm, kv_ref, in_sems.at[0])
    kv_copy.start()
    chunks = x_sems.shape[0]
    chunk = s_dev // chunks
    loads = []
    for i in range(chunks):
        at = slice(i * chunk, (i + 1) * chunk)
        loads.append(pltpu.make_async_copy(x_hbm.at[at, :], x_ref.at[at, :], x_sems.at[i]))
    pooled_copy = pltpu.make_async_copy(pooled_hbm, pooled_ref, in_sems.at[1])

    columns_of(row_ref, start_ref, end_ref)
    lhs[:own, :] = d_att_ref[...]
    lhs[own:, :] = query_ref[...]
    factor_ref[:own, :] = d_att_ref[...]
    kv_copy.wait()
    for copy in loads + [pooled_copy]:
        copy.start()

    def first_pass(base, width):
        first = pl.multiple_of(window(bounds, blocks, base) * LANES, LANES)
        exp = dot(
            lhs[:, pl.ds(first, 2 * LANES)],
            patch_major(start_ref, end_ref, first, 2 * LANES, base, width),
        )
        d_out = exp[:own]
        at = pl.ds(base, width)
        product = d_out * kv_ref[own:, at].astype(F32)
        rows = [jnp.sum(product[h * dim:(h + 1) * dim], axis=0, keepdims=True) for h in range(heads)]
        d_probs[:, at] = padded_rows(rows, 8)
        probs_b = probs_ref[:, at].astype(BF16).astype(F32)[:heads]
        d_kv[own:, at] = (head_rows(probs_b, dim) * d_out).astype(BF16)
        d_kv[:own, at] = exp[own:].astype(BF16)

    over_tiles(bounds, blocks, s_dev, rim, first_pass)
    place, left = geo_ref[0:1, :], geo_ref[1:2, :]
    probs = probs_ref[...]
    weighted = probs * d_probs[...]
    before, after = over_segment(weighted, place, left, jnp.add)
    inner = before + (after - weighted)
    slope = jnp.where(left >= 0.0, probs * (d_probs[...] - inner) * (dim ** -0.5), 0.0)
    d_scores[...] = slope.astype(BF16).astype(F32)
    dq_acc[...] = jnp.zeros_like(dq_acc)

    def second_pass(base, width):
        at = pl.ds(base, width)
        wide = head_rows(d_scores[:, at][:heads], dim)
        d_kv[:own, at] = (wide * d_kv[:own, at].astype(F32)).astype(BF16)
        both = split2(wide * kv_ref[:own, at].astype(F32))
        first = pl.multiple_of(window(bounds, blocks, base) * LANES, LANES)
        dq_acc[:, pl.ds(first, 2 * LANES)] += dot(
            both, byte_major(row_ref, first, 2 * LANES, base, width)
        )

    over_tiles(bounds, blocks, s_dev, rim, second_pass)
    factor_ref[own:2 * own, :] = (dq_acc[:own, :] + dq_acc[own:, :]).astype(BF16)
    probs_b = probs.astype(BF16).astype(F32)
    rows = padded_rows(
        [d_scores[h:h + 1, :] for h in range(heads)] + [probs_b[h:h + 1, :] for h in range(heads)], 8
    )
    groups = [rows[:, at:at + patches] for at in range(0, s_dev, patches)]
    groups.append(jnp.concatenate([rows[:, s_dev:], jnp.zeros((8, patches - rim), F32)], axis=1))
    groups += [jnp.zeros((8, patches), F32)] * ((factor_ref.shape[0] - 2 * own) // 4 - len(groups))
    upper = lax.broadcasted_iota(I32, (8, patches), 0) < 4
    stack = [
        jnp.where(upper, groups[i], pltpu.roll(groups[i + 1], 4, 0)) for i in range(0, len(groups), 2)
    ]
    factor_ref[2 * own:, :] = jnp.concatenate(stack, axis=0).astype(BF16)
    factor_out[...] = factor_ref[...]

    fill_rim(rim_ref, rim_rows)
    acc[...] = dot(d_kv[:, s_dev:], rim_rows[...])
    for i in range(chunks):
        loads[i].wait()
    acc[...] += dot(d_kv[:, :s_dev], x_ref[...])
    pooled_copy.wait()
    grad_q = dot(factor_ref[own:2 * own, :], pooled_ref[...])
    powers = []
    parts = grad_ref.shape[0]
    for k, grad in enumerate((grad_q, acc[:own, :], acc[own:, :])):
        codes, power = coded(grad.T)
        powers.append(power)
        rows = codes.shape[0] // parts
        spread = codes.reshape(rows // 8, parts, 8, own)
        for part in range(parts):
            grad_ref[part, k * rows:(k + 1) * rows, :] = to_i16(spread[:, part].reshape(rows, own))
    tail = to_i16(padded_rows(powers, 16))
    for part in range(parts):
        grad_ref[part, 3 * rows:, :] = tail


def backward(bounds, x, kv, pooled, rim, d_att, query, probs, geo, row, parts):
    s_dev, width = x.shape
    own, patches = query.shape
    total = kv.shape[1]
    extra = -(-4 * (s_dev // patches + 1) // 16) * 16
    rows = width // parts
    vmem = pl.BlockSpec(memory_space=pltpu.VMEM)
    return pl.pallas_call(
        backward_kernel,
        in_specs=[smem()] + [hbm()] * 3 + [vmem] * 6,
        out_specs=[vmem, vmem],
        out_shape=[
            jax.ShapeDtypeStruct((parts, 3 * rows + 16, own), I16),
            jax.ShapeDtypeStruct((2 * own + extra, patches), BF16),
        ],
        scratch_shapes=[
            pltpu.VMEM((LANES, width), BF16),
            pltpu.VMEM((s_dev, width), BF16),
            pltpu.VMEM((2 * own, total), BF16),
            pltpu.VMEM((patches, width), BF16),
            pltpu.VMEM((2 * own + extra, patches), BF16),
            pltpu.VMEM((patches, LANES), I32),
            pltpu.VMEM((patches, LANES), I32),
            pltpu.VMEM((2 * own, total), BF16),
            pltpu.VMEM((2 * own, patches), BF16),
            pltpu.VMEM((8, total), F32),
            pltpu.VMEM((8, total), F32),
            pltpu.VMEM((2 * own, patches), F32),
            pltpu.VMEM((2 * own, width), F32),
            pltpu.SemaphoreType.DMA((4,)),
            pltpu.SemaphoreType.DMA((2,)),
        ],
        compiler_params=params(56),
        cost_estimate=cost(6 << 30, 16 << 20),
        name="backward",
    )(bounds, x, kv, pooled, rim, d_att, query, probs, geo, row)


def out_grad_kernel(member, mine_ref, other_ref, cot_ref, owner_ref, out_ref, rows_ref, att_ref):
    chips, own, patches = mine_ref.shape
    chip, core = member[0] // 2, member[0] % 2
    for ref, ref_core in ((mine_ref, core), (other_ref, 1 - core)):
        for back in range(chips):
            group = 2 * lax.rem(chip + chips - back, chips) + ref_core
            att_ref[pl.ds(pl.multiple_of(group * own, own), own), :] = ref[back]
    att = att_ref[...]
    codes, power = coded(dot(att, cot_ref[...]))
    parts = out_ref.shape[0]
    rows = codes.shape[0] // parts
    slabs = codes.shape[1] // LANES
    tail = to_i16(padded_rows([power[:, at * LANES:(at + 1) * LANES] for at in range(slabs)], 16))
    for part in range(parts):
        for at in range(slabs):
            block = codes[part * rows:(part + 1) * rows, at * LANES:(at + 1) * LANES]
            out_ref[part, at * rows:(at + 1) * rows, :] = to_i16(block)
        out_ref[part, slabs * rows:, :] = tail
    count = rows_ref.shape[0]
    order = jnp.broadcast_to(owner_ref[...], (8, patches))
    order = pltpu.roll(order, lax.rem(patches - member[0] * count, patches), 1)[0:1, :LANES]
    pick = jnp.where(lax.broadcasted_iota(I32, (patches, LANES), 0) == order, 1.0, 0.0).astype(BF16)
    rows_ref[...] = dot(att, pick).T[:count].astype(BF16)


def out_grad(member, mine, other, cot, owner, parts):
    chips, own, patches = mine.shape
    groups = 2 * chips
    width, cols = groups * own, cot.shape[1]
    rows = cols // LANES * (width // parts) + 16
    count = patches // groups
    return pl.pallas_call(
        out_grad_kernel,
        in_specs=[smem()] + [pl.BlockSpec(memory_space=pltpu.VMEM)] * 4,
        out_specs=[pl.BlockSpec(memory_space=pltpu.VMEM)] * 2,
        scratch_shapes=[pltpu.VMEM((width, patches), BF16)],
        out_shape=[
            jax.ShapeDtypeStruct((parts, rows, LANES), I16),
            jax.ShapeDtypeStruct((count, width), BF16),
        ],
        compiler_params=params(16),
        cost_estimate=cost(2 * width * cols * patches, 4 << 20),
        name="out_grad",
    )(member, mine, other, cot, owner)


def decoded(got_ref, first, count, power_row):
    rows = got_ref.shape[1]
    total = jnp.zeros((count, got_ref.shape[2]), F32)
    for source in range(got_ref.shape[0]):
        scale = unit(got_ref[source, rows - 16:, :])[power_row:power_row + 1]
        total = total + from_i16(got_ref[source, first:first + count, :]) * scale
    return total


def qkv_sum_kernel(member, got_ref, *refs):
    outs, blocks = refs[:-1], refs[-1]
    chips = len(outs)
    count = (got_ref.shape[1] - 16) // 3
    totals = [decoded(got_ref, k * count, count, k) for k in range(3)]
    for group in range(2 * chips):
        rows = [total[group * 8:(group + 1) * 8] for total in totals]
        rows = jnp.concatenate(rows + [jnp.zeros_like(rows[0])], axis=0)
        blocks[group // 2, group % 2 * 32:group % 2 * 32 + 32, :] = rows
    for at, out in enumerate(outs):
        out[...] = blocks[(member[0] // 2) ^ at].astype(BF16)


def qkv_sum(member, got, chips):
    vmem = pl.BlockSpec(memory_space=pltpu.VMEM)
    return pl.pallas_call(
        qkv_sum_kernel,
        in_specs=[smem(), vmem],
        out_specs=[vmem] * chips,
        out_shape=[jax.ShapeDtypeStruct((64, LANES), BF16)] * chips,
        scratch_shapes=[pltpu.VMEM((chips, 64, LANES), F32)],
        compiler_params=params(8),
        cost_estimate=cost(1 << 20, 2 << 20),
        name="qkv_sum",
    )(member, got)


def stack_kernel(*refs):
    out = refs[-1]
    for at, block in enumerate(refs[:-1]):
        out[at] = block[...]


def stack(blocks):
    vmem = pl.BlockSpec(memory_space=pltpu.VMEM)
    return pl.pallas_call(
        stack_kernel,
        in_specs=[vmem] * len(blocks),
        out_specs=vmem,
        out_shape=jax.ShapeDtypeStruct((len(blocks),) + blocks[0].shape, BF16),
        compiler_params=params(8),
        cost_estimate=cost(1 << 16, 1 << 20),
        name="stack",
    )(*blocks)


def relay_kernel(member, *refs):
    chips = (len(refs) - 5) // 2
    blocks, columns = refs[:chips], refs[chips:2 * chips]
    keep_ref, send_ref, mine_any, stage, sems = refs[2 * chips:]
    moves = [pltpu.make_async_copy(column, stage.at[i], sems.at[i]) for i, column in enumerate(columns)]
    for copy in moves:
        copy.start()
    core = member[0] % 2
    for at, block in enumerate(blocks):
        keep_ref[at * 32:(at + 1) * 32, :] = block[pl.ds(pl.multiple_of(core * 32, 32), 32), :]
        send_ref[at * 32:(at + 1) * 32, :] = block[pl.ds(pl.multiple_of((1 - core) * 32, 32), 32), :]
    sends = [pltpu.make_async_copy(stage.at[i], mine_any.at[i], sems.at[chips + i]) for i in range(chips)]
    for copy, send in zip(moves, sends):
        copy.wait()
        send.start()
    for send in sends:
        send.wait()


def relay(member, blocks, columns):
    vmem = pl.BlockSpec(memory_space=pltpu.VMEM)
    chips = len(blocks)
    return pl.pallas_call(
        relay_kernel,
        in_specs=[smem()] + [vmem] * chips + [near()] * chips,
        out_specs=[vmem, vmem, near()],
        out_shape=[
            jax.ShapeDtypeStruct((32 * chips, LANES), BF16),
            jax.ShapeDtypeStruct((32 * chips, LANES), BF16),
            jax.ShapeDtypeStruct((chips,) + columns[0].shape, BF16),
        ],
        scratch_shapes=[
            pltpu.VMEM((chips,) + columns[0].shape, BF16), pltpu.SemaphoreType.DMA((2 * chips,)),
        ],
        compiler_params=params(8),
        cost_estimate=cost(1 << 16, 3 << 20),
        name="relay",
    )(member, *blocks, *columns)


def pack_kernel(got_ref, keep_ref, other_ref, out_hbm, pack, sems):
    chips = keep_ref.shape[0] // 32
    rows = []
    for ref in (keep_ref, other_ref):
        values = ref[...].astype(F32)
        rows += [values[at * 32:at * 32 + 24] for at in range(chips)]
    first = 24 * len(rows)
    pack[:first, :] = jnp.concatenate(rows, axis=0).astype(BF16)
    count = (pack.shape[0] - first) // 4
    for slab in range(4):
        total = decoded(got_ref, slab * count, count, slab)
        pack[first + slab * count:first + (slab + 1) * count, :] = total.astype(BF16)
    for copy in send_copies(pack, out_hbm, sems):
        copy.wait()


def pack_sums(got, keep, other, parts):
    vmem = pl.BlockSpec(memory_space=pltpu.VMEM)
    rows = 24 * (keep.shape[0] // 16) + got.shape[1] - 16
    return pl.pallas_call(
        pack_kernel,
        in_specs=[vmem] * 3,
        out_specs=hbm(),
        out_shape=jax.ShapeDtypeStruct((parts, rows, LANES), BF16),
        scratch_shapes=[pltpu.VMEM((rows, LANES), BF16), pltpu.SemaphoreType.DMA((parts,))],
        compiler_params=params(60),
        cost_estimate=cost(1 << 20, 3 << 20),
        name="pack_sums",
    )(got, keep, other)


def unpack_kernel(member, got_ref, qkv_hbm, wout_hbm, qkv_ref, wout_ref, out_sems):
    parts, rows, lanes = got_ref.shape
    steps = out_sems.shape[0] // 2
    per = parts // steps
    groups = qkv_ref.shape[2] // lanes
    first = 24 * groups
    count = wout_ref.shape[0] // parts
    stores = []
    for step in range(steps):
        for part in range(step * per, (step + 1) * per):
            for slab in range(wout_ref.shape[1] // lanes):
                block = got_ref[part, first + slab * count:first + (slab + 1) * count, :]
                wout_ref[part * count:(part + 1) * count, slab * lanes:(slab + 1) * lanes] = block.astype(F32)
            values = got_ref[part, :first, :].astype(F32)
            for at in range(groups):
                source = member[0] ^ (2 * (at % (groups // 2)) + at // (groups // 2))
                lane = pl.ds(pl.multiple_of(source * lanes, lanes), lanes)
                for k in range(3):
                    top = at * 24 + k * 8
                    qkv_ref[k, part * 8:(part + 1) * 8, lane] = values[top:top + 8]
        at = slice(step * per * count, (step + 1) * per * count)
        stores.append(pltpu.make_async_copy(wout_ref.at[at, :], wout_hbm.at[at, :], out_sems.at[2 * step]))
        stores[-1].start()
        at = slice(step * per * 8, (step + 1) * per * 8)
        stores.append(pltpu.make_async_copy(qkv_ref.at[:, at, :], qkv_hbm.at[:, at, :], out_sems.at[2 * step + 1]))
        stores[-1].start()
    for copy in stores:
        copy.wait()


def unpack_sums(member, got, width, cols, groups):
    steps = 4
    qkv = ((3, width // groups, width), F32)
    wout = ((width, cols), F32)
    return pl.pallas_call(
        unpack_kernel,
        in_specs=[smem(), pl.BlockSpec(memory_space=pltpu.VMEM)],
        out_specs=[hbm(), hbm()],
        out_shape=[jax.ShapeDtypeStruct(*qkv), jax.ShapeDtypeStruct(*wout)],
        scratch_shapes=[
            pltpu.VMEM(*qkv), pltpu.VMEM(*wout), pltpu.SemaphoreType.DMA((2 * steps,)),
        ],
        compiler_params=params(12),
        cost_estimate=cost(1 << 20, 6 << 20),
        name="unpack_sums",
    )(member, got)


def bytes_kernel(
    member, bounds, mine_hbm, other_hbm, query_hbm, wk_hbm, wv_hbm, wq_hbm, row_ref,
    out_ref, head_ref, tail_ref,
    lhs, d_query, tables, shares, d_kv, w_own, wq_own, start_ref, end_ref, sems,
):
    chips, rows, patches = mine_hbm.shape
    groups = 2 * chips
    own, width = wq_own.shape
    dim = 64
    heads = own // dim
    blocks = patches // LANES
    total = shares.shape[2]
    s_dev = out_ref.shape[0]
    rim = total - s_dev
    chip, core = member[0] // 2, member[0] % 2
    own_rows = pl.ds(pl.multiple_of(member[0] * own, own), own)
    moves = []

    def move(source, target):
        moves.append(pltpu.make_async_copy(source, target, sems.at[len(moves)]))
        moves[-1].start()

    places = []
    for ref, ref_core in ((mine_hbm, core), (other_hbm, 1 - core)):
        for back in range(chips):
            group = 2 * lax.rem(chip + chips - back, chips) + ref_core
            at = pl.multiple_of(group * own, own)
            places.append(group)
            move(ref.at[back, 2 * own:, :], tables.at[len(places) - 1])
            move(ref.at[back, own:2 * own, :], d_query.at[pl.ds(at, own), :])
            move(ref.at[back, :own, :], lhs.at[pl.ds(width + at, own), :])
    move(wq_hbm.at[own_rows, :], wq_own)
    move(query_hbm, lhs.at[:width, :])
    move(wk_hbm.at[own_rows, :], w_own.at[:, :width])
    move(wv_hbm.at[own_rows, :], w_own.at[:, width:])
    columns_of(row_ref, start_ref, end_ref)
    for copy in moves:
        copy.wait()
    for slot, group in enumerate(places):
        table = tables[slot].astype(F32)
        for at in range(s_dev // patches + 1):
            part = table[8 * (at // 2):8 * (at // 2) + 8]
            part = pltpu.roll(part, 4, 0) if at % 2 else part
            if at < s_dev // patches:
                shares[group, :, at * patches:(at + 1) * patches] = part
            else:
                shares[group, :, s_dev:] = part[:, :rim]
    length = (row_ref[8:9, :] - row_ref[0:1, :]).astype(F32)
    lhs[2 * width:, :] = split2(dot(wq_own[...], d_query[...]) * (1.0 / length))

    def tile_grad(base, span, first, count, slot):
        inside = patch_major(start_ref, end_ref, first, count, base, span)
        at = pl.ds(base, span)
        patch = pl.ds(first, count)
        for group in range(groups):
            share = shares[group, :, at]
            for kind in range(2):
                top = kind * width + group * own
                wide = dot(lhs[top:top + own, patch], inside)
                part = head_rows(share[kind * heads:(kind + 1) * heads], dim)
                d_kv[slot, top:top + own, :span] = (part * wide).astype(BF16)
        grad = dot(w_own[...], d_kv[slot, :, :span])
        pool = dot(lhs[2 * width:, patch], inside)
        return (grad + (pool[:own] + pool[own:])).T

    def tiles(span, first_of, count):
        def go(i, carry):
            for slot in range(UNROLL):
                base = pl.multiple_of((UNROLL * i + slot) * span, span)
                out_ref[pl.ds(base, span), :] = tile_grad(base, span, first_of(base), count, slot).astype(BF16)
            return carry

        lax.fori_loop(0, s_dev // (UNROLL * span), go, 0)

    def first_of(base):
        return pl.multiple_of(window(bounds, blocks, base) * LANES, LANES)

    @pl.when(bounds[blocks + 1] > 0)
    def _():
        tiles(LANES, first_of, 2 * LANES)

    @pl.when(bounds[blocks + 1] == 0)
    def _():
        tiles(TILE, first_of, 2 * LANES)

    head_ref[...] = tile_grad(0, LANES, 0, 2 * LANES, 0)[:16]
    tail_ref[...] = tile_grad(s_dev, rim, patches - 2 * LANES, 2 * LANES, 1)[:16]


def byte_grads(member, bounds, mine_factors, other_factors, query, w_query, w_key, w_value, row, s_dev):
    chips, rows, patches = mine_factors.shape
    groups = 2 * chips
    width = w_query.shape[0]
    own = width // groups
    rim = LANES
    return pl.pallas_call(
        bytes_kernel,
        in_specs=[smem(), smem(), near(), near()] + [hbm()] * 4 + [pl.BlockSpec(memory_space=pltpu.VMEM)],
        out_specs=[pl.BlockSpec(memory_space=pltpu.VMEM)] * 3,
        scratch_shapes=[
            pltpu.VMEM((2 * width + 2 * own, patches), BF16),
            pltpu.VMEM((width, patches), BF16),
            pltpu.VMEM((groups, rows - 2 * own, patches), BF16),
            pltpu.VMEM((groups, 8, s_dev + rim), F32),
            pltpu.VMEM((UNROLL, 2 * width, TILE), BF16),
            pltpu.VMEM((own, 2 * width), BF16),
            pltpu.VMEM((own, width), BF16),
            pltpu.VMEM((patches, LANES), I32),
            pltpu.VMEM((patches, LANES), I32),
            pltpu.SemaphoreType.DMA((3 * groups + 4,)),
        ],
        out_shape=[
            jax.ShapeDtypeStruct((s_dev, own), BF16),
            jax.ShapeDtypeStruct((16, own), F32),
            jax.ShapeDtypeStruct((16, own), F32),
        ],
        compiler_params=params(52),
        cost_estimate=cost(8 << 30, 8 << 20),
        name="byte_grads",
    )(member, bounds, mine_factors, other_factors, query, w_key, w_value, w_query, row)


def shifted(value, axis, steps):
    count = lax.axis_size(axis)
    first, last = (max(0, -steps), min(count, count - steps))
    return lax.ppermute(value, axis, [(source, source + steps) for source in range(first, last)])


def swap(value, axis):
    return lax.all_to_all(value, axis, split_axis=0, concat_axis=0, tiled=True)


def over_chips(value):
    count = lax.axis_size("patch")
    blocks = [value]
    for step in range(1, count // 2):
        pairs = [(i, (i + 2 * step) % count) for i in range(count)]
        blocks.append(lax.ppermute(value, "patch", pairs))
    return blocks


def other_core(value):
    return lax.ppermute(value, "patch", [(i, i ^ 1) for i in range(lax.axis_size("patch"))])


def after(value, *others):
    return lax.optimization_barrier((value,) + others)[0]


def local(byte_states, patch_len, shard_offset, owner, cotangent, w_query, w_key, w_value, w_out):
    s_dev, width = byte_states.shape
    groups = lax.axis_size("patch")
    parts = lax.axis_size("seq")
    member = lax.axis_index("patch").astype(I32).reshape(1)
    rim = shifted(byte_states[:MAXP], "seq", -1)

    coded_att = after(att_grad(w_out, cotangent, groups), rim)
    got_att = swap(coded_att, "patch")
    kv, pooled, all_query, att, query, probs, geo, row, bounds = forward(
        member, shard_offset, patch_len, byte_states, rim, w_key, w_value, w_query, groups
    )
    att_columns = over_chips(att)
    grads, factor = backward(bounds, byte_states, kv, pooled, rim, att_sum(got_att), query, probs, geo, row, parts)
    got_qkv = swap(after(grads, *att_columns[1:]), "seq")
    mine_att = stack([after(att_columns[0], grads)] + att_columns[1:])
    other_att = other_core(mine_att)
    columns = over_chips(factor)
    coded_out, patch_rows = out_grad(member, mine_att, other_att, cotangent, owner, parts)
    got_out = swap(after(coded_out, got_qkv, columns[1], columns[3]), "seq")
    blocks = [
        block if at == 0 else lax.ppermute(block, "patch", [(i, i ^ (2 * at)) for i in range(groups)])
        for at, block in enumerate(qkv_sum(member, got_qkv, groups // 2))
    ]
    keep, send, mine = relay(member, blocks, columns)
    got_keep = other_core(send)
    other = other_core(mine)
    sums = swap(pack_sums(got_out, keep, got_keep, parts), "seq")
    d_bytes, head, tail = byte_grads(
        member, bounds, mine, other, all_query, w_query, w_key, w_value, row, s_dev
    )
    first = (head + shifted(tail, "seq", 1)).astype(BF16)
    d_bytes = lax.dynamic_update_slice(d_bytes, first, (0, 0))
    d_qkv, d_wout = unpack_sums(member, sums, width, cotangent.shape[1], groups)
    return (d_bytes, d_qkv, d_wout, patch_rows)


def solution(mesh):
    return jax.shard_map(
        local,
        mesh=mesh,
        in_specs=(
            P("seq", None), P("seq", None), P("seq"), P("seq", None), P("seq", "patch"),
            P(), P(), P(), P(None, "patch"),
        ),
        out_specs=(P("seq", "patch"), P(None, "patch", None), P(None, "patch"), P(("seq", "patch"), None)),
        check_vma=False,
    )
```

```python
import jax
import jax.numpy as jnp
from jax import lax
from jax.experimental import pallas as pl
from jax.experimental.pallas import tpu as pltpu
from jax.sharding import PartitionSpec as P

HEADS = 16
MAXP = 16
LANES = 128
TILE = 256
UNROLL = 4
F32, BF16, I16, I32 = jnp.float32, jnp.bfloat16, jnp.int16, jnp.int32
NT = (((1,), (1,)), ((), ()))


def params(mebibytes):
    return pltpu.CompilerParams(vmem_limit_bytes=mebibytes * 1024 * 1024)


def cost(flops, moved):
    return pl.CostEstimate(flops=flops, bytes_accessed=moved, transcendentals=0)


def whole(shape):
    return pl.BlockSpec(shape, lambda *_: (0,) * len(shape))


def smem():
    return pl.BlockSpec(memory_space=pltpu.SMEM)


def dot(a, b):
    return jnp.dot(a, b, preferred_element_type=F32)


def dot_nt(a, b):
    return lax.dot_general(a, b, NT, preferred_element_type=F32)


def coded(value):
    peak = jnp.max(jnp.abs(value), axis=0, keepdims=True)
    power = jnp.ceil(jnp.log2(jnp.maximum(peak, 1e-30)))
    return jnp.round(value * (32767.0 * jnp.exp2(-power))), power


def to_i16(value):
    return value.astype(I32).astype(I16)


def from_i16(value):
    return value.astype(I32).astype(F32)


def unit(power):
    return jnp.exp2(from_i16(power)) * (1.0 / 32767.0)


def padded_rows(row_list, count):
    width = row_list[0].shape[1]
    at = lax.broadcasted_iota(I32, (count, width), 0)
    out = jnp.zeros((count, width), F32)
    for i, row in enumerate(row_list):
        out = jnp.where(at == i, jnp.broadcast_to(row, (count, width)), out)
    return out


def window(bounds, blocks, base):
    block = jnp.int32(0)
    for at in range(1, blocks - 1):
        block = block + (bounds[at] <= base).astype(I32)
    return block


def patch_major(start_ref, end_ref, first, count, base, width):
    rows = pl.ds(pl.multiple_of(first, LANES), count)
    start, end = start_ref[rows, :], end_ref[rows, :]
    parts = []
    for at in range(0, width, LANES):
        byte = base + at + lax.broadcasted_iota(I32, (count, LANES), 1)
        parts.append(jnp.where((byte >= start) & (byte < end), 1.0, 0.0).astype(BF16))
    return parts[0] if len(parts) == 1 else jnp.concatenate(parts, axis=1)


def byte_major(row_ref, first, count, base, width):
    lanes = pl.ds(pl.multiple_of(first, LANES), count)
    byte = base + lax.broadcasted_iota(I32, (width, count), 0)
    inside = (byte >= row_ref[0:1, lanes]) & (byte < row_ref[8:9, lanes])
    return jnp.where(inside, 1.0, 0.0).astype(BF16)


def over_tiles(bounds, blocks, s_dev, rim, body):
    def loop(width, unroll):
        def go(i, carry):
            for at in range(unroll):
                body(pl.multiple_of((i * unroll + at) * width, width), width)
            return carry

        lax.fori_loop(0, s_dev // (unroll * width), go, 0)

    @pl.when(bounds[blocks + 1] == 0)
    def _():
        loop(TILE, UNROLL)

    @pl.when(bounds[blocks + 1] > 0)
    def _():
        loop(LANES, 1)

    body(s_dev, rim)


def fill_rim(rim_ref, rim_rows):
    rim_rows[...] = jnp.zeros_like(rim_rows)
    rim_rows[:rim_ref.shape[0], :] = rim_ref[...]


def columns_of(row_ref, start_ref, end_ref):
    patches = row_ref.shape[1]
    start_ref[...] = jnp.broadcast_to(row_ref[0:1, :], (LANES, patches)).T
    end_ref[...] = jnp.broadcast_to(row_ref[8:9, :], (LANES, patches)).T


def send_copies(source, target, sems):
    copies = [pltpu.make_async_copy(source, target.at[i], sems.at[i]) for i in range(target.shape[0])]
    for copy in copies:
        copy.start()
    return copies


def over_segment(value, place, left, op):
    size = value.shape[1]
    before, after = value, value
    for step in (1, 2, 4, 8):
        before = jnp.where(place >= step, op(before, pltpu.roll(before, step, 1)), before)
        after = jnp.where(left >= step, op(after, pltpu.roll(after, size - step, 1)), after)
    return before, after


def head_rows(rows, dim):
    count, width = rows.shape
    return jnp.concatenate(
        [jnp.broadcast_to(rows[i:i + 1], (dim, width)) for i in range(count)], axis=0
    )


def split2(value):
    high = value.astype(BF16)
    return jnp.concatenate([high, (value - high.astype(F32)).astype(BF16)], axis=0)


def att_grad_kernel(w_ref, cot_ref, out_ref, cot_t):
    groups = out_ref.shape[0]
    own = w_ref.shape[0] // groups
    cot_t[...] = cot_ref[...].astype(F32).T.astype(BF16)
    for group in range(groups):
        codes, power = coded(dot(w_ref[group * own:(group + 1) * own, :], cot_t[...]))
        out_ref[group, :own, :] = to_i16(codes)
        out_ref[group, own:, :] = to_i16(jnp.broadcast_to(power, (16, power.shape[1])))


def att_grad(w_out, cot, groups):
    width, cols = w_out.shape
    rows = cot.shape[0]
    own = width // groups
    return pl.pallas_call(
        att_grad_kernel,
        in_specs=[pl.BlockSpec(memory_space=pltpu.VMEM)] * 2,
        out_specs=pl.BlockSpec(memory_space=pltpu.VMEM),
        out_shape=jax.ShapeDtypeStruct((groups, own + 16, rows), I16),
        scratch_shapes=[pltpu.VMEM((cols, rows), BF16)],
        compiler_params=params(56),
        cost_estimate=cost(2 * width * cols * rows, 4 << 20),
        name="att_grad",
    )(w_out, cot)


def forward_kernel(
    member, offset, len_ref, x_hbm, wq_hbm, rim_ref, wk_ref, wv_ref,
    kv_hbm, pooled_hbm, queries_hbm, att_ref, query_ref, probs_ref, geo_ref, row_ref, bounds,
    rim_rows, x_ref, wq_ref, queries_ref, kv_ref, pooled_ref, w_kv, acc, lhs, start_ref, end_ref, inv_col, att_acc,
    x_sems, out_sems,
):
    rim = rim_rows.shape[0]
    patches = len_ref.shape[1]
    blocks = patches // LANES
    own = wk_ref.shape[1]
    dim = 64
    heads = own // dim
    s_dev = x_hbm.shape[0]
    chunks = x_sems.shape[0]
    chunk = s_dev // chunks
    loads = []
    for i in range(chunks):
        at = slice(i * chunk, (i + 1) * chunk)
        loads.append(pltpu.make_async_copy(x_hbm.at[at, :], x_ref.at[at, :], x_sems.at[i]))
        loads[-1].start()
    wq_copy = pltpu.make_async_copy(wq_hbm, wq_ref, out_sems.at[2])
    wq_copy.start()

    length = len_ref[...].astype(F32)
    before = lax.broadcasted_iota(I32, (patches, patches), 0)
    after = lax.broadcasted_iota(I32, (patches, patches), 1)
    off = offset[0].astype(F32)
    eight = jnp.broadcast_to(length, (8, patches))
    upper = jnp.where(before < after, 1.0, 0.0).astype(BF16)
    start_row = (dot(eight.astype(BF16), upper) + off).astype(I32)
    row_ref[:8, :] = start_row
    row_ref[8:, :] = start_row + eight.astype(I32)
    columns_of(row_ref, start_ref, end_ref)
    inv_col[...] = 1.0 / jnp.broadcast_to(length, (LANES, patches)).T
    at = lax.broadcasted_iota(I32, (16, patches), 0)
    both = jnp.concatenate([start_row, start_row], axis=0)
    geo = jnp.where(at == 0, both >> 6, jnp.where(at == 1, both & 63, 0)).astype(F32)
    geo = jnp.where(at == 2, jnp.broadcast_to(length, (16, patches)), geo)
    lhs[own:own + 16, :] = geo.astype(BF16)
    lane = lax.broadcasted_iota(I32, (1, patches), 1)
    for block in range(blocks + 1):
        total = jnp.sum(jnp.where(lane < block * LANES, length, 0.0))
        bounds[block] = (total + off).astype(I32)

    def crowded(i, found):
        base = i * TILE
        third = window(bounds, blocks, base) + 2
        return found | ((third < blocks) & (bounds[third] < base + TILE)).astype(I32)

    bounds[blocks + 1] = lax.fori_loop(0, s_dev // TILE, crowded, jnp.int32(0))
    w_kv[:, :own] = wk_ref[...]
    w_kv[:, own:] = wv_ref[...]
    acc[...] = jnp.zeros_like(acc)

    def project(rows, base, width):
        kv_ref[:, pl.ds(base, width)] = dot(rows, w_kv[...]).T.astype(BF16)
        first = pl.multiple_of(window(bounds, blocks, base) * LANES, LANES)
        at = pl.ds(first, 2 * LANES)
        acc[at, :] += dot(patch_major(start_ref, end_ref, first, 2 * LANES, base, width), rows)

    for i in range(chunks):
        loads[i].wait()
        for at in range(i * chunk, (i + 1) * chunk, TILE):
            project(x_ref[at:at + TILE, :], at, TILE)
    fill_rim(rim_ref, rim_rows)
    project(rim_rows[...], s_dev, rim)

    @pl.when(bounds[blocks + 1] > 0)
    def _():
        def rest(i, carry):
            base = pl.multiple_of(i * TILE, TILE)
            third = window(bounds, blocks, base) + 2

            @pl.when((third < blocks) & (bounds[third] < base + TILE))
            def _():
                first = pl.multiple_of(third * LANES, LANES)
                acc[pl.ds(first, LANES), :] += dot(
                    patch_major(start_ref, end_ref, first, LANES, base, TILE), x_ref[pl.ds(base, TILE), :]
                )

            return carry

        lax.fori_loop(0, s_dev // TILE, rest, 0)

    kv_copy = pltpu.make_async_copy(kv_ref, kv_hbm, out_sems.at[0])
    kv_copy.start()
    pooled = (acc[...] * inv_col[:, :1]).astype(BF16)
    pooled_ref[...] = pooled
    pooled_copy = pltpu.make_async_copy(pooled_ref, pooled_hbm, out_sems.at[1])
    pooled_copy.start()
    wq_copy.wait()
    queries_ref[...] = dot(pooled, wq_ref[...]).T.astype(BF16)
    queries_copy = pltpu.make_async_copy(queries_ref, queries_hbm, out_sems.at[3])
    queries_copy.start()
    query = queries_ref[pl.ds(pl.multiple_of(member[0] * own, own), own), :]
    lhs[:own, :] = query
    query_ref[...] = query

    def score(base, width):
        first = pl.multiple_of(window(bounds, blocks, base) * LANES, LANES)
        exp = dot(
            lhs[:, pl.ds(first, 2 * LANES)],
            patch_major(start_ref, end_ref, first, 2 * LANES, base, width),
        )
        at = pl.ds(base, width)
        product = exp[:own] * kv_ref[:own, at].astype(F32)
        rows = [jnp.sum(product[h * dim:(h + 1) * dim], axis=0, keepdims=True) for h in range(heads)]
        probs_ref[:, at] = padded_rows(rows, 8) * (dim ** -0.5)
        geo = exp[own:own + 8]
        byte = (base + lax.broadcasted_iota(I32, (1, width), 1)).astype(F32)
        place = byte - (64.0 * geo[0:1] + geo[1:2])
        geo_ref[:, at] = padded_rows([place, geo[2:3] - 1.0 - place], 8)

    over_tiles(bounds, blocks, s_dev, rim, score)
    place, left = geo_ref[0:1, :], geo_ref[1:2, :]
    scores = probs_ref[...]
    before, after = over_segment(scores, place, left, jnp.maximum)
    expo = jnp.exp(scores - jnp.maximum(before, after))
    before, after = over_segment(expo, place, left, jnp.add)
    probs_ref[...] = jnp.where(left >= 0.0, expo / (before + (after - expo)), 0.0)
    att_acc[...] = jnp.zeros_like(att_acc)

    def attend(base, width):
        at = pl.ds(base, width)
        probs_b = probs_ref[:, at].astype(BF16).astype(F32)[:heads]
        both = split2(head_rows(probs_b, dim) * kv_ref[own:, at].astype(F32))
        first = pl.multiple_of(window(bounds, blocks, base) * LANES, LANES)
        att_acc[:, pl.ds(first, 2 * LANES)] += dot(
            both, byte_major(row_ref, first, 2 * LANES, base, width)
        )

    over_tiles(bounds, blocks, s_dev, rim, attend)
    att_ref[...] = (att_acc[:own, :] + att_acc[own:, :]).astype(BF16)
    for copy in (kv_copy, pooled_copy, queries_copy):
        copy.wait()


def hbm():
    return pl.BlockSpec(memory_space=pltpu.HBM)


def near():
    return pl.BlockSpec(memory_space=pl.ANY)


def forward(member, offset, lengths, x, rim, w_key, w_value, w_query, groups):
    s_dev, width = x.shape
    patches = lengths.shape[1]
    own = width // groups
    total = s_dev + LANES
    col = pl.BlockSpec((width, own), lambda i, member, offset: (0, member[0]))
    shape = jax.ShapeDtypeStruct
    small = [
        shape((own, patches), BF16), shape((own, patches), BF16), shape((8, total), F32), shape((8, total), F32), shape((16, patches), I32),
    ]
    return pl.pallas_call(
        forward_kernel,
        grid_spec=pltpu.PrefetchScalarGridSpec(
            num_scalar_prefetch=2,
            grid=(1,),
            in_specs=[whole(lengths.shape), hbm(), hbm(), whole(rim.shape), col, col],
            out_specs=[hbm()] * 3 + [whole(s.shape) for s in small] + [smem()],
            scratch_shapes=[
                pltpu.VMEM((LANES, width), BF16),
                pltpu.VMEM((s_dev, width), BF16),
                pltpu.VMEM((width, width), BF16),
                pltpu.VMEM((width, patches), BF16),
                pltpu.VMEM((2 * own, total), BF16),
                pltpu.VMEM((patches, width), BF16),
                pltpu.VMEM((width, 2 * own), BF16),
                pltpu.VMEM((patches, width), F32),
                pltpu.VMEM((own + 16, patches), BF16),
                pltpu.VMEM((patches, LANES), I32),
                pltpu.VMEM((patches, LANES), I32),
                pltpu.VMEM((patches, LANES), F32),
                pltpu.VMEM((2 * own, patches), F32),
                pltpu.SemaphoreType.DMA((4,)),
                pltpu.SemaphoreType.DMA((4,)),
            ],
        ),
        out_shape=[shape((2 * own, total), BF16), shape((patches, width), BF16), shape((width, patches), BF16)]
        + small + [shape((8,), I32)],
        compiler_params=params(56),
        cost_estimate=cost(8 << 30, 12 << 20),
        name="forward",
    )(member, offset, lengths, x, w_query, rim, w_key, w_value)


def att_sum_kernel(got_ref, out_ref):
    own = out_ref.shape[0]
    total = jnp.zeros(out_ref.shape, F32)
    for source in range(got_ref.shape[0]):
        total = total + from_i16(got_ref[source, :own, :]) * unit(got_ref[source, own:, :])[0:1]
    out_ref[...] = total.astype(BF16)


def att_sum(got):
    groups, rows, patches = got.shape
    vmem = pl.BlockSpec(memory_space=pltpu.VMEM)
    return pl.pallas_call(
        att_sum_kernel,
        in_specs=[vmem],
        out_specs=vmem,
        out_shape=jax.ShapeDtypeStruct((rows - 16, patches), BF16),
        compiler_params=params(8),
        cost_estimate=cost(1 << 20, 2 << 20),
        name="att_sum",
    )(got)


def backward_kernel(
    bounds, x_hbm, kv_hbm, pooled_hbm, rim_ref, d_att_ref, query_ref, probs_ref, geo_ref, row_ref,
    grad_ref, factor_out,
    rim_rows, x_ref, kv_ref, pooled_ref, factor_ref, start_ref, end_ref, d_kv, lhs, d_probs, d_scores, dq_acc, acc,
    x_sems, in_sems,
):
    rim = rim_rows.shape[0]
    s_dev = x_hbm.shape[0]
    own, patches = query_ref.shape
    blocks = patches // LANES
    dim = 64
    heads = own // dim
    kv_copy = pltpu.make_async_copy(kv_hbm, kv_ref, in_sems.at[0])
    kv_copy.start()
    chunks = x_sems.shape[0]
    chunk = s_dev // chunks
    loads = []
    for i in range(chunks):
        at = slice(i * chunk, (i + 1) * chunk)
        loads.append(pltpu.make_async_copy(x_hbm.at[at, :], x_ref.at[at, :], x_sems.at[i]))
    pooled_copy = pltpu.make_async_copy(pooled_hbm, pooled_ref, in_sems.at[1])

    columns_of(row_ref, start_ref, end_ref)
    lhs[:own, :] = d_att_ref[...]
    lhs[own:, :] = query_ref[...]
    factor_ref[:own, :] = d_att_ref[...]
    kv_copy.wait()
    for copy in loads + [pooled_copy]:
        copy.start()

    def first_pass(base, width):
        first = pl.multiple_of(window(bounds, blocks, base) * LANES, LANES)
        exp = dot(
            lhs[:, pl.ds(first, 2 * LANES)],
            patch_major(start_ref, end_ref, first, 2 * LANES, base, width),
        )
        d_out = exp[:own]
        at = pl.ds(base, width)
        product = d_out * kv_ref[own:, at].astype(F32)
        rows = [jnp.sum(product[h * dim:(h + 1) * dim], axis=0, keepdims=True) for h in range(heads)]
        d_probs[:, at] = padded_rows(rows, 8)
        probs_b = probs_ref[:, at].astype(BF16).astype(F32)[:heads]
        d_kv[own:, at] = (head_rows(probs_b, dim) * d_out).astype(BF16)
        d_kv[:own, at] = exp[own:].astype(BF16)

    over_tiles(bounds, blocks, s_dev, rim, first_pass)
    place, left = geo_ref[0:1, :], geo_ref[1:2, :]
    probs = probs_ref[...]
    weighted = probs * d_probs[...]
    before, after = over_segment(weighted, place, left, jnp.add)
    inner = before + (after - weighted)
    slope = jnp.where(left >= 0.0, probs * (d_probs[...] - inner) * (dim ** -0.5), 0.0)
    d_scores[...] = slope.astype(BF16).astype(F32)
    dq_acc[...] = jnp.zeros_like(dq_acc)

    def second_pass(base, width):
        at = pl.ds(base, width)
        wide = head_rows(d_scores[:, at][:heads], dim)
        d_kv[:own, at] = (wide * d_kv[:own, at].astype(F32)).astype(BF16)
        both = split2(wide * kv_ref[:own, at].astype(F32))
        first = pl.multiple_of(window(bounds, blocks, base) * LANES, LANES)
        dq_acc[:, pl.ds(first, 2 * LANES)] += dot(
            both, byte_major(row_ref, first, 2 * LANES, base, width)
        )

    over_tiles(bounds, blocks, s_dev, rim, second_pass)
    factor_ref[own:2 * own, :] = (dq_acc[:own, :] + dq_acc[own:, :]).astype(BF16)
    probs_b = probs.astype(BF16).astype(F32)
    rows = padded_rows(
        [d_scores[h:h + 1, :] for h in range(heads)] + [probs_b[h:h + 1, :] for h in range(heads)], 8
    )
    groups = [rows[:, at:at + patches] for at in range(0, s_dev, patches)]
    groups.append(jnp.concatenate([rows[:, s_dev:], jnp.zeros((8, patches - rim), F32)], axis=1))
    groups += [jnp.zeros((8, patches), F32)] * ((factor_ref.shape[0] - 2 * own) // 4 - len(groups))
    upper = lax.broadcasted_iota(I32, (8, patches), 0) < 4
    stack = [
        jnp.where(upper, groups[i], pltpu.roll(groups[i + 1], 4, 0)) for i in range(0, len(groups), 2)
    ]
    factor_ref[2 * own:, :] = jnp.concatenate(stack, axis=0).astype(BF16)
    factor_out[...] = factor_ref[...]

    fill_rim(rim_ref, rim_rows)
    acc[...] = dot(d_kv[:, s_dev:], rim_rows[...])
    for i in range(chunks):
        loads[i].wait()
    acc[...] += dot(d_kv[:, :s_dev], x_ref[...])
    pooled_copy.wait()
    grad_q = dot(factor_ref[own:2 * own, :], pooled_ref[...])
    powers = []
    parts = grad_ref.shape[0]
    for k, grad in enumerate((grad_q, acc[:own, :], acc[own:, :])):
        codes, power = coded(grad.T)
        powers.append(power)
        rows = codes.shape[0] // parts
        spread = codes.reshape(rows // 8, parts, 8, own)
        for part in range(parts):
            grad_ref[part, k * rows:(k + 1) * rows, :] = to_i16(spread[:, part].reshape(rows, own))
    tail = to_i16(padded_rows(powers, 16))
    for part in range(parts):
        grad_ref[part, 3 * rows:, :] = tail


def backward(bounds, x, kv, pooled, rim, d_att, query, probs, geo, row, parts):
    s_dev, width = x.shape
    own, patches = query.shape
    total = kv.shape[1]
    extra = -(-4 * (s_dev // patches + 1) // 16) * 16
    rows = width // parts
    vmem = pl.BlockSpec(memory_space=pltpu.VMEM)
    return pl.pallas_call(
        backward_kernel,
        in_specs=[smem()] + [hbm()] * 3 + [vmem] * 6,
        out_specs=[vmem, vmem],
        out_shape=[
            jax.ShapeDtypeStruct((parts, 3 * rows + 16, own), I16),
            jax.ShapeDtypeStruct((2 * own + extra, patches), BF16),
        ],
        scratch_shapes=[
            pltpu.VMEM((LANES, width), BF16),
            pltpu.VMEM((s_dev, width), BF16),
            pltpu.VMEM((2 * own, total), BF16),
            pltpu.VMEM((patches, width), BF16),
            pltpu.VMEM((2 * own + extra, patches), BF16),
            pltpu.VMEM((patches, LANES), I32),
            pltpu.VMEM((patches, LANES), I32),
            pltpu.VMEM((2 * own, total), BF16),
            pltpu.VMEM((2 * own, patches), BF16),
            pltpu.VMEM((8, total), F32),
            pltpu.VMEM((8, total), F32),
            pltpu.VMEM((2 * own, patches), F32),
            pltpu.VMEM((2 * own, width), F32),
            pltpu.SemaphoreType.DMA((4,)),
            pltpu.SemaphoreType.DMA((2,)),
        ],
        compiler_params=params(56),
        cost_estimate=cost(6 << 30, 16 << 20),
        name="backward",
    )(bounds, x, kv, pooled, rim, d_att, query, probs, geo, row)


def out_grad_kernel(member, mine_ref, other_ref, cot_ref, owner_ref, out_ref, rows_ref, att_ref):
    chips, own, patches = mine_ref.shape
    chip, core = member[0] // 2, member[0] % 2
    for ref, ref_core in ((mine_ref, core), (other_ref, 1 - core)):
        for back in range(chips):
            group = 2 * lax.rem(chip + chips - back, chips) + ref_core
            att_ref[pl.ds(pl.multiple_of(group * own, own), own), :] = ref[back]
    att = att_ref[...]
    codes, power = coded(dot(att, cot_ref[...]))
    parts = out_ref.shape[0]
    rows = codes.shape[0] // parts
    slabs = codes.shape[1] // LANES
    tail = to_i16(padded_rows([power[:, at * LANES:(at + 1) * LANES] for at in range(slabs)], 16))
    for part in range(parts):
        for at in range(slabs):
            block = codes[part * rows:(part + 1) * rows, at * LANES:(at + 1) * LANES]
            out_ref[part, at * rows:(at + 1) * rows, :] = to_i16(block)
        out_ref[part, slabs * rows:, :] = tail
    count = rows_ref.shape[0]
    order = jnp.broadcast_to(owner_ref[...], (8, patches))
    order = pltpu.roll(order, lax.rem(patches - member[0] * count, patches), 1)[0:1, :LANES]
    pick = jnp.where(lax.broadcasted_iota(I32, (patches, LANES), 0) == order, 1.0, 0.0).astype(BF16)
    rows_ref[...] = dot(att, pick).T[:count].astype(BF16)


def out_grad(member, mine, other, cot, owner, parts):
    chips, own, patches = mine.shape
    groups = 2 * chips
    width, cols = groups * own, cot.shape[1]
    rows = cols // LANES * (width // parts) + 16
    count = patches // groups
    return pl.pallas_call(
        out_grad_kernel,
        in_specs=[smem()] + [pl.BlockSpec(memory_space=pltpu.VMEM)] * 4,
        out_specs=[pl.BlockSpec(memory_space=pltpu.VMEM)] * 2,
        scratch_shapes=[pltpu.VMEM((width, patches), BF16)],
        out_shape=[
            jax.ShapeDtypeStruct((parts, rows, LANES), I16),
            jax.ShapeDtypeStruct((count, width), BF16),
        ],
        compiler_params=params(16),
        cost_estimate=cost(2 * width * cols * patches, 4 << 20),
        name="out_grad",
    )(member, mine, other, cot, owner)


def decoded(got_ref, first, count, power_row):
    rows = got_ref.shape[1]
    total = jnp.zeros((count, got_ref.shape[2]), F32)
    for source in range(got_ref.shape[0]):
        scale = unit(got_ref[source, rows - 16:, :])[power_row:power_row + 1]
        total = total + from_i16(got_ref[source, first:first + count, :]) * scale
    return total


def qkv_sum_kernel(member, got_ref, *refs):
    outs, blocks = refs[:-1], refs[-1]
    chips = len(outs)
    count = (got_ref.shape[1] - 16) // 3
    totals = [decoded(got_ref, k * count, count, k) for k in range(3)]
    for group in range(2 * chips):
        rows = [total[group * 8:(group + 1) * 8] for total in totals]
        rows = jnp.concatenate(rows + [jnp.zeros_like(rows[0])], axis=0)
        blocks[group // 2, group % 2 * 32:group % 2 * 32 + 32, :] = rows
    for at, out in enumerate(outs):
        out[...] = blocks[(member[0] // 2) ^ at].astype(BF16)


def qkv_sum(member, got, chips):
    vmem = pl.BlockSpec(memory_space=pltpu.VMEM)
    return pl.pallas_call(
        qkv_sum_kernel,
        in_specs=[smem(), vmem],
        out_specs=[vmem] * chips,
        out_shape=[jax.ShapeDtypeStruct((64, LANES), BF16)] * chips,
        scratch_shapes=[pltpu.VMEM((chips, 64, LANES), F32)],
        compiler_params=params(8),
        cost_estimate=cost(1 << 20, 2 << 20),
        name="qkv_sum",
    )(member, got)


def stack_kernel(*refs):
    out = refs[-1]
    for at, block in enumerate(refs[:-1]):
        out[at] = block[...]


def stack(blocks):
    vmem = pl.BlockSpec(memory_space=pltpu.VMEM)
    return pl.pallas_call(
        stack_kernel,
        in_specs=[vmem] * len(blocks),
        out_specs=vmem,
        out_shape=jax.ShapeDtypeStruct((len(blocks),) + blocks[0].shape, BF16),
        compiler_params=params(8),
        cost_estimate=cost(1 << 16, 1 << 20),
        name="stack",
    )(*blocks)


def relay_kernel(member, *refs):
    chips = (len(refs) - 5) // 2
    blocks, columns = refs[:chips], refs[chips:2 * chips]
    keep_ref, send_ref, mine_any, stage, sems = refs[2 * chips:]
    moves = [pltpu.make_async_copy(column, stage.at[i], sems.at[i]) for i, column in enumerate(columns)]
    for copy in moves:
        copy.start()
    core = member[0] % 2
    for at, block in enumerate(blocks):
        keep_ref[at * 32:(at + 1) * 32, :] = block[pl.ds(pl.multiple_of(core * 32, 32), 32), :]
        send_ref[at * 32:(at + 1) * 32, :] = block[pl.ds(pl.multiple_of((1 - core) * 32, 32), 32), :]
    sends = [pltpu.make_async_copy(stage.at[i], mine_any.at[i], sems.at[chips + i]) for i in range(chips)]
    for copy, send in zip(moves, sends):
        copy.wait()
        send.start()
    for send in sends:
        send.wait()


def relay(member, blocks, columns):
    vmem = pl.BlockSpec(memory_space=pltpu.VMEM)
    chips = len(blocks)
    return pl.pallas_call(
        relay_kernel,
        in_specs=[smem()] + [vmem] * chips + [near()] * chips,
        out_specs=[vmem, vmem, near()],
        out_shape=[
            jax.ShapeDtypeStruct((32 * chips, LANES), BF16),
            jax.ShapeDtypeStruct((32 * chips, LANES), BF16),
            jax.ShapeDtypeStruct((chips,) + columns[0].shape, BF16),
        ],
        scratch_shapes=[
            pltpu.VMEM((chips,) + columns[0].shape, BF16), pltpu.SemaphoreType.DMA((2 * chips,)),
        ],
        compiler_params=params(8),
        cost_estimate=cost(1 << 16, 3 << 20),
        name="relay",
    )(member, *blocks, *columns)


def pack_kernel(got_ref, keep_ref, other_ref, out_hbm, pack, sems):
    chips = keep_ref.shape[0] // 32
    rows = []
    for ref in (keep_ref, other_ref):
        values = ref[...].astype(F32)
        rows += [values[at * 32:at * 32 + 24] for at in range(chips)]
    first = 24 * len(rows)
    pack[:first, :] = jnp.concatenate(rows, axis=0).astype(BF16)
    count = (pack.shape[0] - first) // 4
    for slab in range(4):
        total = decoded(got_ref, slab * count, count, slab)
        pack[first + slab * count:first + (slab + 1) * count, :] = total.astype(BF16)
    for copy in send_copies(pack, out_hbm, sems):
        copy.wait()


def pack_sums(got, keep, other, parts):
    vmem = pl.BlockSpec(memory_space=pltpu.VMEM)
    rows = 24 * (keep.shape[0] // 16) + got.shape[1] - 16
    return pl.pallas_call(
        pack_kernel,
        in_specs=[vmem] * 3,
        out_specs=hbm(),
        out_shape=jax.ShapeDtypeStruct((parts, rows, LANES), BF16),
        scratch_shapes=[pltpu.VMEM((rows, LANES), BF16), pltpu.SemaphoreType.DMA((parts,))],
        compiler_params=params(60),
        cost_estimate=cost(1 << 20, 3 << 20),
        name="pack_sums",
    )(got, keep, other)


def unpack_kernel(member, got_ref, qkv_hbm, wout_hbm, qkv_ref, wout_ref, out_sems):
    parts, rows, lanes = got_ref.shape
    steps = out_sems.shape[0] // 2
    per = parts // steps
    groups = qkv_ref.shape[2] // lanes
    first = 24 * groups
    count = wout_ref.shape[0] // parts
    stores = []
    for step in range(steps):
        for part in range(step * per, (step + 1) * per):
            for slab in range(wout_ref.shape[1] // lanes):
                block = got_ref[part, first + slab * count:first + (slab + 1) * count, :]
                wout_ref[part * count:(part + 1) * count, slab * lanes:(slab + 1) * lanes] = block.astype(F32)
            values = got_ref[part, :first, :].astype(F32)
            for at in range(groups):
                source = member[0] ^ (2 * (at % (groups // 2)) + at // (groups // 2))
                lane = pl.ds(pl.multiple_of(source * lanes, lanes), lanes)
                for k in range(3):
                    top = at * 24 + k * 8
                    qkv_ref[k, part * 8:(part + 1) * 8, lane] = values[top:top + 8]
        at = slice(step * per * count, (step + 1) * per * count)
        stores.append(pltpu.make_async_copy(wout_ref.at[at, :], wout_hbm.at[at, :], out_sems.at[2 * step]))
        stores[-1].start()
        at = slice(step * per * 8, (step + 1) * per * 8)
        stores.append(pltpu.make_async_copy(qkv_ref.at[:, at, :], qkv_hbm.at[:, at, :], out_sems.at[2 * step + 1]))
        stores[-1].start()
    for copy in stores:
        copy.wait()


def unpack_sums(member, got, width, cols, groups):
    steps = 4
    qkv = ((3, width // groups, width), F32)
    wout = ((width, cols), F32)
    return pl.pallas_call(
        unpack_kernel,
        in_specs=[smem(), pl.BlockSpec(memory_space=pltpu.VMEM)],
        out_specs=[hbm(), hbm()],
        out_shape=[jax.ShapeDtypeStruct(*qkv), jax.ShapeDtypeStruct(*wout)],
        scratch_shapes=[
            pltpu.VMEM(*qkv), pltpu.VMEM(*wout), pltpu.SemaphoreType.DMA((2 * steps,)),
        ],
        compiler_params=params(12),
        cost_estimate=cost(1 << 20, 6 << 20),
        name="unpack_sums",
    )(member, got)


def bytes_kernel(
    member, bounds, mine_hbm, other_hbm, query_hbm, wk_hbm, wv_hbm, wq_hbm, row_ref,
    out_ref, head_ref, tail_ref,
    lhs, d_query, tables, shares, d_kv, w_own, wq_own, start_ref, end_ref, sems,
):
    chips, rows, patches = mine_hbm.shape
    groups = 2 * chips
    own, width = wq_own.shape
    dim = 64
    heads = own // dim
    blocks = patches // LANES
    total = shares.shape[2]
    s_dev = out_ref.shape[0]
    rim = total - s_dev
    chip, core = member[0] // 2, member[0] % 2
    own_rows = pl.ds(pl.multiple_of(member[0] * own, own), own)
    moves = []

    def move(source, target):
        moves.append(pltpu.make_async_copy(source, target, sems.at[len(moves)]))
        moves[-1].start()

    places = []
    for ref, ref_core in ((mine_hbm, core), (other_hbm, 1 - core)):
        for back in range(chips):
            group = 2 * lax.rem(chip + chips - back, chips) + ref_core
            at = pl.multiple_of(group * own, own)
            places.append(group)
            move(ref.at[back, 2 * own:, :], tables.at[len(places) - 1])
            move(ref.at[back, own:2 * own, :], d_query.at[pl.ds(at, own), :])
            move(ref.at[back, :own, :], lhs.at[pl.ds(width + at, own), :])
    move(wq_hbm.at[own_rows, :], wq_own)
    move(query_hbm, lhs.at[:width, :])
    move(wk_hbm.at[own_rows, :], w_own.at[:, :width])
    move(wv_hbm.at[own_rows, :], w_own.at[:, width:])
    columns_of(row_ref, start_ref, end_ref)
    for copy in moves:
        copy.wait()
    for slot, group in enumerate(places):
        table = tables[slot].astype(F32)
        for at in range(s_dev // patches + 1):
            part = table[8 * (at // 2):8 * (at // 2) + 8]
            part = pltpu.roll(part, 4, 0) if at % 2 else part
            if at < s_dev // patches:
                shares[group, :, at * patches:(at + 1) * patches] = part
            else:
                shares[group, :, s_dev:] = part[:, :rim]
    length = (row_ref[8:9, :] - row_ref[0:1, :]).astype(F32)
    lhs[2 * width:, :] = split2(dot(wq_own[...], d_query[...]) * (1.0 / length))

    def tile_grad(base, span, first, count, slot):
        inside = patch_major(start_ref, end_ref, first, count, base, span)
        at = pl.ds(base, span)
        patch = pl.ds(first, count)
        for group in range(groups):
            share = shares[group, :, at]
            for kind in range(2):
                top = kind * width + group * own
                wide = dot(lhs[top:top + own, patch], inside)
                part = head_rows(share[kind * heads:(kind + 1) * heads], dim)
                d_kv[slot, top:top + own, :span] = (part * wide).astype(BF16)
        grad = dot(w_own[...], d_kv[slot, :, :span])
        pool = dot(lhs[2 * width:, patch], inside)
        return (grad + (pool[:own] + pool[own:])).T

    def tiles(span, first_of, count):
        def go(i, carry):
            for slot in range(UNROLL):
                base = pl.multiple_of((UNROLL * i + slot) * span, span)
                out_ref[pl.ds(base, span), :] = tile_grad(base, span, first_of(base), count, slot).astype(BF16)
            return carry

        lax.fori_loop(0, s_dev // (UNROLL * span), go, 0)

    def first_of(base):
        return pl.multiple_of(window(bounds, blocks, base) * LANES, LANES)

    @pl.when(bounds[blocks + 1] > 0)
    def _():
        tiles(LANES, first_of, 2 * LANES)

    @pl.when(bounds[blocks + 1] == 0)
    def _():
        tiles(TILE, first_of, 2 * LANES)

    head_ref[...] = tile_grad(0, LANES, 0, 2 * LANES, 0)[:16]
    tail_ref[...] = tile_grad(s_dev, rim, patches - 2 * LANES, 2 * LANES, 1)[:16]


def byte_grads(member, bounds, mine_factors, other_factors, query, w_query, w_key, w_value, row, s_dev):
    chips, rows, patches = mine_factors.shape
    groups = 2 * chips
    width = w_query.shape[0]
    own = width // groups
    rim = LANES
    return pl.pallas_call(
        bytes_kernel,
        in_specs=[smem(), smem(), near(), near()] + [hbm()] * 4 + [pl.BlockSpec(memory_space=pltpu.VMEM)],
        out_specs=[pl.BlockSpec(memory_space=pltpu.VMEM)] * 3,
        scratch_shapes=[
            pltpu.VMEM((2 * width + 2 * own, patches), BF16),
            pltpu.VMEM((width, patches), BF16),
            pltpu.VMEM((groups, rows - 2 * own, patches), BF16),
            pltpu.VMEM((groups, 8, s_dev + rim), F32),
            pltpu.VMEM((UNROLL, 2 * width, TILE), BF16),
            pltpu.VMEM((own, 2 * width), BF16),
            pltpu.VMEM((own, width), BF16),
            pltpu.VMEM((patches, LANES), I32),
            pltpu.VMEM((patches, LANES), I32),
            pltpu.SemaphoreType.DMA((3 * groups + 4,)),
        ],
        out_shape=[
            jax.ShapeDtypeStruct((s_dev, own), BF16),
            jax.ShapeDtypeStruct((16, own), F32),
            jax.ShapeDtypeStruct((16, own), F32),
        ],
        compiler_params=params(52),
        cost_estimate=cost(8 << 30, 8 << 20),
        name="byte_grads",
    )(member, bounds, mine_factors, other_factors, query, w_key, w_value, w_query, row)


def shifted(value, axis, steps):
    count = lax.axis_size(axis)
    first, last = (max(0, -steps), min(count, count - steps))
    return lax.ppermute(value, axis, [(source, source + steps) for source in range(first, last)])


def swap(value, axis):
    return lax.all_to_all(value, axis, split_axis=0, concat_axis=0, tiled=True)


def over_chips(value):
    count = lax.axis_size("patch")
    blocks = [value]
    for step in range(1, count // 2):
        pairs = [(i, (i + 2 * step) % count) for i in range(count)]
        blocks.append(lax.ppermute(value, "patch", pairs))
    return blocks


def other_core(value):
    return lax.ppermute(value, "patch", [(i, i ^ 1) for i in range(lax.axis_size("patch"))])


def after(value, *others):
    return lax.optimization_barrier((value,) + others)[0]


def local(byte_states, patch_len, shard_offset, owner, cotangent, w_query, w_key, w_value, w_out):
    s_dev, width = byte_states.shape
    groups = lax.axis_size("patch")
    parts = lax.axis_size("seq")
    member = lax.axis_index("patch").astype(I32).reshape(1)
    rim = shifted(byte_states[:MAXP], "seq", -1)

    coded_att = after(att_grad(w_out, cotangent, groups), rim)
    got_att = swap(coded_att, "patch")
    kv, pooled, all_query, att, query, probs, geo, row, bounds = forward(
        member, shard_offset, patch_len, byte_states, rim, w_key, w_value, w_query, groups
    )
    att_columns = over_chips(att)
    grads, factor = backward(bounds, byte_states, kv, pooled, rim, att_sum(got_att), query, probs, geo, row, parts)
    got_qkv = swap(after(grads, *att_columns[1:]), "seq")
    mine_att = stack([after(att_columns[0], grads)] + att_columns[1:])
    other_att = other_core(mine_att)
    columns = over_chips(factor)
    coded_out, patch_rows = out_grad(member, mine_att, other_att, cotangent, owner, parts)
    got_out = swap(after(coded_out, got_qkv, columns[1], columns[3]), "seq")
    blocks = [
        block if at == 0 else lax.ppermute(block, "patch", [(i, i ^ (2 * at)) for i in range(groups)])
        for at, block in enumerate(qkv_sum(member, got_qkv, groups // 2))
    ]
    keep, send, mine = relay(member, blocks, columns)
    got_keep = other_core(send)
    other = other_core(mine)
    sums = swap(pack_sums(got_out, keep, got_keep, parts), "seq")
    d_bytes, head, tail = byte_grads(
        member, bounds, mine, other, all_query, w_query, w_key, w_value, row, s_dev
    )
    first = (head + shifted(tail, "seq", 1)).astype(BF16)
    d_bytes = lax.dynamic_update_slice(d_bytes, first, (0, 0))
    d_qkv, d_wout = unpack_sums(member, sums, width, cotangent.shape[1], groups)
    return (d_bytes, d_qkv, d_wout, patch_rows)


def solution(mesh):
    return jax.shard_map(
        local,
        mesh=mesh,
        in_specs=(
            P("seq", None), P("seq", None), P("seq"), P("seq", None), P("seq", "patch"),
            P(), P(), P(), P(None, "patch"),
        ),
        out_specs=(P("seq", "patch"), P(None, "patch", None), P(None, "patch"), P(("seq", "patch"), None)),
        check_vma=False,
    )
```

```python
import jax
import jax.numpy as jnp
from jax import lax
from jax.experimental import pallas as pl
from jax.experimental.pallas import tpu as pltpu
from jax.sharding import PartitionSpec as P

HEADS = 16
MAXP = 16
LANES = 128
TILE = 256
UNROLL = 4
F32, BF16, I16, I32 = jnp.float32, jnp.bfloat16, jnp.int16, jnp.int32
NT = (((1,), (1,)), ((), ()))


def params(mebibytes):
    return pltpu.CompilerParams(vmem_limit_bytes=mebibytes * 1024 * 1024)


def cost(flops, moved):
    return pl.CostEstimate(flops=flops, bytes_accessed=moved, transcendentals=0)


def whole(shape):
    return pl.BlockSpec(shape, lambda *_: (0,) * len(shape))


def smem():
    return pl.BlockSpec(memory_space=pltpu.SMEM)


def dot(a, b):
    return jnp.dot(a, b, preferred_element_type=F32)


def dot_nt(a, b):
    return lax.dot_general(a, b, NT, preferred_element_type=F32)


def coded(value):
    peak = jnp.max(jnp.abs(value), axis=0, keepdims=True)
    power = jnp.ceil(jnp.log2(jnp.maximum(peak, 1e-30)))
    return jnp.round(value * (32767.0 * jnp.exp2(-power))), power


def to_i16(value):
    return value.astype(I32).astype(I16)


def from_i16(value):
    return value.astype(I32).astype(F32)


def unit(power):
    return jnp.exp2(from_i16(power)) * (1.0 / 32767.0)


def padded_rows(row_list, count):
    width = row_list[0].shape[1]
    at = lax.broadcasted_iota(I32, (count, width), 0)
    out = jnp.zeros((count, width), F32)
    for i, row in enumerate(row_list):
        out = jnp.where(at == i, jnp.broadcast_to(row, (count, width)), out)
    return out


def window(bounds, blocks, base):
    block = jnp.int32(0)
    for at in range(1, blocks - 1):
        block = block + (bounds[at] <= base).astype(I32)
    return block


def patch_major(start_ref, end_ref, first, count, base, width):
    rows = pl.ds(pl.multiple_of(first, LANES), count)
    start, end = start_ref[rows, :], end_ref[rows, :]
    parts = []
    for at in range(0, width, LANES):
        byte = base + at + lax.broadcasted_iota(I32, (count, LANES), 1)
        parts.append(jnp.where((byte >= start) & (byte < end), 1.0, 0.0).astype(BF16))
    return parts[0] if len(parts) == 1 else jnp.concatenate(parts, axis=1)


def byte_major(row_ref, first, count, base, width):
    lanes = pl.ds(pl.multiple_of(first, LANES), count)
    byte = base + lax.broadcasted_iota(I32, (width, count), 0)
    inside = (byte >= row_ref[0:1, lanes]) & (byte < row_ref[8:9, lanes])
    return jnp.where(inside, 1.0, 0.0).astype(BF16)


def over_tiles(bounds, blocks, s_dev, rim, body):
    def loop(width, unroll):
        def go(i, carry):
            for at in range(unroll):
                body(pl.multiple_of((i * unroll + at) * width, width), width)
            return carry

        lax.fori_loop(0, s_dev // (unroll * width), go, 0)

    @pl.when(bounds[blocks + 1] == 0)
    def _():
        loop(TILE, 2 * UNROLL)

    @pl.when(bounds[blocks + 1] > 0)
    def _():
        loop(LANES, 1)

    body(s_dev, rim)


def fill_rim(rim_ref, rim_rows):
    rim_rows[...] = jnp.zeros_like(rim_rows)
    rim_rows[:rim_ref.shape[0], :] = rim_ref[...]


def columns_of(row_ref, start_ref, end_ref):
    patches = row_ref.shape[1]
    start_ref[...] = jnp.broadcast_to(row_ref[0:1, :], (LANES, patches)).T
    end_ref[...] = jnp.broadcast_to(row_ref[8:9, :], (LANES, patches)).T


def send_copies(source, target, sems):
    copies = [pltpu.make_async_copy(source, target.at[i], sems.at[i]) for i in range(target.shape[0])]
    for copy in copies:
        copy.start()
    return copies


def over_segment(value, place, left, op):
    size = value.shape[1]
    before, after = value, value
    for step in (1, 2, 4, 8):
        before = jnp.where(place >= step, op(before, pltpu.roll(before, step, 1)), before)
        after = jnp.where(left >= step, op(after, pltpu.roll(after, size - step, 1)), after)
    return before, after


def head_rows(rows, dim):
    count, width = rows.shape
    return jnp.concatenate(
        [jnp.broadcast_to(rows[i:i + 1], (dim, width)) for i in range(count)], axis=0
    )


def split2(value):
    high = value.astype(BF16)
    return jnp.concatenate([high, (value - high.astype(F32)).astype(BF16)], axis=0)


def att_grad_kernel(w_ref, cot_ref, out_ref, cot_t):
    groups = out_ref.shape[0]
    own = w_ref.shape[0] // groups
    cot_t[...] = cot_ref[...].astype(F32).T.astype(BF16)
    for group in range(groups):
        codes, power = coded(dot(w_ref[group * own:(group + 1) * own, :], cot_t[...]))
        out_ref[group, :own, :] = to_i16(codes)
        out_ref[group, own:, :] = to_i16(jnp.broadcast_to(power, (16, power.shape[1])))


def att_grad(w_out, cot, groups):
    width, cols = w_out.shape
    rows = cot.shape[0]
    own = width // groups
    return pl.pallas_call(
        att_grad_kernel,
        in_specs=[pl.BlockSpec(memory_space=pltpu.VMEM)] * 2,
        out_specs=pl.BlockSpec(memory_space=pltpu.VMEM),
        out_shape=jax.ShapeDtypeStruct((groups, own + 16, rows), I16),
        scratch_shapes=[pltpu.VMEM((cols, rows), BF16)],
        compiler_params=params(56),
        cost_estimate=cost(2 * width * cols * rows, 4 << 20),
        name="att_grad",
    )(w_out, cot)


def forward_kernel(
    member, offset, len_ref, x_hbm, wq_hbm, rim_ref, wk_ref, wv_ref,
    kv_hbm, pooled_hbm, queries_hbm, att_ref, query_ref, probs_ref, geo_ref, row_ref, bounds,
    rim_rows, x_ref, wq_ref, queries_ref, kv_ref, pooled_ref, w_kv, acc, lhs, start_ref, end_ref, inv_col, att_acc,
    x_sems, out_sems,
):
    rim = rim_rows.shape[0]
    patches = len_ref.shape[1]
    blocks = patches // LANES
    own = wk_ref.shape[1]
    dim = 64
    heads = own // dim
    s_dev = x_hbm.shape[0]
    chunks = x_sems.shape[0]
    chunk = s_dev // chunks
    loads = []
    for i in range(chunks):
        at = slice(i * chunk, (i + 1) * chunk)
        loads.append(pltpu.make_async_copy(x_hbm.at[at, :], x_ref.at[at, :], x_sems.at[i]))
        loads[-1].start()
    wq_copy = pltpu.make_async_copy(wq_hbm, wq_ref, out_sems.at[2])
    wq_copy.start()

    length = len_ref[...].astype(F32)
    before = lax.broadcasted_iota(I32, (patches, patches), 0)
    after = lax.broadcasted_iota(I32, (patches, patches), 1)
    off = offset[0].astype(F32)
    eight = jnp.broadcast_to(length, (8, patches))
    upper = jnp.where(before < after, 1.0, 0.0).astype(BF16)
    start_row = (dot(eight.astype(BF16), upper) + off).astype(I32)
    row_ref[:8, :] = start_row
    row_ref[8:, :] = start_row + eight.astype(I32)
    columns_of(row_ref, start_ref, end_ref)
    inv_col[...] = 1.0 / jnp.broadcast_to(length, (LANES, patches)).T
    at = lax.broadcasted_iota(I32, (16, patches), 0)
    both = jnp.concatenate([start_row, start_row], axis=0)
    geo = jnp.where(at == 0, both >> 6, jnp.where(at == 1, both & 63, 0)).astype(F32)
    geo = jnp.where(at == 2, jnp.broadcast_to(length, (16, patches)), geo)
    lhs[own:own + 16, :] = geo.astype(BF16)
    lane = lax.broadcasted_iota(I32, (1, patches), 1)
    for block in range(blocks + 1):
        total = jnp.sum(jnp.where(lane < block * LANES, length, 0.0))
        bounds[block] = (total + off).astype(I32)

    def crowded(i, found):
        base = i * TILE
        third = window(bounds, blocks, base) + 2
        return found | ((third < blocks) & (bounds[third] < base + TILE)).astype(I32)

    bounds[blocks + 1] = lax.fori_loop(0, s_dev // TILE, crowded, jnp.int32(0))
    w_kv[:, :own] = wk_ref[...]
    w_kv[:, own:] = wv_ref[...]
    acc[...] = jnp.zeros_like(acc)

    def project(rows, base, width):
        kv_ref[:, pl.ds(base, width)] = dot(rows, w_kv[...]).T.astype(BF16)
        first = pl.multiple_of(window(bounds, blocks, base) * LANES, LANES)
        at = pl.ds(first, 2 * LANES)
        acc[at, :] += dot(patch_major(start_ref, end_ref, first, 2 * LANES, base, width), rows)

    for i in range(chunks):
        loads[i].wait()
        for at in range(i * chunk, (i + 1) * chunk, TILE):
            project(x_ref[at:at + TILE, :], at, TILE)
    fill_rim(rim_ref, rim_rows)
    project(rim_rows[...], s_dev, rim)

    @pl.when(bounds[blocks + 1] > 0)
    def _():
        def rest(i, carry):
            base = pl.multiple_of(i * TILE, TILE)
            third = window(bounds, blocks, base) + 2

            @pl.when((third < blocks) & (bounds[third] < base + TILE))
            def _():
                first = pl.multiple_of(third * LANES, LANES)
                acc[pl.ds(first, LANES), :] += dot(
                    patch_major(start_ref, end_ref, first, LANES, base, TILE), x_ref[pl.ds(base, TILE), :]
                )

            return carry

        lax.fori_loop(0, s_dev // TILE, rest, 0)

    kv_copy = pltpu.make_async_copy(kv_ref, kv_hbm, out_sems.at[0])
    kv_copy.start()
    pooled = (acc[...] * inv_col[:, :1]).astype(BF16)
    pooled_ref[...] = pooled
    pooled_copy = pltpu.make_async_copy(pooled_ref, pooled_hbm, out_sems.at[1])
    pooled_copy.start()
    wq_copy.wait()
    queries_ref[...] = dot(pooled, wq_ref[...]).T.astype(BF16)
    queries_copy = pltpu.make_async_copy(queries_ref, queries_hbm, out_sems.at[3])
    queries_copy.start()
    query = queries_ref[pl.ds(pl.multiple_of(member[0] * own, own), own), :]
    lhs[:own, :] = query
    query_ref[...] = query

    def score(base, width):
        first = pl.multiple_of(window(bounds, blocks, base) * LANES, LANES)
        exp = dot(
            lhs[:, pl.ds(first, 2 * LANES)],
            patch_major(start_ref, end_ref, first, 2 * LANES, base, width),
        )
        at = pl.ds(base, width)
        product = exp[:own] * kv_ref[:own, at].astype(F32)
        rows = [jnp.sum(product[h * dim:(h + 1) * dim], axis=0, keepdims=True) for h in range(heads)]
        probs_ref[:, at] = padded_rows(rows, 8) * (dim ** -0.5)
        geo = exp[own:own + 8]
        byte = (base + lax.broadcasted_iota(I32, (1, width), 1)).astype(F32)
        place = byte - (64.0 * geo[0:1] + geo[1:2])
        geo_ref[:, at] = padded_rows([place, geo[2:3] - 1.0 - place], 8)

    over_tiles(bounds, blocks, s_dev, rim, score)
    place, left = geo_ref[0:1, :], geo_ref[1:2, :]
    scores = probs_ref[...]
    before, after = over_segment(scores, place, left, jnp.maximum)
    expo = jnp.exp(scores - jnp.maximum(before, after))
    before, after = over_segment(expo, place, left, jnp.add)
    probs_ref[...] = jnp.where(left >= 0.0, expo / (before + (after - expo)), 0.0)
    att_acc[...] = jnp.zeros_like(att_acc)

    def attend(base, width):
        at = pl.ds(base, width)
        probs_b = probs_ref[:, at].astype(BF16).astype(F32)[:heads]
        both = split2(head_rows(probs_b, dim) * kv_ref[own:, at].astype(F32))
        first = pl.multiple_of(window(bounds, blocks, base) * LANES, LANES)
        att_acc[:, pl.ds(first, 2 * LANES)] += dot(
            both, byte_major(row_ref, first, 2 * LANES, base, width)
        )

    over_tiles(bounds, blocks, s_dev, rim, attend)
    att_ref[...] = (att_acc[:own, :] + att_acc[own:, :]).astype(BF16)
    for copy in (kv_copy, pooled_copy, queries_copy):
        copy.wait()


def hbm():
    return pl.BlockSpec(memory_space=pltpu.HBM)


def near():
    return pl.BlockSpec(memory_space=pl.ANY)


def forward(member, offset, lengths, x, rim, w_key, w_value, w_query, groups):
    s_dev, width = x.shape
    patches = lengths.shape[1]
    own = width // groups
    total = s_dev + LANES
    col = pl.BlockSpec((width, own), lambda i, member, offset: (0, member[0]))
    shape = jax.ShapeDtypeStruct
    small = [
        shape((own, patches), BF16), shape((own, patches), BF16), shape((8, total), F32), shape((8, total), F32), shape((16, patches), I32),
    ]
    return pl.pallas_call(
        forward_kernel,
        grid_spec=pltpu.PrefetchScalarGridSpec(
            num_scalar_prefetch=2,
            grid=(1,),
            in_specs=[whole(lengths.shape), hbm(), hbm(), whole(rim.shape), col, col],
            out_specs=[hbm()] * 3 + [whole(s.shape) for s in small] + [smem()],
            scratch_shapes=[
                pltpu.VMEM((LANES, width), BF16),
                pltpu.VMEM((s_dev, width), BF16),
                pltpu.VMEM((width, width), BF16),
                pltpu.VMEM((width, patches), BF16),
                pltpu.VMEM((2 * own, total), BF16),
                pltpu.VMEM((patches, width), BF16),
                pltpu.VMEM((width, 2 * own), BF16),
                pltpu.VMEM((patches, width), F32),
                pltpu.VMEM((own + 16, patches), BF16),
                pltpu.VMEM((patches, LANES), I32),
                pltpu.VMEM((patches, LANES), I32),
                pltpu.VMEM((patches, LANES), F32),
                pltpu.VMEM((2 * own, patches), F32),
                pltpu.SemaphoreType.DMA((4,)),
                pltpu.SemaphoreType.DMA((4,)),
            ],
        ),
        out_shape=[shape((2 * own, total), BF16), shape((patches, width), BF16), shape((width, patches), BF16)]
        + small + [shape((8,), I32)],
        compiler_params=params(56),
        cost_estimate=cost(8 << 30, 12 << 20),
        name="forward",
    )(member, offset, lengths, x, w_query, rim, w_key, w_value)


def att_sum_kernel(got_ref, out_ref):
    own = out_ref.shape[0]
    total = jnp.zeros(out_ref.shape, F32)
    for source in range(got_ref.shape[0]):
        total = total + from_i16(got_ref[source, :own, :]) * unit(got_ref[source, own:, :])[0:1]
    out_ref[...] = total.astype(BF16)


def att_sum(got):
    groups, rows, patches = got.shape
    vmem = pl.BlockSpec(memory_space=pltpu.VMEM)
    return pl.pallas_call(
        att_sum_kernel,
        in_specs=[vmem],
        out_specs=vmem,
        out_shape=jax.ShapeDtypeStruct((rows - 16, patches), BF16),
        compiler_params=params(8),
        cost_estimate=cost(1 << 20, 2 << 20),
        name="att_sum",
    )(got)


def backward_kernel(
    bounds, x_hbm, kv_hbm, pooled_hbm, rim_ref, d_att_ref, query_ref, probs_ref, geo_ref, row_ref,
    grad_ref, factor_out,
    rim_rows, x_ref, kv_ref, pooled_ref, factor_ref, start_ref, end_ref, d_kv, lhs, d_probs, d_scores, dq_acc, acc,
    x_sems, in_sems,
):
    rim = rim_rows.shape[0]
    s_dev = x_hbm.shape[0]
    own, patches = query_ref.shape
    blocks = patches // LANES
    dim = 64
    heads = own // dim
    kv_copy = pltpu.make_async_copy(kv_hbm, kv_ref, in_sems.at[0])
    kv_copy.start()
    chunks = x_sems.shape[0]
    chunk = s_dev // chunks
    loads = []
    for i in range(chunks):
        at = slice(i * chunk, (i + 1) * chunk)
        loads.append(pltpu.make_async_copy(x_hbm.at[at, :], x_ref.at[at, :], x_sems.at[i]))
    pooled_copy = pltpu.make_async_copy(pooled_hbm, pooled_ref, in_sems.at[1])

    columns_of(row_ref, start_ref, end_ref)
    lhs[:own, :] = d_att_ref[...]
    lhs[own:, :] = query_ref[...]
    factor_ref[:own, :] = d_att_ref[...]
    kv_copy.wait()
    for copy in loads + [pooled_copy]:
        copy.start()

    def first_pass(base, width):
        first = pl.multiple_of(window(bounds, blocks, base) * LANES, LANES)
        exp = dot(
            lhs[:, pl.ds(first, 2 * LANES)],
            patch_major(start_ref, end_ref, first, 2 * LANES, base, width),
        )
        d_out = exp[:own]
        at = pl.ds(base, width)
        product = d_out * kv_ref[own:, at].astype(F32)
        rows = [jnp.sum(product[h * dim:(h + 1) * dim], axis=0, keepdims=True) for h in range(heads)]
        d_probs[:, at] = padded_rows(rows, 8)
        probs_b = probs_ref[:, at].astype(BF16).astype(F32)[:heads]
        d_kv[own:, at] = (head_rows(probs_b, dim) * d_out).astype(BF16)
        d_kv[:own, at] = exp[own:].astype(BF16)

    over_tiles(bounds, blocks, s_dev, rim, first_pass)
    place, left = geo_ref[0:1, :], geo_ref[1:2, :]
    probs = probs_ref[...]
    weighted = probs * d_probs[...]
    before, after = over_segment(weighted, place, left, jnp.add)
    inner = before + (after - weighted)
    slope = jnp.where(left >= 0.0, probs * (d_probs[...] - inner) * (dim ** -0.5), 0.0)
    d_scores[...] = slope.astype(BF16).astype(F32)
    dq_acc[...] = jnp.zeros_like(dq_acc)

    def second_pass(base, width):
        at = pl.ds(base, width)
        wide = head_rows(d_scores[:, at][:heads], dim)
        d_kv[:own, at] = (wide * d_kv[:own, at].astype(F32)).astype(BF16)
        both = split2(wide * kv_ref[:own, at].astype(F32))
        first = pl.multiple_of(window(bounds, blocks, base) * LANES, LANES)
        dq_acc[:, pl.ds(first, 2 * LANES)] += dot(
            both, byte_major(row_ref, first, 2 * LANES, base, width)
        )

    over_tiles(bounds, blocks, s_dev, rim, second_pass)
    factor_ref[own:2 * own, :] = (dq_acc[:own, :] + dq_acc[own:, :]).astype(BF16)
    probs_b = probs.astype(BF16).astype(F32)
    rows = padded_rows(
        [d_scores[h:h + 1, :] for h in range(heads)] + [probs_b[h:h + 1, :] for h in range(heads)], 8
    )
    groups = [rows[:, at:at + patches] for at in range(0, s_dev, patches)]
    groups.append(jnp.concatenate([rows[:, s_dev:], jnp.zeros((8, patches - rim), F32)], axis=1))
    groups += [jnp.zeros((8, patches), F32)] * ((factor_ref.shape[0] - 2 * own) // 4 - len(groups))
    upper = lax.broadcasted_iota(I32, (8, patches), 0) < 4
    stack = [
        jnp.where(upper, groups[i], pltpu.roll(groups[i + 1], 4, 0)) for i in range(0, len(groups), 2)
    ]
    factor_ref[2 * own:, :] = jnp.concatenate(stack, axis=0).astype(BF16)
    factor_out[...] = factor_ref[...]

    fill_rim(rim_ref, rim_rows)
    acc[...] = dot(d_kv[:, s_dev:], rim_rows[...])
    for i in range(chunks):
        loads[i].wait()
    acc[...] += dot(d_kv[:, :s_dev], x_ref[...])
    pooled_copy.wait()
    grad_q = dot(factor_ref[own:2 * own, :], pooled_ref[...])
    powers = []
    parts = grad_ref.shape[0]
    for k, grad in enumerate((grad_q, acc[:own, :], acc[own:, :])):
        codes, power = coded(grad.T)
        powers.append(power)
        rows = codes.shape[0] // parts
        spread = codes.reshape(rows // 8, parts, 8, own)
        for part in range(parts):
            grad_ref[part, k * rows:(k + 1) * rows, :] = to_i16(spread[:, part].reshape(rows, own))
    tail = to_i16(padded_rows(powers, 16))
    for part in range(parts):
        grad_ref[part, 3 * rows:, :] = tail


def backward(bounds, x, kv, pooled, rim, d_att, query, probs, geo, row, parts):
    s_dev, width = x.shape
    own, patches = query.shape
    total = kv.shape[1]
    extra = -(-4 * (s_dev // patches + 1) // 16) * 16
    rows = width // parts
    vmem = pl.BlockSpec(memory_space=pltpu.VMEM)
    return pl.pallas_call(
        backward_kernel,
        in_specs=[smem()] + [hbm()] * 3 + [vmem] * 6,
        out_specs=[vmem, vmem],
        out_shape=[
            jax.ShapeDtypeStruct((parts, 3 * rows + 16, own), I16),
            jax.ShapeDtypeStruct((2 * own + extra, patches), BF16),
        ],
        scratch_shapes=[
            pltpu.VMEM((LANES, width), BF16),
            pltpu.VMEM((s_dev, width), BF16),
            pltpu.VMEM((2 * own, total), BF16),
            pltpu.VMEM((patches, width), BF16),
            pltpu.VMEM((2 * own + extra, patches), BF16),
            pltpu.VMEM((patches, LANES), I32),
            pltpu.VMEM((patches, LANES), I32),
            pltpu.VMEM((2 * own, total), BF16),
            pltpu.VMEM((2 * own, patches), BF16),
            pltpu.VMEM((8, total), F32),
            pltpu.VMEM((8, total), F32),
            pltpu.VMEM((2 * own, patches), F32),
            pltpu.VMEM((2 * own, width), F32),
            pltpu.SemaphoreType.DMA((4,)),
            pltpu.SemaphoreType.DMA((2,)),
        ],
        compiler_params=params(56),
        cost_estimate=cost(6 << 30, 16 << 20),
        name="backward",
    )(bounds, x, kv, pooled, rim, d_att, query, probs, geo, row)


def out_grad_kernel(member, mine_ref, other_ref, cot_ref, owner_ref, out_ref, rows_ref, att_ref):
    chips, own, patches = mine_ref.shape
    chip, core = member[0] // 2, member[0] % 2
    for ref, ref_core in ((mine_ref, core), (other_ref, 1 - core)):
        for back in range(chips):
            group = 2 * lax.rem(chip + chips - back, chips) + ref_core
            att_ref[pl.ds(pl.multiple_of(group * own, own), own), :] = ref[back]
    att = att_ref[...]
    codes, power = coded(dot(att, cot_ref[...]))
    parts = out_ref.shape[0]
    rows = codes.shape[0] // parts
    slabs = codes.shape[1] // LANES
    tail = to_i16(padded_rows([power[:, at * LANES:(at + 1) * LANES] for at in range(slabs)], 16))
    for part in range(parts):
        for at in range(slabs):
            block = codes[part * rows:(part + 1) * rows, at * LANES:(at + 1) * LANES]
            out_ref[part, at * rows:(at + 1) * rows, :] = to_i16(block)
        out_ref[part, slabs * rows:, :] = tail
    count = rows_ref.shape[0]
    order = jnp.broadcast_to(owner_ref[...], (8, patches))
    order = pltpu.roll(order, lax.rem(patches - member[0] * count, patches), 1)[0:1, :LANES]
    pick = jnp.where(lax.broadcasted_iota(I32, (patches, LANES), 0) == order, 1.0, 0.0).astype(BF16)
    rows_ref[...] = dot(att, pick).T[:count].astype(BF16)


def out_grad(member, mine, other, cot, owner, parts):
    chips, own, patches = mine.shape
    groups = 2 * chips
    width, cols = groups * own, cot.shape[1]
    rows = cols // LANES * (width // parts) + 16
    count = patches // groups
    return pl.pallas_call(
        out_grad_kernel,
        in_specs=[smem()] + [pl.BlockSpec(memory_space=pltpu.VMEM)] * 4,
        out_specs=[pl.BlockSpec(memory_space=pltpu.VMEM)] * 2,
        scratch_shapes=[pltpu.VMEM((width, patches), BF16)],
        out_shape=[
            jax.ShapeDtypeStruct((parts, rows, LANES), I16),
            jax.ShapeDtypeStruct((count, width), BF16),
        ],
        compiler_params=params(16),
        cost_estimate=cost(2 * width * cols * patches, 4 << 20),
        name="out_grad",
    )(member, mine, other, cot, owner)


def decoded(got_ref, first, count, power_row):
    rows = got_ref.shape[1]
    total = jnp.zeros((count, got_ref.shape[2]), F32)
    for source in range(got_ref.shape[0]):
        scale = unit(got_ref[source, rows - 16:, :])[power_row:power_row + 1]
        total = total + from_i16(got_ref[source, first:first + count, :]) * scale
    return total


def qkv_sum_kernel(member, got_ref, *refs):
    outs, blocks = refs[:-1], refs[-1]
    chips = len(outs)
    count = (got_ref.shape[1] - 16) // 3
    totals = [decoded(got_ref, k * count, count, k) for k in range(3)]
    for group in range(2 * chips):
        rows = [total[group * 8:(group + 1) * 8] for total in totals]
        rows = jnp.concatenate(rows + [jnp.zeros_like(rows[0])], axis=0)
        blocks[group // 2, group % 2 * 32:group % 2 * 32 + 32, :] = rows
    for at, out in enumerate(outs):
        out[...] = blocks[(member[0] // 2) ^ at].astype(BF16)


def qkv_sum(member, got, chips):
    vmem = pl.BlockSpec(memory_space=pltpu.VMEM)
    return pl.pallas_call(
        qkv_sum_kernel,
        in_specs=[smem(), vmem],
        out_specs=[vmem] * chips,
        out_shape=[jax.ShapeDtypeStruct((64, LANES), BF16)] * chips,
        scratch_shapes=[pltpu.VMEM((chips, 64, LANES), F32)],
        compiler_params=params(8),
        cost_estimate=cost(1 << 20, 2 << 20),
        name="qkv_sum",
    )(member, got)


def stack_kernel(*refs):
    out = refs[-1]
    for at, block in enumerate(refs[:-1]):
        out[at] = block[...]


def stack(blocks):
    vmem = pl.BlockSpec(memory_space=pltpu.VMEM)
    return pl.pallas_call(
        stack_kernel,
        in_specs=[vmem] * len(blocks),
        out_specs=vmem,
        out_shape=jax.ShapeDtypeStruct((len(blocks),) + blocks[0].shape, BF16),
        compiler_params=params(8),
        cost_estimate=cost(1 << 16, 1 << 20),
        name="stack",
    )(*blocks)


def relay_kernel(member, *refs):
    chips = (len(refs) - 5) // 2
    blocks, columns = refs[:chips], refs[chips:2 * chips]
    keep_ref, send_ref, mine_any, stage, sems = refs[2 * chips:]
    moves = [pltpu.make_async_copy(column, stage.at[i], sems.at[i]) for i, column in enumerate(columns)]
    for copy in moves:
        copy.start()
    core = member[0] % 2
    for at, block in enumerate(blocks):
        keep_ref[at * 32:(at + 1) * 32, :] = block[pl.ds(pl.multiple_of(core * 32, 32), 32), :]
        send_ref[at * 32:(at + 1) * 32, :] = block[pl.ds(pl.multiple_of((1 - core) * 32, 32), 32), :]
    sends = [pltpu.make_async_copy(stage.at[i], mine_any.at[i], sems.at[chips + i]) for i in range(chips)]
    for copy, send in zip(moves, sends):
        copy.wait()
        send.start()
    for send in sends:
        send.wait()


def relay(member, blocks, columns):
    vmem = pl.BlockSpec(memory_space=pltpu.VMEM)
    chips = len(blocks)
    return pl.pallas_call(
        relay_kernel,
        in_specs=[smem()] + [vmem] * chips + [near()] * chips,
        out_specs=[vmem, vmem, near()],
        out_shape=[
            jax.ShapeDtypeStruct((32 * chips, LANES), BF16),
            jax.ShapeDtypeStruct((32 * chips, LANES), BF16),
            jax.ShapeDtypeStruct((chips,) + columns[0].shape, BF16),
        ],
        scratch_shapes=[
            pltpu.VMEM((chips,) + columns[0].shape, BF16), pltpu.SemaphoreType.DMA((2 * chips,)),
        ],
        compiler_params=params(8),
        cost_estimate=cost(1 << 16, 3 << 20),
        name="relay",
    )(member, *blocks, *columns)


def pack_kernel(got_ref, keep_ref, other_ref, out_hbm, pack, sems):
    chips = keep_ref.shape[0] // 32
    rows = []
    for ref in (keep_ref, other_ref):
        values = ref[...].astype(F32)
        rows += [values[at * 32:at * 32 + 24] for at in range(chips)]
    first = 24 * len(rows)
    pack[:first, :] = jnp.concatenate(rows, axis=0).astype(BF16)
    count = (pack.shape[0] - first) // 4
    for slab in range(4):
        total = decoded(got_ref, slab * count, count, slab)
        pack[first + slab * count:first + (slab + 1) * count, :] = total.astype(BF16)
    for copy in send_copies(pack, out_hbm, sems):
        copy.wait()


def pack_sums(got, keep, other, parts):
    vmem = pl.BlockSpec(memory_space=pltpu.VMEM)
    rows = 24 * (keep.shape[0] // 16) + got.shape[1] - 16
    return pl.pallas_call(
        pack_kernel,
        in_specs=[vmem] * 3,
        out_specs=hbm(),
        out_shape=jax.ShapeDtypeStruct((parts, rows, LANES), BF16),
        scratch_shapes=[pltpu.VMEM((rows, LANES), BF16), pltpu.SemaphoreType.DMA((parts,))],
        compiler_params=params(60),
        cost_estimate=cost(1 << 20, 3 << 20),
        name="pack_sums",
    )(got, keep, other)


def unpack_kernel(member, got_ref, qkv_hbm, wout_hbm, qkv_ref, wout_ref, out_sems):
    parts, rows, lanes = got_ref.shape
    steps = out_sems.shape[0] // 2
    per = parts // steps
    groups = qkv_ref.shape[2] // lanes
    first = 24 * groups
    count = wout_ref.shape[0] // parts
    stores = []
    for step in range(steps):
        for part in range(step * per, (step + 1) * per):
            for slab in range(wout_ref.shape[1] // lanes):
                block = got_ref[part, first + slab * count:first + (slab + 1) * count, :]
                wout_ref[part * count:(part + 1) * count, slab * lanes:(slab + 1) * lanes] = block.astype(F32)
            values = got_ref[part, :first, :].astype(F32)
            for at in range(groups):
                source = member[0] ^ (2 * (at % (groups // 2)) + at // (groups // 2))
                lane = pl.ds(pl.multiple_of(source * lanes, lanes), lanes)
                for k in range(3):
                    top = at * 24 + k * 8
                    qkv_ref[k, part * 8:(part + 1) * 8, lane] = values[top:top + 8]
        at = slice(step * per * count, (step + 1) * per * count)
        stores.append(pltpu.make_async_copy(wout_ref.at[at, :], wout_hbm.at[at, :], out_sems.at[2 * step]))
        stores[-1].start()
        at = slice(step * per * 8, (step + 1) * per * 8)
        stores.append(pltpu.make_async_copy(qkv_ref.at[:, at, :], qkv_hbm.at[:, at, :], out_sems.at[2 * step + 1]))
        stores[-1].start()
    for copy in stores:
        copy.wait()


def unpack_sums(member, got, width, cols, groups):
    steps = 4
    qkv = ((3, width // groups, width), F32)
    wout = ((width, cols), F32)
    return pl.pallas_call(
        unpack_kernel,
        in_specs=[smem(), pl.BlockSpec(memory_space=pltpu.VMEM)],
        out_specs=[hbm(), hbm()],
        out_shape=[jax.ShapeDtypeStruct(*qkv), jax.ShapeDtypeStruct(*wout)],
        scratch_shapes=[
            pltpu.VMEM(*qkv), pltpu.VMEM(*wout), pltpu.SemaphoreType.DMA((2 * steps,)),
        ],
        compiler_params=params(12),
        cost_estimate=cost(1 << 20, 6 << 20),
        name="unpack_sums",
    )(member, got)


def bytes_kernel(
    member, bounds, mine_hbm, other_hbm, query_hbm, wk_hbm, wv_hbm, wq_hbm, row_ref,
    out_ref, head_ref, tail_ref,
    lhs, d_query, tables, shares, d_kv, w_own, wq_own, start_ref, end_ref, sems,
):
    chips, rows, patches = mine_hbm.shape
    groups = 2 * chips
    own, width = wq_own.shape
    dim = 64
    heads = own // dim
    blocks = patches // LANES
    total = shares.shape[2]
    s_dev = out_ref.shape[0]
    rim = total - s_dev
    chip, core = member[0] // 2, member[0] % 2
    own_rows = pl.ds(pl.multiple_of(member[0] * own, own), own)
    moves = []

    def move(source, target):
        moves.append(pltpu.make_async_copy(source, target, sems.at[len(moves)]))
        moves[-1].start()

    places = []
    for ref, ref_core in ((mine_hbm, core), (other_hbm, 1 - core)):
        for back in range(chips):
            group = 2 * lax.rem(chip + chips - back, chips) + ref_core
            at = pl.multiple_of(group * own, own)
            places.append(group)
            move(ref.at[back, 2 * own:, :], tables.at[len(places) - 1])
            move(ref.at[back, own:2 * own, :], d_query.at[pl.ds(at, own), :])
            move(ref.at[back, :own, :], lhs.at[pl.ds(width + at, own), :])
    move(wq_hbm.at[own_rows, :], wq_own)
    move(query_hbm, lhs.at[:width, :])
    move(wk_hbm.at[own_rows, :], w_own.at[:, :width])
    move(wv_hbm.at[own_rows, :], w_own.at[:, width:])
    columns_of(row_ref, start_ref, end_ref)
    for copy in moves:
        copy.wait()
    for slot, group in enumerate(places):
        table = tables[slot].astype(F32)
        for at in range(s_dev // patches + 1):
            part = table[8 * (at // 2):8 * (at // 2) + 8]
            part = pltpu.roll(part, 4, 0) if at % 2 else part
            if at < s_dev // patches:
                shares[group, :, at * patches:(at + 1) * patches] = part
            else:
                shares[group, :, s_dev:] = part[:, :rim]
    length = (row_ref[8:9, :] - row_ref[0:1, :]).astype(F32)
    lhs[2 * width:, :] = split2(dot(wq_own[...], d_query[...]) * (1.0 / length))

    def tile_grad(base, span, first, count, slot):
        inside = patch_major(start_ref, end_ref, first, count, base, span)
        at = pl.ds(base, span)
        patch = pl.ds(first, count)
        for group in range(groups):
            share = shares[group, :, at]
            for kind in range(2):
                top = kind * width + group * own
                wide = dot(lhs[top:top + own, patch], inside)
                part = head_rows(share[kind * heads:(kind + 1) * heads], dim)
                d_kv[slot, top:top + own, :span] = (part * wide).astype(BF16)
        grad = dot(w_own[...], d_kv[slot, :, :span])
        pool = dot(lhs[2 * width:, patch], inside)
        return (grad + (pool[:own] + pool[own:])).T

    def tiles(span, first_of, count):
        def go(i, carry):
            for slot in range(UNROLL):
                base = pl.multiple_of((UNROLL * i + slot) * span, span)
                out_ref[pl.ds(base, span), :] = tile_grad(base, span, first_of(base), count, slot).astype(BF16)
            return carry

        lax.fori_loop(0, s_dev // (UNROLL * span), go, 0)

    def first_of(base):
        return pl.multiple_of(window(bounds, blocks, base) * LANES, LANES)

    @pl.when(bounds[blocks + 1] > 0)
    def _():
        tiles(LANES, first_of, 2 * LANES)

    @pl.when(bounds[blocks + 1] == 0)
    def _():
        tiles(TILE, first_of, 2 * LANES)

    head_ref[...] = tile_grad(0, LANES, 0, 2 * LANES, 0)[:16]
    tail_ref[...] = tile_grad(s_dev, rim, patches - 2 * LANES, 2 * LANES, 1)[:16]


def byte_grads(member, bounds, mine_factors, other_factors, query, w_query, w_key, w_value, row, s_dev):
    chips, rows, patches = mine_factors.shape
    groups = 2 * chips
    width = w_query.shape[0]
    own = width // groups
    rim = LANES
    return pl.pallas_call(
        bytes_kernel,
        in_specs=[smem(), smem(), near(), near()] + [hbm()] * 4 + [pl.BlockSpec(memory_space=pltpu.VMEM)],
        out_specs=[pl.BlockSpec(memory_space=pltpu.VMEM)] * 3,
        scratch_shapes=[
            pltpu.VMEM((2 * width + 2 * own, patches), BF16),
            pltpu.VMEM((width, patches), BF16),
            pltpu.VMEM((groups, rows - 2 * own, patches), BF16),
            pltpu.VMEM((groups, 8, s_dev + rim), F32),
            pltpu.VMEM((UNROLL, 2 * width, TILE), BF16),
            pltpu.VMEM((own, 2 * width), BF16),
            pltpu.VMEM((own, width), BF16),
            pltpu.VMEM((patches, LANES), I32),
            pltpu.VMEM((patches, LANES), I32),
            pltpu.SemaphoreType.DMA((3 * groups + 4,)),
        ],
        out_shape=[
            jax.ShapeDtypeStruct((s_dev, own), BF16),
            jax.ShapeDtypeStruct((16, own), F32),
            jax.ShapeDtypeStruct((16, own), F32),
        ],
        compiler_params=params(52),
        cost_estimate=cost(8 << 30, 8 << 20),
        name="byte_grads",
    )(member, bounds, mine_factors, other_factors, query, w_key, w_value, w_query, row)


def shifted(value, axis, steps):
    count = lax.axis_size(axis)
    first, last = (max(0, -steps), min(count, count - steps))
    return lax.ppermute(value, axis, [(source, source + steps) for source in range(first, last)])


def swap(value, axis):
    return lax.all_to_all(value, axis, split_axis=0, concat_axis=0, tiled=True)


def over_chips(value):
    count = lax.axis_size("patch")
    blocks = [value]
    for step in range(1, count // 2):
        pairs = [(i, (i + 2 * step) % count) for i in range(count)]
        blocks.append(lax.ppermute(value, "patch", pairs))
    return blocks


def other_core(value):
    return lax.ppermute(value, "patch", [(i, i ^ 1) for i in range(lax.axis_size("patch"))])


def after(value, *others):
    return lax.optimization_barrier((value,) + others)[0]


def local(byte_states, patch_len, shard_offset, owner, cotangent, w_query, w_key, w_value, w_out):
    s_dev, width = byte_states.shape
    groups = lax.axis_size("patch")
    parts = lax.axis_size("seq")
    member = lax.axis_index("patch").astype(I32).reshape(1)
    rim = shifted(byte_states[:MAXP], "seq", -1)

    coded_att = after(att_grad(w_out, cotangent, groups), rim)
    got_att = swap(coded_att, "patch")
    kv, pooled, all_query, att, query, probs, geo, row, bounds = forward(
        member, shard_offset, patch_len, byte_states, rim, w_key, w_value, w_query, groups
    )
    att_columns = over_chips(att)
    grads, factor = backward(bounds, byte_states, kv, pooled, rim, att_sum(got_att), query, probs, geo, row, parts)
    got_qkv = swap(after(grads, *att_columns[1:]), "seq")
    mine_att = stack([after(att_columns[0], grads)] + att_columns[1:])
    other_att = other_core(mine_att)
    columns = over_chips(factor)
    coded_out, patch_rows = out_grad(member, mine_att, other_att, cotangent, owner, parts)
    got_out = swap(after(coded_out, got_qkv, columns[1], columns[3]), "seq")
    blocks = [
        block if at == 0 else lax.ppermute(block, "patch", [(i, i ^ (2 * at)) for i in range(groups)])
        for at, block in enumerate(qkv_sum(member, got_qkv, groups // 2))
    ]
    keep, send, mine = relay(member, blocks, columns)
    got_keep = other_core(send)
    other = other_core(mine)
    sums = swap(pack_sums(got_out, keep, got_keep, parts), "seq")
    d_bytes, head, tail = byte_grads(
        member, bounds, mine, other, all_query, w_query, w_key, w_value, row, s_dev
    )
    first = (head + shifted(tail, "seq", 1)).astype(BF16)
    d_bytes = lax.dynamic_update_slice(d_bytes, first, (0, 0))
    d_qkv, d_wout = unpack_sums(member, sums, width, cotangent.shape[1], groups)
    return (d_bytes, d_qkv, d_wout, patch_rows)


def solution(mesh):
    return jax.shard_map(
        local,
        mesh=mesh,
        in_specs=(
            P("seq", None), P("seq", None), P("seq"), P("seq", None), P("seq", "patch"),
            P(), P(), P(), P(None, "patch"),
        ),
        out_specs=(P("seq", "patch"), P(None, "patch", None), P(None, "patch"), P(("seq", "patch"), None)),
        check_vma=False,
    )
```
